128 devices in a mesh: section: 2 (over x_hi), mp: 4 (over x_lo, core), dp: 16 (over z, y).
Axes of the slice: x: 4 (x_hi: 2, x_lo: 2; x = x_hi * 2 + x_lo), y: 4, z: 4, core: 2. Of those that a mesh axis runs over, the one named last changes fastest.
Arguments:
- embeds: bfloat16 [2, 256, 8192], P('section', 'mp', 'dp'), may hold values from -6 to 6
- cotangent: bfloat16 [2, 256, 8192], P('section', 'mp', 'dp'), may hold values from -6 to 6
- norm_gain: float32 [1, 2, 8192], P(None, 'section', 'dp'), may hold values from 0.25 to 1.75
- w_query: bfloat16 [1, 2, 8192, 8192], P(None, 'section', 'dp', 'mp')
- w_keyval: bfloat16 [1, 2, 8192, 2, 1024], P(None, 'section', 'dp', None, 'mp')
- w_out: bfloat16 [1, 2, 8192, 8192], P(None, 'section', 'mp', 'dp'), may hold values from -0.0625 to 0.0625
- seq_lengths: int32 [2, 3], replicated, may hold values from 1 to 128, 256 in all within a row
- image_mask: int32 [2, 32], P('section'), may hold values from 0 to 1
- block_owner: int32 [2, 32], P('section'), may hold values from 0 to 31, as said below
- merger_weight: bfloat16 [5120, 8192], P('mp', 'dp'), may hold values from -0.078125 to 0.078125
- merger_pre: bfloat16 [32, 2, 2, 8, 5120], P(('section', 'dp'), None, None, None, 'mp'), may hold values from -5 to 5
Outputs:
- input_grad: bfloat16 [2, 256, 8192], P('section', 'mp', 'dp')
- merger_pre_grad: float32 [32, 2, 2, 8, 5120], P(('section', 'dp'), None, None, None, 'mp')
The draws below stay inside these ranges and needn't reach their ends.
Inputs may be any that keep to these rules, and one draw needn't show every extreme that they name: `block_owner`: within one micro-batch at most 2 image blocks have the same owner; some owner has exactly 2 image blocks in every micro-batch.
All inputs are finite; a program needn't handle non-finite values.
Results may differ from the reference program's by a relative error of at most 0.029.
Values may be sent and summed in bfloat16 or wider, within the bound.
No kernel may reach another device: no remote copies, remote signals or barrier semaphores. Data moves between devices by JAX's collectives and lax.ppermute only.
A program may use at most 128 MiB of HBM per device.

```python
import math
import jax
import jax.numpy as jnp
import numpy as np
from jax import lax

MODEL_WIDTH = 8192
QUERY_HEAD_COUNT = 64
KEYVALUE_HEADS = 8
HEAD_SIZE = 128
VH = 5120
TOK = 256
NSEQ = 3
GROUP_LAYERS = 1
CAP = 2
VB = 8
NB = 32
MICRO_BATCHES = 2
NOWN = 32
N_SECTION = 2


def draw_layout(key):
    key_one, key_two, key_three = jax.random.split(key, 3)
    target_owner = jax.random.randint(key_one, (), 0, NOWN)
    orders = jax.vmap(lambda subkey: jax.random.permutation(subkey, NOWN))(jax.random.split(key_two, MICRO_BATCHES))
    leading = orders[:, :1]
    orders = jnp.where(orders == target_owner, leading, orders)
    orders = orders.at[:, 0].set(target_owner)
    chosen = orders[:, :NB // 2]
    places = jax.vmap(lambda subkey: jax.random.permutation(subkey, NB))(jax.random.split(key_three, MICRO_BATCHES))
    owners = jnp.take_along_axis(chosen, places // 2, axis=1)
    return (owners.astype(jnp.int32), places)


def draw_block_owner(key, part):
    owners, places = draw_layout(key)
    return owners


def draw_image_mask(key, part):
    owners, places = draw_layout(key)
    key = jax.random.fold_in(key, 5)
    marks = (jax.random.randint(key, (MICRO_BATCHES, NB), 0, 4) > 0).astype(jnp.int32)
    return jnp.where(places // 2 == 0, 1, marks).astype(jnp.int32)


def draw_base_offset(key):
    return jax.random.normal(key, (GROUP_LAYERS, MICRO_BATCHES, MODEL_WIDTH, KEYVALUE_HEADS * HEAD_SIZE), jnp.float32)


def draw_w_keyval(key, part):
    base_offset = draw_base_offset(key)
    key = jax.random.fold_in(key, 7)
    values = jax.random.normal(key, base_offset.shape, jnp.float32) / math.sqrt(MODEL_WIDTH)
    keys = base_offset / math.sqrt(MODEL_WIDTH)
    return jnp.stack([keys, values], axis=3).astype(jnp.bfloat16)


def draw_w_query(key, part):
    key = jax.random.fold_in(key, 9)
    noise = jax.random.normal(key, (GROUP_LAYERS, MICRO_BATCHES, MODEL_WIDTH, QUERY_HEAD_COUNT * HEAD_SIZE), jnp.float32) / math.sqrt(MODEL_WIDTH)
    return noise.astype(jnp.bfloat16)


def steps_of(own_key, shape, shards, smallest, top_value):
    gain = 1.0
    for dim, blocks in shards:
        heights = jax.random.uniform(jax.random.fold_in(jax.random.fold_in(own_key, 6), dim), (blocks,), jnp.float32, smallest / len(shards), top_value / len(shards))
        gain = gain * jnp.repeat(jnp.exp(heights), shape[dim] // blocks).reshape((-1,) + (1,) * (len(shape) - 1 - dim))
    return gain


def profile(count, total, most, skew):
    portions = [(1 << 20) // math.isqrt(grade ** skew) + 1 for grade in range(2, count + 1)]
    surplus, counts = total - most - (count - 1), [1] * (count - 1)
    while surplus > 0:
        free = [i for i in range(count - 1) if counts[i] < most]
        whole, budget = sum([portions[i] for i in free]), surplus
        for i in free:
            addition = min(most - counts[i], max(1, budget * portions[i] // whole), surplus)
            counts[i] = counts[i] + addition
            surplus = surplus - addition
    return np.array([most] + counts)


def uneven_parts(own_key, count, total, most, slope):
    if count == 2:
        one = jax.random.randint(own_key, (), max(1, total - most), min(most, total - 1) + 1)
        return jnp.stack([one, total - one])
    sizes = jnp.asarray(profile(count, total, most, slope), jnp.int32)
    twos = (count - 1) // 2
    source_of, taker = sizes[1:1 + 2 * twos:2], sizes[2:2 + 2 * twos:2]
    margin = jnp.minimum(source_of - 1, most - taker)
    passed = jax.random.randint(jax.random.fold_in(own_key, 1), (twos,), 0, 1 << 20) % (margin + 1)
    sizes = sizes.at[1:1 + 2 * twos:2].set(source_of - passed).at[2:2 + 2 * twos:2].set(taker + passed)
    return sizes[jax.random.permutation(jax.random.fold_in(own_key, 2), count)]


def scatter_about(key, extent, spread, most, cuts=(), held_as=jnp.bfloat16):
    array = jax.random.normal(key, extent, jnp.float32) * spread
    if len(cuts) > 0:
        array = steps_of(key, extent, cuts, -0.22, 0.18) * array
    return jnp.clip(array, min=-most, max=most).astype(held_as)


def setup_inputs(seed: int = 0) -> dict:
    seeds = jax.random.split(jax.random.key(seed), 12)
    embeds = scatter_about(seeds[0], (MICRO_BATCHES, TOK, MODEL_WIDTH), 1.0, 6.0, ((0, 2), (1, 4), (2, 16)))
    cotangent = scatter_about(seeds[1], (MICRO_BATCHES, TOK, MODEL_WIDTH), 1.0, 6.0, ((0, 2), (1, 4), (2, 16)))
    norm_gain = jnp.clip(1.0 + 0.15 * jax.random.normal(seeds[2], (GROUP_LAYERS, MICRO_BATCHES, MODEL_WIDTH), jnp.float32), 0.25, 1.75)
    w_query = draw_w_query(jax.random.fold_in(seeds[11], 71), 0)
    w_keyval = draw_w_keyval(jax.random.fold_in(seeds[11], 71), 0)
    w_out = scatter_about(seeds[5], (GROUP_LAYERS, MICRO_BATCHES, QUERY_HEAD_COUNT * HEAD_SIZE, MODEL_WIDTH), (QUERY_HEAD_COUNT * HEAD_SIZE) ** -0.5, 0.0625, ((1, 2), (2, 4), (3, 16)))
    seq_lengths = jax.vmap(lambda own: uneven_parts(own, NSEQ, TOK, TOK // 2, 2))(jax.random.split(seeds[6], MICRO_BATCHES)).reshape((MICRO_BATCHES, NSEQ)).astype(jnp.int32)
    image_mask = draw_image_mask(jax.random.fold_in(seeds[11], 71), 0)
    block_owner = draw_block_owner(jax.random.fold_in(seeds[11], 71), 0)
    merger_weight = scatter_about(seeds[9], (VH, MODEL_WIDTH), VH ** -0.5, 0.078125, ((0, 4), (1, 16)))
    merger_pre = scatter_about(seeds[10], (NOWN, MICRO_BATCHES, CAP, VB, VH), 1.0, 5.0, ((0, 32), (4, 4)))
    return {"embeds": embeds, "cotangent": cotangent, "norm_gain": norm_gain, "w_query": w_query, "w_keyval": w_keyval, "w_out": w_out, "seq_lengths": seq_lengths, "image_mask": image_mask, "block_owner": block_owner, "merger_weight": merger_weight, "merger_pre": merger_pre}


EPSILON = 1e-06
MASKED = -1e+30

def build_masks(seq_lengths, tokens):
    bounds = jnp.cumsum(seq_lengths, axis=1)
    places = jnp.arange(tokens, dtype=jnp.int32)
    segment = lax.optimization_barrier(jnp.sum((places[None, :, None] >= bounds[:, None, :]).astype(jnp.int32), axis=2))
    causal = places[None, :] <= places[:, None]
    return (segment[:, :, None] == segment[:, None, :]) & causal[None]

def split_heads(query, keys, values):
    tokens = query.shape[0]
    groups = keys.shape[1] // HEAD_SIZE
    group_size = query.shape[1] // keys.shape[1]
    return (query.reshape(tokens, groups, group_size, HEAD_SIZE).astype(jnp.float32), keys.reshape(tokens, groups, HEAD_SIZE).astype(jnp.float32), values.reshape(tokens, groups, HEAD_SIZE).astype(jnp.float32))

def head_weights(query_heads, key_heads, allowed):
    scores = jnp.einsum('qhgd,khd->hgqk', query_heads, key_heads) * (1.0 / math.sqrt(HEAD_SIZE))
    scores = jnp.where(allowed[None, None], scores, MASKED)
    largest = lax.optimization_barrier(jnp.max(scores, axis=-1, keepdims=True))
    raised = jnp.exp(scores - largest)
    return raised / lax.optimization_barrier(jnp.sum(raised, axis=-1, keepdims=True))

def rounded_copy(values):
    return lax.optimization_barrier(values.astype(jnp.bfloat16)).astype(jnp.float32)

def attend(query, keys, values, allowed):
    query_heads, key_heads, value_heads = split_heads(query, keys, values)
    weights = head_weights(query_heads, key_heads, allowed)
    mixture = jnp.einsum('hgqk,khd->qhgd', rounded_copy(weights), value_heads)
    return mixture.reshape(query.shape[0], -1).astype(jnp.bfloat16)

def attend_back(query, keys, values, head_grad, allowed):
    query_heads, key_heads, value_heads = split_heads(query, keys, values)
    weights = head_weights(query_heads, key_heads, allowed)
    grad_heads = head_grad.astype(jnp.float32).reshape(query_heads.shape)
    value_grad = jnp.einsum('hgqk,qhgd->khd', rounded_copy(weights), grad_heads)
    weight_grad = jnp.einsum('qhgd,khd->hgqk', grad_heads, value_heads)
    centred = weight_grad - lax.optimization_barrier(jnp.sum(weight_grad * weights, axis=-1, keepdims=True))
    score_grad = rounded_copy(weights * centred * (1.0 / math.sqrt(HEAD_SIZE)))
    query_grad = jnp.einsum('hgqk,khd->qhgd', score_grad, key_heads)
    key_grad = jnp.einsum('hgqk,qhgd->khd', score_grad, query_heads)
    tokens = query.shape[0]
    return jnp.concatenate([query_grad.reshape(tokens, -1), key_grad.reshape(tokens, -1), value_grad.reshape(tokens, -1)], axis=1)

def gelu_slope(values):
    cumulative = 0.5 * (1.0 + lax.erf(values * (1.0 / math.sqrt(2.0))))
    return cumulative + values * jnp.exp(-0.5 * values * values) * (1.0 / math.sqrt(2.0 * math.pi))

def reference(embeds, cotangent, norm_gain, w_query, w_keyval, w_out, seq_lengths, image_mask, block_owner, merger_weight, merger_pre):
    allowed_all = build_masks(seq_lengths, TOK)
    q_cols = QUERY_HEAD_COUNT * HEAD_SIZE
    keyvalue_columns = KEYVALUE_HEADS * HEAD_SIZE
    layer_count = GROUP_LAYERS * N_SECTION
    results = []
    for micro_batch in range(MICRO_BATCHES):
        allowed = allowed_all[micro_batch]
        resident = embeds[micro_batch]
        stored = []
        for layer_index in range(layer_count):
            round_index = layer_index // N_SECTION
            section_pos = layer_index % N_SECTION
            query_w = w_query[round_index, section_pos]
            keyval_w = w_keyval[round_index, section_pos].reshape(MODEL_WIDTH, 2 * keyvalue_columns)
            resident_f = resident.astype(jnp.float32)
            normed = (resident_f * norm_gain[round_index, section_pos]).astype(jnp.bfloat16)
            projected = jnp.concatenate([jnp.dot(normed, query_w, preferred_element_type=jnp.float32), jnp.dot(normed, keyval_w, preferred_element_type=jnp.float32)], axis=1)
            scale_rows = lax.rsqrt(lax.optimization_barrier(jnp.sum(resident_f * resident_f, axis=1)) / MODEL_WIDTH + EPSILON)
            qkv = (projected * scale_rows[:, None]).astype(jnp.bfloat16)
            attended = attend(qkv[:, :q_cols], qkv[:, q_cols:q_cols + keyvalue_columns], qkv[:, q_cols + keyvalue_columns:], allowed)
            stored.append((qkv, scale_rows))
            added = jnp.dot(attended, w_out[round_index, section_pos], preferred_element_type=jnp.float32)
            resident = (resident_f + added).astype(jnp.bfloat16)
        grad_rows = cotangent[micro_batch]
        for layer_index in range(layer_count - 1, -1, -1):
            round_index = layer_index // N_SECTION
            section_pos = layer_index % N_SECTION
            query_w = w_query[round_index, section_pos]
            keyval_w = w_keyval[round_index, section_pos].reshape(MODEL_WIDTH, 2 * keyvalue_columns)
            qkv, scale_rows = stored[layer_index]
            head_grad = jnp.dot(grad_rows, w_out[round_index, section_pos].T, preferred_element_type=jnp.float32).astype(jnp.bfloat16)
            grads = attend_back(qkv[:, :q_cols], qkv[:, q_cols:q_cols + keyvalue_columns], qkv[:, q_cols + keyvalue_columns:], head_grad, allowed)
            scaled = (grads * scale_rows[:, None]).astype(jnp.bfloat16)
            through = jnp.dot(scaled[:, :q_cols], query_w.T, preferred_element_type=jnp.float32)
            through = through + jnp.dot(scaled[:, q_cols:], keyval_w.T, preferred_element_type=jnp.float32)
            grad_rows = (grad_rows.astype(jnp.float32) + norm_gain[round_index, section_pos] * through).astype(jnp.bfloat16)
        results.append(grad_rows)
    input_grad = jnp.stack(results)
    hidden_grad = jnp.stack([jnp.dot(input_grad[index], merger_weight.T, preferred_element_type=jnp.float32) for index in range(MICRO_BATCHES)])
    blocks = hidden_grad.reshape(MICRO_BATCHES, NB, VB * VH)
    positions = jnp.arange(NB, dtype=jnp.int32)
    earlier = (block_owner[:, :, None] == block_owner[:, None, :]) & (image_mask[:, None, :] == 1) & (positions[None, None, :] < positions[None, :, None])
    slots = lax.optimization_barrier(jnp.sum(earlier.astype(jnp.int32), axis=2)).astype(jnp.int32)
    target = (block_owner * CAP + slots).astype(jnp.int32)
    targets_all = jnp.arange(NOWN * CAP, dtype=jnp.int32)
    selector = ((targets_all[None, :, None] == target[:, None, :]) & (image_mask[:, None, :] == 1)).astype(jnp.float32)
    picked = jnp.einsum('bsn,bnx->bsx', selector, blocks, precision=lax.Precision.HIGHEST)
    arranged = jnp.transpose(picked.reshape(MICRO_BATCHES, NOWN, CAP, VB, VH), (1, 0, 2, 3, 4))
    return (input_grad, gelu_slope(merger_pre.astype(jnp.float32)) * arranged)
```

```python
import functools
import math

import jax
import jax.numpy as jnp
from jax import lax
from jax.experimental import pallas as pl
from jax.experimental.pallas import tpu as pltpu
from jax.sharding import PartitionSpec as P

MODEL_WIDTH = 8192
HEAD_SIZE = 128
GROUP_HEADS = 8
CAP = 2
VB = 8
NSEQ = 3

EPSILON = 1e-06
MASKED = -1e30
SOFT = 1.0 / math.sqrt(HEAD_SIZE)
LOG2E = math.log2(math.e)
QB = 128

BF = jnp.bfloat16
F32 = jnp.float32

VMEM = pl.BlockSpec(memory_space=pltpu.VMEM)
SMEM = pl.BlockSpec(memory_space=pltpu.SMEM)
ANY = pl.BlockSpec(memory_space=pl.ANY)
HBM = pl.BlockSpec(memory_space=pltpu.HBM)


def shape_of(shape, dtype):
    return jax.ShapeDtypeStruct(shape, dtype)


def in_hbm(*arrays):
    return [pltpu.with_memory_space_constraint(array, pltpu.HBM) for array in arrays]


def params(mebibytes):
    return pltpu.CompilerParams(vmem_limit_bytes=mebibytes << 20)


def cost(flops, bytes_accessed):
    return pl.CostEstimate(flops=flops, bytes_accessed=bytes_accessed, transcendentals=0)


def dot_nn(left, right):
    return jnp.dot(left, right, preferred_element_type=F32)


def dot_nt(left, right):
    return lax.dot_general(left, right, (((1,), (1,)), ((), ())), preferred_element_type=F32)


def two_lanes(column):
    high = column.astype(BF).astype(F32)
    lane = lax.broadcasted_iota(jnp.int32, (column.shape[0], 128), 1)
    return jnp.where(lane == 0, high, jnp.where(lane == 1, column - high, 0.0)).astype(BF)


def start_columns(sources, chunks, sems):
    width, index = chunks.shape[2], 0
    for source in sources:
        for start in range(0, source.shape[1], width):
            block = source.at[:, start : start + width]
            pltpu.make_async_copy(block, chunks.at[index], sems.at[index]).start()
            index += 1


def start_rows(sources, chunks, sems):
    rows, at = chunks.shape[1], 0
    for source in sources:
        start = 0
        while start < source.shape[0]:
            index, within = at // rows, at % rows
            count = min(rows - within, source.shape[0] - start)
            block = source.at[start : start + count, :]
            place = chunks.at[index, within : within + count, :]
            pltpu.make_async_copy(block, place, sems.at[index]).start()
            start, at = start + count, at + count


def start_joined(wqs, wkv_ref, chunks, sems):
    start_columns(wqs, chunks, sems)
    last = chunks.shape[0] - 1
    pltpu.make_async_copy(wkv_ref, chunks.at[last], sems.at[last]).start()


def landed(chunks, sems, index):
    pltpu.make_async_copy(chunks.at[index], chunks.at[index], sems.at[index]).wait()
    return chunks.at[index]


def by_section(first, second):
    section = lax.axis_index("section")
    pl.when(section == 0)(first)
    pl.when(section != 0)(second)


def spans(cols):
    return [slice(start, min(start + 512, cols)) for start in range(0, cols, 512)]


def start_spans(source, target, sems):
    for index, span in enumerate(spans(target.shape[-1])):
        at = (slice(None),) * (len(target.shape) - 1) + (span,)
        pltpu.make_async_copy(source.at[at], target.at[at], sems.at[index]).start()


def wait_span(target, sems, index):
    at = (slice(None),) * (len(target.shape) - 1) + (spans(target.shape[-1])[index],)
    pltpu.make_async_copy(target.at[at], target.at[at], sems.at[index]).wait()


def sender(staged, out_ref, sems):
    owners, share, cols = staged.shape

    def put(start, tile):
        span = slice(start, start + tile.shape[1])
        staged[:, :, span] = tile.reshape(owners, share, tile.shape[1])
        index = spans(cols).index(span)
        at = (slice(None), slice(None), span)
        pltpu.make_async_copy(staged.at[at], out_ref.at[at], sems.at[index]).start()

    def finish():
        for index in range(len(spans(cols))):
            wait_span(staged, sems, index)

    return put, finish


def repeat_out(tile, out_ref, sems):
    for place in range(out_ref.shape[0]):
        pltpu.make_async_copy(tile, out_ref.at[place], sems.at[place]).start()


def repeat_wait(tile, out_ref, sems):
    for place in range(out_ref.shape[0]):
        pltpu.make_async_copy(tile, out_ref.at[place], sems.at[place]).wait()


def project_rows(rows, gain, chunks, chunk_at, put):
    rows_f = rows.astype(F32)
    normed = (rows_f * gain).astype(BF)
    count, _, width = chunks.shape
    put(count * width, two_lanes(jnp.sum(rows_f * rows_f, axis=1, keepdims=True)))
    for index in range(count):
        put(index * width, dot_nn(normed, chunk_at(index)[...]).astype(BF))


def load_kernel(joined, pieces, *refs):
    *sources, out_ref, sems = refs

    def load(refs):
        if joined:
            start_joined(refs[:-1], refs[-1], out_ref, sems)
        else:
            start_rows(refs, out_ref, sems)

    by_section(lambda: load(sources[:pieces]), lambda: load(sources[pieces:]))
    for index in range(out_ref.shape[0]):
        landed(out_ref, sems, index)


def first_kernel(
    x_ref, gain_ref, wq_ref, wkv_ref, wout_ref, out_ref, chunks, staged, sems, out_sems
):
    put, finish = sender(staged, out_ref, out_sems)
    tokens = x_ref.shape[0]

    def rows():
        return jnp.concatenate([x_ref[tokens // 2 :, :], x_ref[: tokens // 2, :]], axis=0)

    def first():
        start_joined([wq_ref], wkv_ref, chunks, sems)
        project_rows(rows(), gain_ref[...], chunks, lambda at: landed(chunks, sems, at), put)

    def second():
        start_rows([wout_ref], chunks, sems)
        count, width, _ = chunks.shape
        put(count * width, jnp.zeros((tokens, 128), BF))
        put((count - 1) * width, jnp.zeros((tokens, width), BF))
        x = rows()
        for index in range(count - 1):
            put(index * width, dot_nt(x, landed(chunks, sems, index)[...]).astype(BF))

    by_section(first, second)
    finish()


def first_load_kernel(wq_ref, wkv_ref, wout_ref, out_ref, sems):
    def wait(count):
        for index in range(count):
            landed(out_ref, sems, index)

    def first():
        start_joined([wq_ref], wkv_ref, out_ref, sems)
        wait(out_ref.shape[0])

    def second():
        start_rows([wout_ref], out_ref, sems)
        wait(out_ref.shape[0] - 1)

    by_section(first, second)


def first_own_kernel(
    mine_ref, near_ref, far_ref, cross_ref, gain_ref, chunks, out_ref, x_ref, x, staged, out_sems
):
    rank = lax.axis_index("mp")
    share = mine_ref.shape[0]
    for distance, ref in enumerate((mine_ref, near_ref, far_ref, cross_ref)):
        at = pl.multiple_of(jnp.bitwise_xor(rank, distance) * share, share)
        x[pl.ds(at, share), :] = ref[...].astype(F32)
    x_ref[...] = x[...].astype(BF)
    put, finish = sender(staged, out_ref, out_sems)
    tokens = x_ref.shape[0]
    count, width, _ = chunks.shape

    def first():
        project_rows(x_ref[...], gain_ref[...], chunks, lambda at: chunks.at[at], put)

    def second():
        put(count * width, jnp.zeros((tokens, 128), BF))
        put((count - 1) * width, jnp.zeros((tokens, width), BF))
        for index in range(count - 1):
            put(index * width, dot_nt(x_ref[...], chunks[index]).astype(BF))

    by_section(first, second)
    finish()


def chosen(first_ref, second_ref):
    return jnp.where(lax.axis_index("section") == 0, first_ref[...], second_ref[...])


def summed(pair_ref, across_ref, beside_ref):
    even = lax.axis_index("mp") % 2 == 0
    lower = jnp.where(even, across_ref[...], beside_ref[...])
    upper = jnp.where(even, beside_ref[...], across_ref[...])
    return pair_ref[...].astype(F32) + jnp.concatenate([lower, upper], axis=0).astype(F32)


def project_kernel(
    r0_ref, r1_ref, pair_ref, across_ref, beside_ref, g0_ref, g1_ref, chunks, out_ref,
    staged, out_sems,
):
    added = summed(pair_ref, across_ref, beside_ref)
    rows = (chosen(r0_ref, r1_ref).astype(F32) + added).astype(BF)
    put, finish = sender(staged, out_ref, out_sems)
    project_rows(rows, chosen(g0_ref, g1_ref), chunks, lambda at: chunks.at[at], put)
    finish()


def head_grad_kernel(
    r0_ref, r1_ref, pair_ref, across_ref, beside_ref, g0_ref, g1_ref, chunks, out_ref, rows_ref,
    staged, out_sems,
):
    added = summed(pair_ref, across_ref, beside_ref)
    rows = chosen(r0_ref, r1_ref).astype(F32) + chosen(g0_ref, g1_ref) * added
    rows_ref[...] = rows.astype(BF)
    count, width, _ = chunks.shape
    put, finish = sender(staged, out_ref, out_sems)
    for index in range(count):
        put(index * width, dot_nt(rows_ref[...], chunks[index]).astype(BF))
    finish()


def add_parts(load, count):
    total = load(0).astype(F32)
    for index in range(1, count):
        total = total + load(index).astype(F32)
    return total


def part_sums(parts, sems):
    def total(index):
        wait_span(parts, sems, index)
        span = spans(parts.shape[2])[index]
        return add_parts(lambda source: parts[source, :, span], parts.shape[0])

    return total


def scaled_sum(total, tile):
    ranges = spans(tile.shape[1])
    squares = jnp.sum(total(len(ranges) - 1), axis=1, keepdims=True)
    scale = lax.rsqrt(squares / MODEL_WIDTH + EPSILON)
    for index, span in enumerate(ranges[:-1]):
        tile[:, span] = (total(index) * scale).astype(BF)
    tile[:, ranges[-1]] = two_lanes(scale)


def plain_sum(total, tile):
    for index, span in enumerate(spans(tile.shape[1])):
        tile[:, span] = total(index).astype(BF)


def first_sum_kernel(parts_ref, out_ref, parts, sems):
    start_spans(parts_ref, parts, sems)
    total = part_sums(parts, sems)
    by_section(lambda: scaled_sum(total, out_ref), lambda: plain_sum(total, out_ref))


def sum_kernel(adder, parts_ref, out_ref, parts, tile, sems, out_sems):
    start_spans(parts_ref, parts, sems)
    adder(part_sums(parts, sems), tile)
    repeat_out(tile, out_ref, out_sems)
    repeat_wait(tile, out_ref, out_sems)


def choose_kernel(first_ref, second_ref, out_ref, sems):
    first = first_ref.at[:, : out_ref.shape[2]]
    second = second_ref.at[:, : out_ref.shape[2]]
    by_section(
        lambda: repeat_out(first, out_ref, sems), lambda: repeat_out(second, out_ref, sems)
    )
    repeat_wait(first, out_ref, sems)


def fill_bias(seq_ref, bias):
    section = lax.axis_index("section")
    tokens = bias.shape[0]
    keys = lax.broadcasted_iota(jnp.int32, (tokens, tokens), 0)
    queries = lax.broadcasted_iota(jnp.int32, (tokens, tokens), 1)
    key_segment = jnp.zeros((tokens, tokens), jnp.int32)
    query_segment = jnp.zeros((tokens, tokens), jnp.int32)
    bound = 0
    for index in range(NSEQ):
        bound = bound + seq_ref[section, index]
        key_segment = key_segment + (keys >= bound).astype(jnp.int32)
        query_segment = query_segment + (queries >= bound).astype(jnp.int32)
    allowed = (keys <= queries) & (key_segment == query_segment)
    bias[...] = jnp.where(allowed, 0.0, MASKED)


def head_columns(head):
    return slice(head * HEAD_SIZE, (head + 1) * HEAD_SIZE)


def softmax_blocks(tokens, body):
    def one_head(head, carry):
        for at in range(0, tokens, QB):
            lanes = pl.ds(pl.multiple_of(head * tokens + at, QB), QB)
            body(slice(at, at + QB), lanes, at + QB)
        return carry

    lax.fori_loop(0, GROUP_HEADS, one_head, 0, unroll=2)


def clear_unreached(target, tokens):
    for head in range(GROUP_HEADS):
        for at in range(0, tokens - QB, QB):
            lanes = slice(head * tokens + at, head * tokens + at + QB)
            target[at + QB :, lanes] = jnp.zeros((tokens - at - QB, QB), target.dtype)


def weights_of(scores, bias):
    scores = scores * (SOFT * LOG2E) + bias
    raised = jnp.exp2(scores - jnp.max(scores, axis=0, keepdims=True))
    return raised * (1.0 / jnp.sum(raised, axis=0, keepdims=True))


def start_qkv(qkv_ref, qkv, q_cols, sems):
    pltpu.make_async_copy(qkv_ref.at[:, q_cols:], qkv.at[:, q_cols:], sems.at[0]).start()
    start_groups(qkv_ref, qkv, q_cols, sems, 1)


def start_groups(source, target, q_cols, sems, first):
    width = GROUP_HEADS * HEAD_SIZE
    for group in range(q_cols // width):
        at = (slice(None), slice(group * width, (group + 1) * width))
        pltpu.make_async_copy(source.at[at], target.at[at], sems.at[first + group]).start()


def wait_group(target, sems, first, group):
    width = GROUP_HEADS * HEAD_SIZE
    at = (slice(None), slice(group * width, (group + 1) * width))
    pltpu.make_async_copy(target.at[at], target.at[at], sems.at[first + group]).wait()


def forward_kernel(seq_ref, qkv_ref, wout0_ref, *refs):
    *wout1_refs, out_ref, qkv, chunks, bias, scores, weights, attended, sems, in_sems = refs
    tokens, q_cols = attended.shape
    start_qkv(qkv_ref, qkv, q_cols, in_sems)
    by_section(
        lambda: start_rows([wout0_ref], chunks, sems),
        lambda: start_rows(wout1_refs, chunks, sems),
    )
    fill_bias(seq_ref, bias)
    clear_unreached(weights, tokens)
    groups = q_cols // (GROUP_HEADS * HEAD_SIZE)
    pltpu.make_async_copy(qkv.at[:, q_cols:], qkv.at[:, q_cols:], in_sems.at[0]).wait()
    for group in range(groups):
        at = q_cols + group * HEAD_SIZE
        keys = qkv[:, at : at + HEAD_SIZE]
        at = at + groups * HEAD_SIZE
        values_t = qkv[:, at : at + HEAD_SIZE].astype(F32).T.astype(BF)
        wait_group(qkv, in_sems, 1, group)
        for index in range(GROUP_HEADS):
            columns = head_columns(group * GROUP_HEADS + index)
            scores[:, index * tokens : (index + 1) * tokens] = dot_nt(keys, qkv[:, columns])

        def block(queries, lanes, reach):
            weights[:reach, lanes] = weights_of(
                scores[:reach, lanes], bias[:reach, queries]
            ).astype(BF)

        softmax_blocks(tokens, block)
        for index in range(GROUP_HEADS):
            columns = head_columns(group * GROUP_HEADS + index)
            mixed = dot_nn(values_t, weights[:, index * tokens : (index + 1) * tokens])
            attended[:, columns] = mixed.T.astype(BF)
    count, width, _ = chunks.shape
    out = dot_nn(attended[:, :width], landed(chunks, sems, 0)[...])
    for index in range(1, count):
        columns = slice(index * width, (index + 1) * width)
        out = out + dot_nn(attended[:, columns], landed(chunks, sems, index)[...])
    out_ref[...] = out.astype(BF)


def softmax_kernel(seq_ref, qkv_ref, out_ref, qkv, bias, scores, in_sems, out_sems):
    tokens = bias.shape[0]
    groups = out_ref.shape[0]
    q_cols = groups * GROUP_HEADS * HEAD_SIZE
    start_qkv(qkv_ref, qkv, q_cols, in_sems)
    fill_bias(seq_ref, bias)
    pltpu.make_async_copy(qkv.at[:, q_cols:], qkv.at[:, q_cols:], in_sems.at[0]).wait()
    for group in range(groups):
        at = q_cols + group * HEAD_SIZE
        keys = qkv[:, at : at + HEAD_SIZE]
        wait_group(qkv, in_sems, 1, group)
        for index in range(GROUP_HEADS):
            columns = head_columns(group * GROUP_HEADS + index)
            lanes = slice(index * tokens, (index + 1) * tokens)
            scores[group, :, lanes] = dot_nt(keys, qkv[:, columns])

        def block(queries, lanes, reach):
            scores[group, :reach, lanes] = weights_of(
                scores[group, :reach, lanes], bias[:reach, queries]
            )

        softmax_blocks(tokens, block)
        pltpu.make_async_copy(scores.at[group], out_ref.at[group], out_sems.at[group]).start()
    for group in range(groups):
        pltpu.make_async_copy(scores.at[group], out_ref.at[group], out_sems.at[group]).wait()


def backward_kernel(known, pieces, seq_ref, qkv_ref, grads_ref, *refs):
    wq0_refs, (wq1_ref, wkv0_ref, wkv1_ref, *refs) = refs[:pieces], refs[pieces:]
    known_ref, refs = (refs[0], refs[1:]) if known else (None, refs)
    (
        out_ref, qkv, grads, chunks, bias, scores, weight_grads, weights, score_grads, scaled_q,
        scaled_kv, sems, in_sems,
    ) = refs
    tokens, q_cols = grads.shape
    start_qkv(qkv_ref, qkv, q_cols, in_sems)
    groups = q_cols // (GROUP_HEADS * HEAD_SIZE)
    start_groups(grads_ref, grads, q_cols, in_sems, 1 + groups)
    stored = [
        pltpu.make_async_copy(known_ref.at[group], scores.at[group], in_sems.at[5 + group])
        for group in range(groups if known else 0)
    ]
    for copy in stored:
        copy.start()
    by_section(
        lambda: start_joined(wq0_refs, wkv0_ref, chunks, sems),
        lambda: start_joined([wq1_ref], wkv1_ref, chunks, sems),
    )
    if not known:
        fill_bias(seq_ref, bias)
    clear_unreached(weights, tokens)
    clear_unreached(score_grads, tokens)
    kv_cols = groups * HEAD_SIZE
    pltpu.make_async_copy(qkv.at[:, q_cols:], qkv.at[:, q_cols:], in_sems.at[0]).wait()
    scale_lanes = qkv[:, q_cols + 2 * kv_cols :].astype(F32)
    scale_column = jnp.sum(scale_lanes, axis=1, keepdims=True)
    scale_row = jnp.sum(scale_lanes.T, axis=0, keepdims=True) * SOFT
    for group in range(groups):
        at = q_cols + group * HEAD_SIZE
        keys = qkv[:, at : at + HEAD_SIZE]
        keys_t = keys.astype(F32).T.astype(BF)
        at = at + kv_cols
        values = qkv[:, at : at + HEAD_SIZE]
        wait_group(qkv, in_sems, 1, group)
        wait_group(grads, in_sems, 1 + groups, group)
        for index in range(GROUP_HEADS):
            columns = head_columns(group * GROUP_HEADS + index)
            lanes = slice(index * tokens, (index + 1) * tokens)
            if not known:
                scores[group, :, lanes] = dot_nt(keys, qkv[:, columns])
            weight_grads[:, lanes] = dot_nt(values, grads[:, columns])
        if known:
            stored[group].wait()
        def block(queries, lanes, reach):
            weight = scores[group, :reach, lanes]
            if not known:
                weight = weights_of(weight, bias[:reach, queries])
            weights[:reach, lanes] = weight.astype(BF)
            weight_grad = weight_grads[:reach, lanes]
            mean = jnp.sum(weight_grad * weight, axis=0, keepdims=True)
            score_grads[:reach, lanes] = (weight * (weight_grad - mean)).astype(BF)

        softmax_blocks(tokens, block)
        key_grad = jnp.zeros((tokens, HEAD_SIZE), F32)
        value_grad = jnp.zeros((tokens, HEAD_SIZE), F32)
        for index in range(GROUP_HEADS):
            columns = head_columns(group * GROUP_HEADS + index)
            lanes = slice(index * tokens, (index + 1) * tokens)
            score_grad = score_grads[:, lanes]
            scaled_q[columns, :] = (dot_nn(keys_t, score_grad) * scale_row).astype(BF)
            key_grad = key_grad + dot_nn(score_grad, qkv[:, columns])
            value_grad = value_grad + dot_nn(weights[:, lanes], grads[:, columns])
        at = group * HEAD_SIZE
        scaled_kv[:, at : at + HEAD_SIZE] = (key_grad * (scale_column * SOFT)).astype(BF)
        at = at + kv_cols
        scaled_kv[:, at : at + HEAD_SIZE] = (value_grad * scale_column).astype(BF)
    count, width, _ = chunks.shape
    through = dot_nt(landed(chunks, sems, count - 1)[...], scaled_kv[...])
    for index in range(count - 1):
        rows = slice(index * width, (index + 1) * width)
        through = through + dot_nn(landed(chunks, sems, index)[...], scaled_q[rows, :])
    out_ref[...] = through.T.astype(BF)


def merger_kernel(
    marks_ref, owners_ref, last_ref, pair_ref, across_ref, beside_ref, g0_ref, g1_ref, weight_ref,
    out_ref, grad_ref, rows, hidden, counts, places,
):
    added = summed(pair_ref, across_ref, beside_ref)
    rows[...] = last_ref[...].astype(F32) + chosen(g0_ref, g1_ref) * added
    share = grad_ref.shape[0]
    at = pl.multiple_of(lax.axis_index("mp") * share, share)
    grad_ref[...] = rows[pl.ds(at, share), :].astype(BF)
    x = rows[...].astype(BF)
    cols = weight_ref.shape[0]
    for start in range(0, cols, 256):
        hidden[:, start : start + 256] = dot_nt(x, weight_ref[start : start + 256, :])
    dp_count, sections = out_ref.shape[:2]
    owner_count = dp_count * sections

    def clear(owner, carry):
        counts[owner] = 0
        for slot in range(CAP):
            places[owner * CAP + slot] = -1
        return carry

    lax.fori_loop(0, owner_count, clear, 0)

    def place(block, carry):
        owner = owners_ref[0, block]

        @pl.when(marks_ref[0, block] == 1)
        def _():
            slot = counts[owner]
            places[owner * CAP + slot] = block
            counts[owner] = slot + 1

        return carry

    lax.fori_loop(0, marks_ref.shape[1], place, 0)

    def send(owner, carry):
        pieces = []
        for slot in range(CAP):
            block = places[owner * CAP + slot]
            at = pl.multiple_of(jnp.maximum(block, 0) * VB, VB)
            pieces.append(jnp.where(block >= 0, hidden[pl.ds(at, VB), :], 0.0))
        out_ref[lax.rem(owner, dp_count), lax.div(owner, dp_count)] = jnp.concatenate(
            pieces, axis=0
        ).astype(BF)
        return carry

    lax.fori_loop(0, owner_count, send, 0)


def merger_sum_kernel(parts_ref, own_ref, other_ref):
    section = lax.axis_index("section")
    sources = parts_ref.shape[0]

    def total(index):
        return add_parts(lambda source: parts_ref[source, index], sources)

    first, second = total(0), total(1)
    own_ref[...] = jnp.where(section == 0, first, second)
    other_ref[...] = jnp.where(section == 0, second, first).astype(BF)


def gelu_slope(values):
    cumulative = 0.5 * (1.0 + lax.erf(values * (1.0 / math.sqrt(2.0))))
    return cumulative + values * jnp.exp(-0.5 * values * values) * (1.0 / math.sqrt(2.0 * math.pi))


def local(
    embeds,
    cotangent,
    norm_gain,
    w_query,
    w_keyval,
    w_out,
    seq_lengths,
    image_mask,
    block_owner,
    merger_weight,
    merger_pre,
):
    section = lax.axis_index("section")
    mp_count = lax.axis_size("mp")
    dp_count = lax.axis_size("dp")
    rows, width = embeds.shape[1:]
    tokens = rows * mp_count
    share = tokens // dp_count
    q_cols = w_query.shape[3]
    kv_cols = w_keyval.shape[4]
    joined = q_cols + 2 * kv_cols + 128
    emb, cot = embeds[0], cotangent[0]
    wq, wout = w_query[0, 0], w_out[0, 0]
    wkv = w_keyval[0, 0].reshape(width, 2 * kv_cols)
    gain = norm_gain[0]

    def partner(index):
        other, rank = 1 - index // mp_count, (index % mp_count + mp_count // 2) % mp_count
        return other * mp_count + rank

    everyone = range(2 * mp_count)
    from_first = [(i, partner(i)) for i in everyone if i < mp_count]
    from_second = [(i, partner(i)) for i in everyone if i >= mp_count]

    def swap(array, pairs):
        return lax.ppermute(array, ("section", "mp"), pairs)

    def scatter(array, axis):
        return lax.all_to_all(array, axis, split_axis=0, concat_axis=0, tiled=True)

    def spread(copies):
        return scatter(copies, "dp").reshape(tokens, copies.shape[2])

    def gather(array, axis):
        return lax.all_gather(array, axis, axis=0, tiled=True)

    def chunks_of(count):
        return pltpu.VMEM((count, width, width), BF)

    own_x, other_x = jnp.where(section == 0, emb, cot), jnp.where(section == 0, cot, emb)
    received_x = swap(other_x, from_first + from_second)
    gain_x = swap(gain, from_first + from_second)
    def vmem(*shape):
        return pltpu.VMEM(shape, BF)

    def dma(count):
        return pltpu.SemaphoreType.DMA((count,))

    def other_rows_parts(x):
        return pl.pallas_call(
            first_kernel,
            out_shape=pltpu.HBM((dp_count, share, joined), BF),
            in_specs=[VMEM] * 2 + [HBM] * 3,
            out_specs=HBM,
            scratch_shapes=[chunks_of(5), vmem(dp_count, share, joined), dma(5), dma(6)],
            compiler_params=params(24),
            cost_estimate=cost(2 * tokens * width * joined, 6 << 20),
        )(x, gain, *in_hbm(wq, wkv, wout))

    def first_sum(parts):
        return pl.pallas_call(
            first_sum_kernel,
            out_shape=shape_of((share, joined), BF),
            in_specs=[ANY],
            out_specs=VMEM,
            scratch_shapes=[vmem(dp_count, share, joined), dma(6)],
            compiler_params=params(24),
            cost_estimate=cost(parts.size, 2 << 20),
        )(parts)

    def summed_copies(adder, parts):
        cols = parts.shape[2]
        return pl.pallas_call(
            functools.partial(sum_kernel, adder),
            out_shape=pltpu.HBM((dp_count, share, cols), BF),
            in_specs=[ANY],
            out_specs=HBM,
            scratch_shapes=[vmem(dp_count, share, cols), vmem(share, cols), dma(6), dma(dp_count)],
            compiler_params=params(24),
            cost_estimate=cost(parts.size, 4 << 20),
        )(parts)

    def chosen_copies(first, second, cols):
        return pl.pallas_call(
            choose_kernel,
            out_shape=pltpu.HBM((dp_count, share, cols), BF),
            in_specs=[VMEM] * 2,
            out_specs=HBM,
            scratch_shapes=[dma(dp_count)],
            compiler_params=params(24),
            cost_estimate=cost(0, 2 << 20),
        )(first, second)

    def loaded(joins, firsts, seconds):
        count = 5 if joins else 4
        return pl.pallas_call(
            functools.partial(load_kernel, joins, len(firsts)),
            out_shape=pltpu.VMEM((count, width, width), BF),
            in_specs=[HBM] * (len(firsts) + len(seconds)),
            out_specs=VMEM,
            scratch_shapes=[dma(count)],
            compiler_params=params(16),
            cost_estimate=cost(0, 5 << 20),
        )(*in_hbm(*firsts, *seconds))

    def beside(array, distance):
        return lax.ppermute(array, "mp", [(i, i ^ distance) for i in range(mp_count)])

    def sum_over_mp(part, *later):
        mate = beside(part, 1)
        at = lax.axis_index("mp") % 2 * (tokens // 2)

        def half(array):
            return lax.dynamic_slice_in_dim(array, at, tokens // 2).astype(F32)

        pair_half = (half(part) + half(mate)).astype(BF)
        across = beside(pair_half, 2)
        pair_half, part, mate, *later = lax.optimization_barrier((pair_half, part, mate, *later))
        pair = (part.astype(F32) + mate.astype(F32)).astype(BF)
        return (pair, across, beside(across, 1)), later

    around = [beside(own_x, distance) for distance in (1, 2, 3)]
    first_chunks = pl.pallas_call(
        first_load_kernel,
        out_shape=pltpu.VMEM((5, width, width), BF),
        in_specs=[HBM] * 3,
        out_specs=VMEM,
        scratch_shapes=[dma(5)],
        compiler_params=params(16),
        cost_estimate=cost(0, 5 << 20),
    )(*in_hbm(wq, wkv, wout))
    own_parts, own_all = pl.pallas_call(
        first_own_kernel,
        out_shape=[pltpu.HBM((dp_count, share, joined), BF), shape_of((tokens, width), BF)],
        in_specs=[VMEM] * 6,
        out_specs=[HBM, VMEM],
        scratch_shapes=[
            pltpu.VMEM((tokens, width), F32),
            vmem(dp_count, share, joined),
            dma(6),
        ],
        compiler_params=params(24),
        cost_estimate=cost(2 * tokens * width * joined, 6 << 20),
    )(own_x, *around, gain, first_chunks)
    own_parts, received_x, gain_x, wq_s, wout_s = lax.optimization_barrier(
        (own_parts, received_x, gain_x, wq, wout)
    )
    own_parts = scatter(own_parts, "dp")
    wq_b = swap(wq_s, from_second)
    cuts = (5 * q_cols // 16, 5 * q_cols // 8)
    wout_a0 = swap(wout_s[: cuts[0]], from_first)
    wout_a1, wout_a2 = wout_s[cuts[0] : cuts[1]], wout_s[cuts[1] :]
    other_parts = other_rows_parts(gather(received_x, "mp"))
    own_parts, other_parts, wout_a0, wout_a1, wout_a2 = lax.optimization_barrier(
        (own_parts, other_parts, wout_a0, wout_a1, wout_a2)
    )
    wout_a1 = swap(wout_a1, from_first)
    own = first_sum(own_parts)
    mine_all = gather(other_x, "mp")
    other_parts, own, mine_all, wout_a1 = lax.optimization_barrier(
        (scatter(other_parts, "dp"), own, mine_all, wout_a1)
    )
    other = first_sum(other_parts)
    received = swap(other, from_first)
    received_grad, wkv_s = lax.optimization_barrier((swap(other, from_second), wkv))
    wkv_b = swap(wkv_s, from_second)
    copies, wout_a2 = lax.optimization_barrier((chosen_copies(own, received, joined), wout_a2))
    wout_a2 = swap(wout_a2, from_first)
    grad_copies = chosen_copies(received_grad, own, q_cols)
    qkv_first, grad_copies, wout_a2, wq_b, wq_s, wkv_s = lax.optimization_barrier(
        (spread(copies), grad_copies, wout_a2, wq_b, wq, wkv)
    )
    wout_a = (wout_a0, wout_a1, wout_a2)
    wq_a, wkv_a = swap(wq_s, from_first), swap(wkv_s, from_first)
    head_grad_last = spread(grad_copies)

    def layer_forward(qkv, wouts):
        out = pl.pallas_call(
            forward_kernel,
            out_shape=shape_of((tokens, width), BF),
            in_specs=[SMEM, ANY] + [HBM] * (1 + len(wouts[1])),
            out_specs=VMEM,
            scratch_shapes=[
                vmem(tokens, joined),
                chunks_of(4),
                pltpu.VMEM((tokens, tokens), F32),
                pltpu.VMEM((tokens, GROUP_HEADS * tokens), F32),
                vmem(tokens, GROUP_HEADS * tokens),
                vmem(tokens, q_cols),
                dma(4),
                dma(3),
            ],
            compiler_params=params(32),
            cost_estimate=cost(6 * tokens * tokens * q_cols, 4 << 20),
        )(seq_lengths, qkv, *in_hbm(wouts[0], *wouts[1]))
        return out

    def rows_after(resident, sums):
        even = lax.axis_index("mp") % 2 == 0
        lower, upper = jnp.where(even, *sums[1:]), jnp.where(even, *sums[:0:-1])
        added = sums[0].astype(F32) + jnp.concatenate([lower, upper], axis=0).astype(F32)
        return (resident.astype(F32) + added).astype(BF)

    out, wkv_b = lax.optimization_barrier((layer_forward(qkv_first, (wout, wout_a)), wkv_b))
    sums, pieces = sum_over_mp(out, wq_b, wkv_b, wq, wkv)
    joined_last = loaded(True, pieces[:2], pieces[2:])
    parts = pl.pallas_call(
        project_kernel,
        out_shape=pltpu.HBM((dp_count, share, joined), BF),
        in_specs=[VMEM] * 8,
        out_specs=HBM,
        scratch_shapes=[vmem(dp_count, share, joined), dma(6)],
        compiler_params=params(24),
        cost_estimate=cost(2 * tokens * width * joined, 6 << 20),
    )(own_all, mine_all, *sums, gain_x, gain, joined_last)
    parts, head_grad_last = lax.optimization_barrier((parts, head_grad_last))
    qkv_last = spread(summed_copies(scaled_sum, scatter(parts, "dp")))
    wout_b = swap(wout, from_second)
    wout_last = jnp.where(section == 0, wout_b, wout)
    h_one = rows_after(jnp.where(section == 0, own_all, mine_all), sums)
    rows_after(h_one, sum_over_mp(layer_forward(qkv_last, (wout_last, (wout_last,))))[0])

    def layer_backward(qkv, head_grads, wqs, wkvs, *known, later=()):
        through = pl.pallas_call(
            functools.partial(backward_kernel, len(known), len(wqs[0])),
            out_shape=shape_of((tokens, width), BF),
            in_specs=[SMEM, ANY, ANY] + [HBM] * (3 + len(wqs[0]) + len(known)),
            out_specs=VMEM,
            scratch_shapes=[
                vmem(tokens, joined),
                vmem(tokens, q_cols),
                chunks_of(5),
                pltpu.VMEM((tokens, tokens), F32),
                pltpu.VMEM((groups, tokens, GROUP_HEADS * tokens), F32),
                pltpu.VMEM((tokens, GROUP_HEADS * tokens), F32),
                vmem(tokens, GROUP_HEADS * tokens),
                vmem(tokens, GROUP_HEADS * tokens),
                vmem(q_cols, tokens),
                vmem(tokens, 2 * kv_cols),
                dma(5),
                dma(7),
            ],
            compiler_params=params(32),
            cost_estimate=cost(12 * tokens * tokens * q_cols, 6 << 20),
        )(seq_lengths, qkv, head_grads, *in_hbm(*wqs[0], *wqs[1], *wkvs, *known))
        return sum_over_mp(through, *later)

    groups = kv_cols // HEAD_SIZE
    sums, pieces = layer_backward(
        qkv_last,
        *in_hbm(head_grad_last),
        ((wq_b,), (wq,)),
        (wkv_b, wkv),
        later=(wout, *wout_a),
    )
    parts, grad_one = pl.pallas_call(
        head_grad_kernel,
        out_shape=[pltpu.HBM((dp_count, share, q_cols), BF), shape_of((tokens, width), BF)],
        in_specs=[VMEM] * 8,
        out_specs=[HBM, VMEM],
        scratch_shapes=[vmem(dp_count, share, q_cols), dma(4)],
        compiler_params=params(24),
        cost_estimate=cost(2 * tokens * width * q_cols, 4 << 20),
    )(mine_all, own_all, *sums, gain_x, gain, loaded(False, pieces[:1], pieces[1:]))
    parts, qkv_late = lax.optimization_barrier((parts, qkv_first))
    softmax_first = pl.pallas_call(
        softmax_kernel,
        out_shape=pltpu.HBM((groups, tokens, GROUP_HEADS * tokens), F32),
        in_specs=[SMEM, ANY],
        out_specs=HBM,
        scratch_shapes=[
            vmem(tokens, joined),
            pltpu.VMEM((tokens, tokens), F32),
            pltpu.VMEM((groups, tokens, GROUP_HEADS * tokens), F32),
            dma(3),
            dma(2),
        ],
        compiler_params=params(32),
        cost_estimate=cost(4 * tokens * tokens * q_cols, 6 << 20),
    )(seq_lengths, *in_hbm(qkv_late))
    parts, softmax_first, wq_a, wkv_a = lax.optimization_barrier(
        (scatter(parts, "dp"), softmax_first, wq_a, wkv_a)
    )
    head_grad_first = spread(summed_copies(plain_sum, parts))
    sums, _ = layer_backward(
        *in_hbm(qkv_late), head_grad_first, ((wq,), (wq_a,)), (wkv, wkv_a), softmax_first
    )

    hidden_cols = merger_weight.shape[0]
    outgoing, input_grad = pl.pallas_call(
        merger_kernel,
        out_shape=[
            shape_of((dp_count, 2, CAP * VB, hidden_cols), BF),
            shape_of((rows, width), BF),
        ],
        in_specs=[SMEM, SMEM] + [VMEM] * 7,
        out_specs=[VMEM] * 2,
        scratch_shapes=[
            pltpu.VMEM((tokens, width), F32),
            pltpu.VMEM((tokens, hidden_cols), F32),
            pltpu.SMEM((2 * dp_count,), jnp.int32),
            pltpu.SMEM((2 * dp_count * CAP,), jnp.int32),
        ],
        compiler_params=params(24),
    )(image_mask, block_owner, grad_one, *sums, gain, gain_x, merger_weight)
    kept, passed = pl.pallas_call(
        merger_sum_kernel,
        out_shape=[
            shape_of((CAP * VB, hidden_cols), F32),
            shape_of((CAP * VB, hidden_cols), BF),
        ],
        in_specs=[VMEM],
        out_specs=[VMEM] * 2,
        compiler_params=params(24),
    )(scatter(outgoing, "dp"))
    crossed = lax.ppermute(passed, "section", [(0, 1), (1, 0)]).astype(F32)
    first = jnp.where(section == 0, kept, crossed)
    second = jnp.where(section == 0, crossed, kept)
    hidden_grad = jnp.stack([first, second]).reshape(2, CAP, VB, hidden_cols)
    merger_grad = gelu_slope(merger_pre[0].astype(F32)) * hidden_grad
    return (input_grad[None], merger_grad[None])


def solution(mesh):
    placed = (
        P("section", "mp", "dp"),
        P("section", "mp", "dp"),
        P(None, "section", "dp"),
        P(None, "section", "dp", "mp"),
        P(None, "section", "dp", None, "mp"),
        P(None, "section", "mp", "dp"),
        P(),
        P("section", None),
        P("section", None),
        P("mp", "dp"),
        P(("section", "dp"), None, None, None, "mp"),
    )
    return jax.shard_map(
        local,
        mesh=mesh,
        in_specs=placed,
        out_specs=(P("section", "mp", "dp"), P(("section", "dp"), None, None, None, "mp")),
        check_vma=False,
    )
```

```python
import functools
import math

import jax
import jax.numpy as jnp
from jax import lax
from jax.experimental import pallas as pl
from jax.experimental.pallas import tpu as pltpu
from jax.sharding import PartitionSpec as P

MODEL_WIDTH = 8192
HEAD_SIZE = 128
GROUP_HEADS = 8
CAP = 2
VB = 8
NSEQ = 3

EPSILON = 1e-06
MASKED = -1e30
SOFT = 1.0 / math.sqrt(HEAD_SIZE)
LOG2E = math.log2(math.e)
QB = 128

BF = jnp.bfloat16
F32 = jnp.float32

VMEM = pl.BlockSpec(memory_space=pltpu.VMEM)
SMEM = pl.BlockSpec(memory_space=pltpu.SMEM)
ANY = pl.BlockSpec(memory_space=pl.ANY)
HBM = pl.BlockSpec(memory_space=pltpu.HBM)


def shape_of(shape, dtype):
    return jax.ShapeDtypeStruct(shape, dtype)


def in_hbm(*arrays):
    return [pltpu.with_memory_space_constraint(array, pltpu.HBM) for array in arrays]


def params(mebibytes):
    return pltpu.CompilerParams(vmem_limit_bytes=mebibytes << 20)


def cost(flops, bytes_accessed):
    return pl.CostEstimate(flops=flops, bytes_accessed=bytes_accessed, transcendentals=0)


def dot_nn(left, right):
    return jnp.dot(left, right, preferred_element_type=F32)


def dot_nt(left, right):
    return lax.dot_general(left, right, (((1,), (1,)), ((), ())), preferred_element_type=F32)


def two_lanes(column):
    high = column.astype(BF).astype(F32)
    lane = lax.broadcasted_iota(jnp.int32, (column.shape[0], 128), 1)
    return jnp.where(lane == 0, high, jnp.where(lane == 1, column - high, 0.0)).astype(BF)


def start_columns(sources, chunks, sems):
    width, index = chunks.shape[2], 0
    for source in sources:
        for start in range(0, source.shape[1], width):
            block = source.at[:, start : start + width]
            pltpu.make_async_copy(block, chunks.at[index], sems.at[index]).start()
            index += 1


def start_rows(sources, chunks, sems):
    rows, at = chunks.shape[1], 0
    for source in sources:
        start = 0
        while start < source.shape[0]:
            index, within = at // rows, at % rows
            count = min(rows - within, source.shape[0] - start)
            block = source.at[start : start + count, :]
            place = chunks.at[index, within : within + count, :]
            pltpu.make_async_copy(block, place, sems.at[index]).start()
            start, at = start + count, at + count


def start_joined(wqs, wkv_ref, chunks, sems):
    start_columns(wqs, chunks, sems)
    last = chunks.shape[0] - 1
    pltpu.make_async_copy(wkv_ref, chunks.at[last], sems.at[last]).start()


def landed(chunks, sems, index):
    pltpu.make_async_copy(chunks.at[index], chunks.at[index], sems.at[index]).wait()
    return chunks.at[index]


def by_section(first, second):
    section = lax.axis_index("section")
    pl.when(section == 0)(first)
    pl.when(section != 0)(second)


def spans(cols):
    return [slice(start, min(start + 512, cols)) for start in range(0, cols, 512)]


def start_spans(source, target, sems):
    for index, span in enumerate(spans(target.shape[-1])):
        at = (slice(None),) * (len(target.shape) - 1) + (span,)
        pltpu.make_async_copy(source.at[at], target.at[at], sems.at[index]).start()


def wait_span(target, sems, index):
    at = (slice(None),) * (len(target.shape) - 1) + (spans(target.shape[-1])[index],)
    pltpu.make_async_copy(target.at[at], target.at[at], sems.at[index]).wait()


def sender(staged, out_ref, sems):
    owners, share, cols = staged.shape

    def put(start, tile):
        span = slice(start, start + tile.shape[1])
        staged[:, :, span] = tile.reshape(owners, share, tile.shape[1])
        index = spans(cols).index(span)
        at = (slice(None), slice(None), span)
        pltpu.make_async_copy(staged.at[at], out_ref.at[at], sems.at[index]).start()

    def finish():
        for index in range(len(spans(cols))):
            wait_span(staged, sems, index)

    return put, finish


def repeat_out(tile, out_ref, sems):
    for place in range(out_ref.shape[0]):
        pltpu.make_async_copy(tile, out_ref.at[place], sems.at[place]).start()


def repeat_wait(tile, out_ref, sems):
    for place in range(out_ref.shape[0]):
        pltpu.make_async_copy(tile, out_ref.at[place], sems.at[place]).wait()


def project_rows(rows, gain, chunks, chunk_at, put):
    rows_f = rows.astype(F32)
    normed = (rows_f * gain).astype(BF)
    count, _, width = chunks.shape
    put(count * width, two_lanes(jnp.sum(rows_f * rows_f, axis=1, keepdims=True)))
    for index in range(count):
        put(index * width, dot_nn(normed, chunk_at(index)[...]).astype(BF))


def load_kernel(joined, pieces, *refs):
    *sources, out_ref, sems = refs

    def load(refs):
        if joined:
            start_joined(refs[:-1], refs[-1], out_ref, sems)
        else:
            start_rows(refs, out_ref, sems)

    by_section(lambda: load(sources[:pieces]), lambda: load(sources[pieces:]))
    for index in range(out_ref.shape[0]):
        landed(out_ref, sems, index)


def first_kernel(
    x_ref, gain_ref, wq_ref, wkv_ref, wout_ref, out_ref, chunks, staged, sems, out_sems
):
    put, finish = sender(staged, out_ref, out_sems)
    tokens = x_ref.shape[0]

    def rows():
        return jnp.concatenate([x_ref[tokens // 2 :, :], x_ref[: tokens // 2, :]], axis=0)

    def first():
        start_joined([wq_ref], wkv_ref, chunks, sems)
        project_rows(rows(), gain_ref[...], chunks, lambda at: landed(chunks, sems, at), put)

    def second():
        start_rows([wout_ref], chunks, sems)
        count, width, _ = chunks.shape
        put(count * width, jnp.zeros((tokens, 128), BF))
        put((count - 1) * width, jnp.zeros((tokens, width), BF))
        x = rows()
        for index in range(count - 1):
            put(index * width, dot_nt(x, landed(chunks, sems, index)[...]).astype(BF))

    by_section(first, second)
    finish()


def first_load_kernel(wq_ref, wkv_ref, wout_ref, out_ref, sems):
    def wait(count):
        for index in range(count):
            landed(out_ref, sems, index)

    def first():
        start_joined([wq_ref], wkv_ref, out_ref, sems)
        wait(out_ref.shape[0])

    def second():
        start_rows([wout_ref], out_ref, sems)
        wait(out_ref.shape[0] - 1)

    by_section(first, second)


def first_own_kernel(
    mine_ref, near_ref, far_ref, cross_ref, gain_ref, chunks, out_ref, x_ref, x, staged, out_sems
):
    rank = lax.axis_index("mp")
    share = mine_ref.shape[0]
    for distance, ref in enumerate((mine_ref, near_ref, far_ref, cross_ref)):
        at = pl.multiple_of(jnp.bitwise_xor(rank, distance) * share, share)
        x[pl.ds(at, share), :] = ref[...].astype(F32)
    x_ref[...] = x[...].astype(BF)
    put, finish = sender(staged, out_ref, out_sems)
    tokens = x_ref.shape[0]
    count, width, _ = chunks.shape

    def first():
        project_rows(x_ref[...], gain_ref[...], chunks, lambda at: chunks.at[at], put)

    def second():
        put(count * width, jnp.zeros((tokens, 128), BF))
        put((count - 1) * width, jnp.zeros((tokens, width), BF))
        for index in range(count - 1):
            put(index * width, dot_nt(x_ref[...], chunks[index]).astype(BF))

    by_section(first, second)
    finish()


def chosen(first_ref, second_ref):
    return jnp.where(lax.axis_index("section") == 0, first_ref[...], second_ref[...])


def summed(pair_ref, across_ref, beside_ref):
    even = lax.axis_index("mp") % 2 == 0
    lower = jnp.where(even, across_ref[...], beside_ref[...])
    upper = jnp.where(even, beside_ref[...], across_ref[...])
    return pair_ref[...].astype(F32) + jnp.concatenate([lower, upper], axis=0).astype(F32)


def project_kernel(
    r0_ref, r1_ref, pair_ref, across_ref, beside_ref, g0_ref, g1_ref, chunks, out_ref,
    staged, out_sems,
):
    added = summed(pair_ref, across_ref, beside_ref)
    rows = (chosen(r0_ref, r1_ref).astype(F32) + added).astype(BF)
    put, finish = sender(staged, out_ref, out_sems)
    project_rows(rows, chosen(g0_ref, g1_ref), chunks, lambda at: chunks.at[at], put)
    finish()


def head_grad_kernel(
    r0_ref, r1_ref, pair_ref, across_ref, beside_ref, g0_ref, g1_ref, chunks, out_ref, rows_ref,
    staged, out_sems,
):
    added = summed(pair_ref, across_ref, beside_ref)
    rows = chosen(r0_ref, r1_ref).astype(F32) + chosen(g0_ref, g1_ref) * added
    rows_ref[...] = rows.astype(BF)
    count, width, _ = chunks.shape
    put, finish = sender(staged, out_ref, out_sems)
    for index in range(count):
        put(index * width, dot_nt(rows_ref[...], chunks[index]).astype(BF))
    finish()


def add_parts(load, count):
    total = load(0).astype(F32)
    for index in range(1, count):
        total = total + load(index).astype(F32)
    return total


def part_sums(parts, sems):
    def total(index):
        wait_span(parts, sems, index)
        span = spans(parts.shape[2])[index]
        return add_parts(lambda source: parts[source, :, span], parts.shape[0])

    return total


def scaled_sum(total, tile):
    ranges = spans(tile.shape[1])
    squares = jnp.sum(total(len(ranges) - 1), axis=1, keepdims=True)
    scale = lax.rsqrt(squares / MODEL_WIDTH + EPSILON)
    for index, span in enumerate(ranges[:-1]):
        tile[:, span] = (total(index) * scale).astype(BF)
    tile[:, ranges[-1]] = two_lanes(scale)


def plain_sum(total, tile):
    for index, span in enumerate(spans(tile.shape[1])):
        tile[:, span] = total(index).astype(BF)


def first_sum_kernel(parts_ref, out_ref, parts, sems):
    start_spans(parts_ref, parts, sems)
    total = part_sums(parts, sems)
    by_section(lambda: scaled_sum(total, out_ref), lambda: plain_sum(total, out_ref))


def sum_kernel(adder, parts_ref, out_ref, parts, tile, sems, out_sems):
    start_spans(parts_ref, parts, sems)
    adder(part_sums(parts, sems), tile)
    repeat_out(tile, out_ref, out_sems)
    repeat_wait(tile, out_ref, out_sems)


def choose_kernel(first_ref, second_ref, out_ref, sems):
    first = first_ref.at[:, : out_ref.shape[2]]
    second = second_ref.at[:, : out_ref.shape[2]]
    by_section(
        lambda: repeat_out(first, out_ref, sems), lambda: repeat_out(second, out_ref, sems)
    )
    repeat_wait(first, out_ref, sems)


def fill_bias(seq_ref, bias):
    section = lax.axis_index("section")
    tokens = bias.shape[0]
    keys = lax.broadcasted_iota(jnp.int32, (tokens, tokens), 0)
    queries = lax.broadcasted_iota(jnp.int32, (tokens, tokens), 1)
    key_segment = jnp.zeros((tokens, tokens), jnp.int32)
    query_segment = jnp.zeros((tokens, tokens), jnp.int32)
    bound = 0
    for index in range(NSEQ):
        bound = bound + seq_ref[section, index]
        key_segment = key_segment + (keys >= bound).astype(jnp.int32)
        query_segment = query_segment + (queries >= bound).astype(jnp.int32)
    allowed = (keys <= queries) & (key_segment == query_segment)
    bias[...] = jnp.where(allowed, 0.0, MASKED)


def head_columns(head):
    return slice(head * HEAD_SIZE, (head + 1) * HEAD_SIZE)


def softmax_blocks(tokens, body):
    def one_head(head, carry):
        for at in range(0, tokens, QB):
            lanes = pl.ds(pl.multiple_of(head * tokens + at, QB), QB)
            body(slice(at, at + QB), lanes, at + QB)
        return carry

    lax.fori_loop(0, GROUP_HEADS, one_head, 0, unroll=4)


def clear_unreached(target, tokens):
    for head in range(GROUP_HEADS):
        for at in range(0, tokens - QB, QB):
            lanes = slice(head * tokens + at, head * tokens + at + QB)
            target[at + QB :, lanes] = jnp.zeros((tokens - at - QB, QB), target.dtype)


def weights_of(scores, bias):
    scores = scores * (SOFT * LOG2E) + bias
    raised = jnp.exp2(scores - jnp.max(scores, axis=0, keepdims=True))
    return raised * (1.0 / jnp.sum(raised, axis=0, keepdims=True))


def start_qkv(qkv_ref, qkv, q_cols, sems):
    pltpu.make_async_copy(qkv_ref.at[:, q_cols:], qkv.at[:, q_cols:], sems.at[0]).start()
    for group in range(q_cols // (GROUP_HEADS * HEAD_SIZE)):
        start_group(qkv_ref, qkv, sems, 1, group)


def start_group(source, target, sems, first, group):
    width = GROUP_HEADS * HEAD_SIZE
    at = (slice(None), slice(group * width, (group + 1) * width))
    pltpu.make_async_copy(source.at[at], target.at[at], sems.at[first + group]).start()


def wait_group(target, sems, first, group):
    width = GROUP_HEADS * HEAD_SIZE
    at = (slice(None), slice(group * width, (group + 1) * width))
    pltpu.make_async_copy(target.at[at], target.at[at], sems.at[first + group]).wait()


def forward_kernel(seq_ref, qkv_ref, wout0_ref, *refs):
    *wout1_refs, out_ref, qkv, chunks, bias, scores, weights, attended, sems, in_sems = refs
    tokens, q_cols = attended.shape
    start_qkv(qkv_ref, qkv, q_cols, in_sems)
    by_section(
        lambda: start_rows([wout0_ref], chunks, sems),
        lambda: start_rows(wout1_refs, chunks, sems),
    )
    fill_bias(seq_ref, bias)
    clear_unreached(weights, tokens)
    groups = q_cols // (GROUP_HEADS * HEAD_SIZE)
    pltpu.make_async_copy(qkv.at[:, q_cols:], qkv.at[:, q_cols:], in_sems.at[0]).wait()
    for group in range(groups):
        at = q_cols + group * HEAD_SIZE
        keys = qkv[:, at : at + HEAD_SIZE]
        at = at + groups * HEAD_SIZE
        values_t = qkv[:, at : at + HEAD_SIZE].astype(F32).T.astype(BF)
        wait_group(qkv, in_sems, 1, group)
        for index in range(GROUP_HEADS):
            columns = head_columns(group * GROUP_HEADS + index)
            scores[:, index * tokens : (index + 1) * tokens] = dot_nt(keys, qkv[:, columns])

        def block(queries, lanes, reach):
            weights[:reach, lanes] = weights_of(
                scores[:reach, lanes], bias[:reach, queries]
            ).astype(BF)

        softmax_blocks(tokens, block)
        for index in range(GROUP_HEADS):
            columns = head_columns(group * GROUP_HEADS + index)
            mixed = dot_nn(values_t, weights[:, index * tokens : (index + 1) * tokens])
            attended[:, columns] = mixed.T.astype(BF)
    count, width, _ = chunks.shape
    out = dot_nn(attended[:, :width], landed(chunks, sems, 0)[...])
    for index in range(1, count):
        columns = slice(index * width, (index + 1) * width)
        out = out + dot_nn(attended[:, columns], landed(chunks, sems, index)[...])
    out_ref[...] = out.astype(BF)


def backward_kernel(
    seq_ref, qkv_ref, grads_ref, wq0_ref, wq1_ref, wkv0_ref, wkv1_ref, out_ref,
    qkv, grads, chunks, bias, scores, weight_grads, weights, score_grads, scaled_q, scaled_kv,
    sems, in_sems,
):
    tokens, q_cols = grads.shape
    groups = q_cols // (GROUP_HEADS * HEAD_SIZE)
    pltpu.make_async_copy(qkv_ref.at[:, q_cols:], qkv.at[:, q_cols:], in_sems.at[0]).start()
    start_group(qkv_ref, qkv, in_sems, 1, 0)
    start_group(grads_ref, grads, in_sems, 1 + groups, 0)
    fill_bias(seq_ref, bias)
    clear_unreached(weights, tokens)
    clear_unreached(score_grads, tokens)
    kv_cols = groups * HEAD_SIZE
    pltpu.make_async_copy(qkv.at[:, q_cols:], qkv.at[:, q_cols:], in_sems.at[0]).wait()
    wait_group(qkv, in_sems, 1, 0)
    wait_group(grads, in_sems, 1 + groups, 0)
    for group in range(1, groups):
        start_group(qkv_ref, qkv, in_sems, 1, group)
        start_group(grads_ref, grads, in_sems, 1 + groups, group)
    by_section(
        lambda: start_joined([wq0_ref], wkv0_ref, chunks, sems),
        lambda: start_joined([wq1_ref], wkv1_ref, chunks, sems),
    )
    scale_lanes = qkv[:, q_cols + 2 * kv_cols :].astype(F32)
    scale_column = jnp.sum(scale_lanes, axis=1, keepdims=True)
    scale_row = jnp.sum(scale_lanes.T, axis=0, keepdims=True) * SOFT
    for group in range(groups):
        at = q_cols + group * HEAD_SIZE
        keys = qkv[:, at : at + HEAD_SIZE]
        keys_t = keys.astype(F32).T.astype(BF)
        at = at + kv_cols
        values = qkv[:, at : at + HEAD_SIZE]
        if group > 0:
            wait_group(qkv, in_sems, 1, group)
            wait_group(grads, in_sems, 1 + groups, group)
        for index in range(GROUP_HEADS):
            columns = head_columns(group * GROUP_HEADS + index)
            lanes = slice(index * tokens, (index + 1) * tokens)
            scores[:, lanes] = dot_nt(keys, qkv[:, columns])
            weight_grads[:, lanes] = dot_nt(values, grads[:, columns])
        def block(queries, lanes, reach):
            weight = weights_of(scores[:reach, lanes], bias[:reach, queries])
            weights[:reach, lanes] = weight.astype(BF)
            weight_grad = weight_grads[:reach, lanes]
            mean = jnp.sum(weight_grad * weight, axis=0, keepdims=True)
            score_grads[:reach, lanes] = (weight * (weight_grad - mean)).astype(BF)

        softmax_blocks(tokens, block)
        key_grad = jnp.zeros((tokens, HEAD_SIZE), F32)
        value_grad = jnp.zeros((tokens, HEAD_SIZE), F32)
        for index in range(GROUP_HEADS):
            columns = head_columns(group * GROUP_HEADS + index)
            lanes = slice(index * tokens, (index + 1) * tokens)
            score_grad = score_grads[:, lanes]
            scaled_q[columns, :] = (dot_nn(keys_t, score_grad) * scale_row).astype(BF)
            key_grad = key_grad + dot_nn(score_grad, qkv[:, columns])
            value_grad = value_grad + dot_nn(weights[:, lanes], grads[:, columns])
        at = group * HEAD_SIZE
        scaled_kv[:, at : at + HEAD_SIZE] = (key_grad * (scale_column * SOFT)).astype(BF)
        at = at + kv_cols
        scaled_kv[:, at : at + HEAD_SIZE] = (value_grad * scale_column).astype(BF)
    count, width, _ = chunks.shape
    through = dot_nt(landed(chunks, sems, count - 1)[...], scaled_kv[...])
    for index in range(count - 1):
        rows = slice(index * width, (index + 1) * width)
        through = through + dot_nn(landed(chunks, sems, index)[...], scaled_q[rows, :])
    out_ref[...] = through.T.astype(BF)


def merger_kernel(
    marks_ref, owners_ref, last_ref, pair_ref, across_ref, beside_ref, g0_ref, g1_ref, weight_ref,
    out_ref, grad_ref, rows, hidden, counts, places,
):
    added = summed(pair_ref, across_ref, beside_ref)
    rows[...] = last_ref[...].astype(F32) + chosen(g0_ref, g1_ref) * added
    share = grad_ref.shape[0]
    at = pl.multiple_of(lax.axis_index("mp") * share, share)
    grad_ref[...] = rows[pl.ds(at, share), :].astype(BF)
    x = rows[...].astype(BF)
    cols = weight_ref.shape[0]
    for start in range(0, cols, 256):
        hidden[:, start : start + 256] = dot_nt(x, weight_ref[start : start + 256, :])
    dp_count, sections = out_ref.shape[:2]
    owner_count = dp_count * sections

    def clear(owner, carry):
        counts[owner] = 0
        for slot in range(CAP):
            places[owner * CAP + slot] = -1
        return carry

    lax.fori_loop(0, owner_count, clear, 0)

    def place(block, carry):
        owner = owners_ref[0, block]

        @pl.when(marks_ref[0, block] == 1)
        def _():
            slot = counts[owner]
            places[owner * CAP + slot] = block
            counts[owner] = slot + 1

        return carry

    lax.fori_loop(0, marks_ref.shape[1], place, 0)

    def send(owner, carry):
        pieces = []
        for slot in range(CAP):
            block = places[owner * CAP + slot]
            at = pl.multiple_of(jnp.maximum(block, 0) * VB, VB)
            pieces.append(jnp.where(block >= 0, hidden[pl.ds(at, VB), :], 0.0))
        out_ref[lax.rem(owner, dp_count), lax.div(owner, dp_count)] = jnp.concatenate(
            pieces, axis=0
        ).astype(BF)
        return carry

    lax.fori_loop(0, owner_count, send, 0)


def merger_sum_kernel(parts_ref, own_ref, other_ref):
    section = lax.axis_index("section")
    sources = parts_ref.shape[0]

    def total(index):
        return add_parts(lambda source: parts_ref[source, index], sources)

    first, second = total(0), total(1)
    own_ref[...] = jnp.where(section == 0, first, second)
    other_ref[...] = jnp.where(section == 0, second, first).astype(BF)


def gelu_slope(values):
    cumulative = 0.5 * (1.0 + lax.erf(values * (1.0 / math.sqrt(2.0))))
    return cumulative + values * jnp.exp(-0.5 * values * values) * (1.0 / math.sqrt(2.0 * math.pi))


def local(
    embeds,
    cotangent,
    norm_gain,
    w_query,
    w_keyval,
    w_out,
    seq_lengths,
    image_mask,
    block_owner,
    merger_weight,
    merger_pre,
):
    section = lax.axis_index("section")
    mp_count = lax.axis_size("mp")
    dp_count = lax.axis_size("dp")
    rows, width = embeds.shape[1:]
    tokens = rows * mp_count
    share = tokens // dp_count
    q_cols = w_query.shape[3]
    kv_cols = w_keyval.shape[4]
    joined = q_cols + 2 * kv_cols + 128
    emb, cot = embeds[0], cotangent[0]
    wq, wout = w_query[0, 0], w_out[0, 0]
    wkv = w_keyval[0, 0].reshape(width, 2 * kv_cols)
    gain = norm_gain[0]

    def partner(index):
        other, rank = 1 - index // mp_count, (index % mp_count + mp_count // 2) % mp_count
        return other * mp_count + rank

    everyone = range(2 * mp_count)
    from_first = [(i, partner(i)) for i in everyone if i < mp_count]
    from_second = [(i, partner(i)) for i in everyone if i >= mp_count]

    def swap(array, pairs):
        return lax.ppermute(array, ("section", "mp"), pairs)

    def scatter(array, axis):
        return lax.all_to_all(array, axis, split_axis=0, concat_axis=0, tiled=True)

    def spread(copies):
        return scatter(copies, "dp").reshape(tokens, copies.shape[2])

    def gather(array, axis):
        return lax.all_gather(array, axis, axis=0, tiled=True)

    def chunks_of(count):
        return pltpu.VMEM((count, width, width), BF)

    own_x, other_x = jnp.where(section == 0, emb, cot), jnp.where(section == 0, cot, emb)
    received_x = swap(other_x, from_first + from_second)
    gain_x = swap(gain, from_first + from_second)
    def vmem(*shape):
        return pltpu.VMEM(shape, BF)

    def dma(count):
        return pltpu.SemaphoreType.DMA((count,))

    def other_rows_parts(x):
        return pl.pallas_call(
            first_kernel,
            out_shape=pltpu.HBM((dp_count, share, joined), BF),
            in_specs=[VMEM] * 2 + [HBM] * 3,
            out_specs=HBM,
            scratch_shapes=[chunks_of(5), vmem(dp_count, share, joined), dma(5), dma(6)],
            compiler_params=params(24),
            cost_estimate=cost(2 * tokens * width * joined, 6 << 20),
        )(x, gain, *in_hbm(wq, wkv, wout))

    def first_sum(parts):
        return pl.pallas_call(
            first_sum_kernel,
            out_shape=shape_of((share, joined), BF),
            in_specs=[ANY],
            out_specs=VMEM,
            scratch_shapes=[vmem(dp_count, share, joined), dma(6)],
            compiler_params=params(24),
            cost_estimate=cost(parts.size, 2 << 20),
        )(parts)

    def summed_copies(adder, parts):
        cols = parts.shape[2]
        return pl.pallas_call(
            functools.partial(sum_kernel, adder),
            out_shape=pltpu.HBM((dp_count, share, cols), BF),
            in_specs=[ANY],
            out_specs=HBM,
            scratch_shapes=[vmem(dp_count, share, cols), vmem(share, cols), dma(6), dma(dp_count)],
            compiler_params=params(24),
            cost_estimate=cost(parts.size, 4 << 20),
        )(parts)

    def chosen_copies(first, second, cols):
        return pl.pallas_call(
            choose_kernel,
            out_shape=pltpu.HBM((dp_count, share, cols), BF),
            in_specs=[VMEM] * 2,
            out_specs=HBM,
            scratch_shapes=[dma(dp_count)],
            compiler_params=params(24),
            cost_estimate=cost(0, 2 << 20),
        )(first, second)

    def loaded(joins, firsts, seconds):
        count = 5 if joins else 4
        return pl.pallas_call(
            functools.partial(load_kernel, joins, len(firsts)),
            out_shape=pltpu.VMEM((count, width, width), BF),
            in_specs=[HBM] * (len(firsts) + len(seconds)),
            out_specs=VMEM,
            scratch_shapes=[dma(count)],
            compiler_params=params(16),
            cost_estimate=cost(0, 5 << 20),
        )(*in_hbm(*firsts, *seconds))

    def beside(array, distance):
        return lax.ppermute(array, "mp", [(i, i ^ distance) for i in range(mp_count)])

    def sum_over_mp(part, *later):
        mate = beside(part, 1)
        at = lax.axis_index("mp") % 2 * (tokens // 2)

        def half(array):
            return lax.dynamic_slice_in_dim(array, at, tokens // 2).astype(F32)

        pair_half = (half(part) + half(mate)).astype(BF)
        across = beside(pair_half, 2)
        pair_half, part, mate, *later = lax.optimization_barrier((pair_half, part, mate, *later))
        pair = (part.astype(F32) + mate.astype(F32)).astype(BF)
        return (pair, across, beside(across, 1)), later

    others = [beside(own_x, distance) for distance in (1, 2, 3)]
    first_chunks = pl.pallas_call(
        first_load_kernel,
        out_shape=pltpu.VMEM((5, width, width), BF),
        in_specs=[HBM] * 3,
        out_specs=VMEM,
        scratch_shapes=[dma(5)],
        compiler_params=params(16),
        cost_estimate=cost(0, 5 << 20),
    )(*in_hbm(wq, wkv, wout))
    own_parts, own_all = pl.pallas_call(
        first_own_kernel,
        out_shape=[pltpu.HBM((dp_count, share, joined), BF), shape_of((tokens, width), BF)],
        in_specs=[VMEM] * 6,
        out_specs=[HBM, VMEM],
        scratch_shapes=[
            pltpu.VMEM((tokens, width), F32),
            vmem(dp_count, share, joined),
            dma(6),
        ],
        compiler_params=params(24),
        cost_estimate=cost(2 * tokens * width * joined, 6 << 20),
    )(own_x, *others, gain, first_chunks)
    own_parts, received_x, gain_x, wq_s, wout_s = lax.optimization_barrier(
        (own_parts, received_x, gain_x, wq, wout)
    )
    own_parts = scatter(own_parts, "dp")
    wq_b = swap(wq_s, from_second)
    cuts = (5 * q_cols // 16, 5 * q_cols // 8)
    wout_a0 = swap(wout_s[: cuts[0]], from_first)
    wout_a1, wout_a2 = wout_s[cuts[0] : cuts[1]], wout_s[cuts[1] :]
    other_parts = other_rows_parts(gather(received_x, "mp"))
    own_parts, other_parts, wout_a0, wout_a1, wout_a2 = lax.optimization_barrier(
        (own_parts, other_parts, wout_a0, wout_a1, wout_a2)
    )
    wout_a1 = swap(wout_a1, from_first)
    own = first_sum(own_parts)
    mine_all = gather(other_x, "mp")
    other_parts, own, mine_all, wout_a1 = lax.optimization_barrier(
        (scatter(other_parts, "dp"), own, mine_all, wout_a1)
    )
    other = first_sum(other_parts)
    received = swap(other, from_first)
    received_grad, wkv_s = lax.optimization_barrier((swap(other, from_second), wkv))
    wkv_b = swap(wkv_s, from_second)
    copies, wout_a2 = lax.optimization_barrier((chosen_copies(own, received, joined), wout_a2))
    wout_a2 = swap(wout_a2, from_first)
    grad_copies = chosen_copies(received_grad, own, q_cols)
    qkv_first, grad_copies, wout_a2, wq_b, wq_s, wkv_s = lax.optimization_barrier(
        (spread(copies), grad_copies, wout_a2, wq_b, wq, wkv)
    )
    wout_a = (wout_a0, wout_a1, wout_a2)
    wq_a, wkv_a = swap(wq_s, from_first), swap(wkv_s, from_first)
    head_grad_last = spread(grad_copies)

    def layer_forward(qkv, wouts):
        out = pl.pallas_call(
            forward_kernel,
            out_shape=shape_of((tokens, width), BF),
            in_specs=[SMEM, ANY] + [HBM] * (1 + len(wouts[1])),
            out_specs=VMEM,
            scratch_shapes=[
                vmem(tokens, joined),
                chunks_of(4),
                pltpu.VMEM((tokens, tokens), F32),
                pltpu.VMEM((tokens, GROUP_HEADS * tokens), F32),
                vmem(tokens, GROUP_HEADS * tokens),
                vmem(tokens, q_cols),
                dma(4),
                dma(3),
            ],
            compiler_params=params(32),
            cost_estimate=cost(6 * tokens * tokens * q_cols, 4 << 20),
        )(seq_lengths, qkv, *in_hbm(wouts[0], *wouts[1]))
        return out

    def rows_after(resident, sums):
        even = lax.axis_index("mp") % 2 == 0
        lower, upper = jnp.where(even, *sums[1:]), jnp.where(even, *sums[:0:-1])
        added = sums[0].astype(F32) + jnp.concatenate([lower, upper], axis=0).astype(F32)
        return (resident.astype(F32) + added).astype(BF)

    out, wkv_b = lax.optimization_barrier((layer_forward(qkv_first, (wout, wout_a)), wkv_b))
    sums, pieces = sum_over_mp(out, wq_b, wkv_b, wq, wkv)
    joined_last = loaded(True, pieces[:2], pieces[2:])
    parts = pl.pallas_call(
        project_kernel,
        out_shape=pltpu.HBM((dp_count, share, joined), BF),
        in_specs=[VMEM] * 8,
        out_specs=HBM,
        scratch_shapes=[vmem(dp_count, share, joined), dma(6)],
        compiler_params=params(24),
        cost_estimate=cost(2 * tokens * width * joined, 6 << 20),
    )(own_all, mine_all, *sums, gain_x, gain, joined_last)
    parts, head_grad_last = lax.optimization_barrier((parts, head_grad_last))
    qkv_last = spread(summed_copies(scaled_sum, scatter(parts, "dp")))
    wout_b = swap(wout, from_second)
    wout_last = jnp.where(section == 0, wout_b, wout)
    h_one = rows_after(jnp.where(section == 0, own_all, mine_all), sums)
    rows_after(h_one, sum_over_mp(layer_forward(qkv_last, (wout_last, (wout_last,))))[0])

    def layer_backward(qkv, head_grads, wqs, wkvs, later=()):
        through = pl.pallas_call(
            backward_kernel,
            out_shape=shape_of((tokens, width), BF),
            in_specs=[SMEM, ANY, ANY] + [HBM] * 4,
            out_specs=VMEM,
            scratch_shapes=[
                vmem(tokens, joined),
                vmem(tokens, q_cols),
                chunks_of(5),
                pltpu.VMEM((tokens, tokens), F32),
                pltpu.VMEM((tokens, GROUP_HEADS * tokens), F32),
                pltpu.VMEM((tokens, GROUP_HEADS * tokens), F32),
                vmem(tokens, GROUP_HEADS * tokens),
                vmem(tokens, GROUP_HEADS * tokens),
                vmem(q_cols, tokens),
                vmem(tokens, 2 * kv_cols),
                dma(5),
                dma(5),
            ],
            compiler_params=params(32),
            cost_estimate=cost(12 * tokens * tokens * q_cols, 6 << 20),
        )(seq_lengths, qkv, head_grads, *in_hbm(*wqs, *wkvs))
        return sum_over_mp(through, *later)

    sums, pieces = layer_backward(
        qkv_last,
        *in_hbm(head_grad_last),
        (wq_b, wq),
        (wkv_b, wkv),
        later=(wout, *wout_a),
    )
    parts, grad_one = pl.pallas_call(
        head_grad_kernel,
        out_shape=[pltpu.HBM((dp_count, share, q_cols), BF), shape_of((tokens, width), BF)],
        in_specs=[VMEM] * 8,
        out_specs=[HBM, VMEM],
        scratch_shapes=[vmem(dp_count, share, q_cols), dma(4)],
        compiler_params=params(24),
        cost_estimate=cost(2 * tokens * width * q_cols, 4 << 20),
    )(mine_all, own_all, *sums, gain_x, gain, loaded(False, pieces[:1], pieces[1:]))
    parts, wq_a, wkv_a = lax.optimization_barrier((scatter(parts, "dp"), wq_a, wkv_a))
    head_grad_first = spread(summed_copies(plain_sum, parts))
    sums, _ = layer_backward(qkv_first, head_grad_first, (wq, wq_a), (wkv, wkv_a))

    hidden_cols = merger_weight.shape[0]
    outgoing, input_grad = pl.pallas_call(
        merger_kernel,
        out_shape=[
            shape_of((dp_count, 2, CAP * VB, hidden_cols), BF),
            shape_of((rows, width), BF),
        ],
        in_specs=[SMEM, SMEM] + [VMEM] * 7,
        out_specs=[VMEM] * 2,
        scratch_shapes=[
            pltpu.VMEM((tokens, width), F32),
            pltpu.VMEM((tokens, hidden_cols), F32),
            pltpu.SMEM((2 * dp_count,), jnp.int32),
            pltpu.SMEM((2 * dp_count * CAP,), jnp.int32),
        ],
        compiler_params=params(24),
    )(image_mask, block_owner, grad_one, *sums, gain, gain_x, merger_weight)
    kept, passed = pl.pallas_call(
        merger_sum_kernel,
        out_shape=[
            shape_of((CAP * VB, hidden_cols), F32),
            shape_of((CAP * VB, hidden_cols), BF),
        ],
        in_specs=[VMEM],
        out_specs=[VMEM] * 2,
        compiler_params=params(24),
    )(scatter(outgoing, "dp"))
    crossed = lax.ppermute(passed, "section", [(0, 1), (1, 0)]).astype(F32)
    first = jnp.where(section == 0, kept, crossed)
    second = jnp.where(section == 0, crossed, kept)
    hidden_grad = jnp.stack([first, second]).reshape(2, CAP, VB, hidden_cols)
    merger_grad = gelu_slope(merger_pre[0].astype(F32)) * hidden_grad
    return (input_grad[None], merger_grad[None])


def solution(mesh):
    placed = (
        P("section", "mp", "dp"),
        P("section", "mp", "dp"),
        P(None, "section", "dp"),
        P(None, "section", "dp", "mp"),
        P(None, "section", "dp", None, "mp"),
        P(None, "section", "mp", "dp"),
        P(),
        P("section", None),
        P("section", None),
        P("mp", "dp"),
        P(("section", "dp"), None, None, None, "mp"),
    )
    return jax.shard_map(
        local,
        mesh=mesh,
        in_specs=placed,
        out_specs=(P("section", "mp", "dp"), P(("section", "dp"), None, None, None, "mp")),
        check_vma=False,
    )
```

```python
import functools
import math

import jax
import jax.numpy as jnp
from jax import lax
from jax.experimental import pallas as pl
from jax.experimental.pallas import tpu as pltpu
from jax.sharding import PartitionSpec as P

MODEL_WIDTH = 8192
HEAD_SIZE = 128
GROUP_HEADS = 8
CAP = 2
VB = 8
NSEQ = 3

EPSILON = 1e-06
MASKED = -1e30
SOFT = 1.0 / math.sqrt(HEAD_SIZE)
LOG2E = math.log2(math.e)
QB = 128

BF = jnp.bfloat16
F32 = jnp.float32

VMEM = pl.BlockSpec(memory_space=pltpu.VMEM)
SMEM = pl.BlockSpec(memory_space=pltpu.SMEM)
ANY = pl.BlockSpec(memory_space=pl.ANY)
HBM = pl.BlockSpec(memory_space=pltpu.HBM)


def shape_of(shape, dtype):
    return jax.ShapeDtypeStruct(shape, dtype)


def in_hbm(*arrays):
    return [pltpu.with_memory_space_constraint(array, pltpu.HBM) for array in arrays]


def params(mebibytes):
    return pltpu.CompilerParams(vmem_limit_bytes=mebibytes << 20)


def cost(flops, bytes_accessed):
    return pl.CostEstimate(flops=flops, bytes_accessed=bytes_accessed, transcendentals=0)


def dot_nn(left, right):
    return jnp.dot(left, right, preferred_element_type=F32)


def dot_nt(left, right):
    return lax.dot_general(left, right, (((1,), (1,)), ((), ())), preferred_element_type=F32)


def two_lanes(column):
    high = column.astype(BF).astype(F32)
    lane = lax.broadcasted_iota(jnp.int32, (column.shape[0], 128), 1)
    return jnp.where(lane == 0, high, jnp.where(lane == 1, column - high, 0.0)).astype(BF)


def start_columns(sources, chunks, sems):
    width, index = chunks.shape[2], 0
    for source in sources:
        for start in range(0, source.shape[1], width):
            block = source.at[:, start : start + width]
            pltpu.make_async_copy(block, chunks.at[index], sems.at[index]).start()
            index += 1


def start_rows(sources, chunks, sems):
    rows, at = chunks.shape[1], 0
    for source in sources:
        start = 0
        while start < source.shape[0]:
            index, within = at // rows, at % rows
            count = min(rows - within, source.shape[0] - start)
            block = source.at[start : start + count, :]
            place = chunks.at[index, within : within + count, :]
            pltpu.make_async_copy(block, place, sems.at[index]).start()
            start, at = start + count, at + count


def start_joined(wqs, wkv_ref, chunks, sems):
    start_columns(wqs, chunks, sems)
    last = chunks.shape[0] - 1
    pltpu.make_async_copy(wkv_ref, chunks.at[last], sems.at[last]).start()


def landed(chunks, sems, index):
    pltpu.make_async_copy(chunks.at[index], chunks.at[index], sems.at[index]).wait()
    return chunks.at[index]


def by_section(first, second):
    section = lax.axis_index("section")
    pl.when(section == 0)(first)
    pl.when(section != 0)(second)


def spans(cols):
    return [slice(start, min(start + 512, cols)) for start in range(0, cols, 512)]


def start_spans(source, target, sems):
    for index, span in enumerate(spans(target.shape[-1])):
        at = (slice(None),) * (len(target.shape) - 1) + (span,)
        pltpu.make_async_copy(source.at[at], target.at[at], sems.at[index]).start()


def wait_span(target, sems, index):
    at = (slice(None),) * (len(target.shape) - 1) + (spans(target.shape[-1])[index],)
    pltpu.make_async_copy(target.at[at], target.at[at], sems.at[index]).wait()


def sender(staged, out_ref, sems):
    owners, share, cols = staged.shape

    def put(start, tile):
        span = slice(start, start + tile.shape[1])
        staged[:, :, span] = tile.reshape(owners, share, tile.shape[1])
        index = spans(cols).index(span)
        at = (slice(None), slice(None), span)
        pltpu.make_async_copy(staged.at[at], out_ref.at[at], sems.at[index]).start()

    def finish():
        for index in range(len(spans(cols))):
            wait_span(staged, sems, index)

    return put, finish


def repeat_out(tile, out_ref, sems):
    for place in range(out_ref.shape[0]):
        pltpu.make_async_copy(tile, out_ref.at[place], sems.at[place]).start()


def repeat_wait(tile, out_ref, sems):
    for place in range(out_ref.shape[0]):
        pltpu.make_async_copy(tile, out_ref.at[place], sems.at[place]).wait()


def project_rows(rows, gain, chunks, chunk_at, put):
    rows_f = rows.astype(F32)
    normed = (rows_f * gain).astype(BF)
    count, _, width = chunks.shape
    put(count * width, two_lanes(jnp.sum(rows_f * rows_f, axis=1, keepdims=True)))
    for index in range(count):
        put(index * width, dot_nn(normed, chunk_at(index)[...]).astype(BF))


def load_kernel(joined, pieces, *refs):
    *sources, out_ref, sems = refs

    def load(refs):
        if joined:
            start_joined(refs[:-1], refs[-1], out_ref, sems)
        else:
            start_rows(refs, out_ref, sems)

    by_section(lambda: load(sources[:pieces]), lambda: load(sources[pieces:]))
    for index in range(out_ref.shape[0]):
        landed(out_ref, sems, index)


def first_kernel(
    x_ref, gain_ref, wq_ref, wkv_ref, wout_ref, out_ref, chunks, staged, sems, out_sems
):
    put, finish = sender(staged, out_ref, out_sems)
    tokens = x_ref.shape[0]

    def rows():
        return jnp.concatenate([x_ref[tokens // 2 :, :], x_ref[: tokens // 2, :]], axis=0)

    def first():
        start_joined([wq_ref], wkv_ref, chunks, sems)
        project_rows(rows(), gain_ref[...], chunks, lambda at: landed(chunks, sems, at), put)

    def second():
        start_rows([wout_ref], chunks, sems)
        count, width, _ = chunks.shape
        put(count * width, jnp.zeros((tokens, 128), BF))
        put((count - 1) * width, jnp.zeros((tokens, width), BF))
        x = rows()
        for index in range(count - 1):
            put(index * width, dot_nt(x, landed(chunks, sems, index)[...]).astype(BF))

    by_section(first, second)
    finish()


def first_load_kernel(wq_ref, wkv_ref, wout_ref, out_ref, sems):
    def wait(count):
        for index in range(count):
            landed(out_ref, sems, index)

    def first():
        start_joined([wq_ref], wkv_ref, out_ref, sems)
        wait(out_ref.shape[0])

    def second():
        start_rows([wout_ref], out_ref, sems)
        wait(out_ref.shape[0] - 1)

    by_section(first, second)


def first_own_kernel(
    mine_ref, near_ref, far_ref, cross_ref, gain_ref, chunks, out_ref, x_ref, x, staged, out_sems
):
    rank = lax.axis_index("mp")
    share = mine_ref.shape[0]
    for distance, ref in enumerate((mine_ref, near_ref, far_ref, cross_ref)):
        at = pl.multiple_of(jnp.bitwise_xor(rank, distance) * share, share)
        x[pl.ds(at, share), :] = ref[...].astype(F32)
    x_ref[...] = x[...].astype(BF)
    put, finish = sender(staged, out_ref, out_sems)
    tokens = x_ref.shape[0]
    count, width, _ = chunks.shape

    def first():
        project_rows(x_ref[...], gain_ref[...], chunks, lambda at: chunks.at[at], put)

    def second():
        put(count * width, jnp.zeros((tokens, 128), BF))
        put((count - 1) * width, jnp.zeros((tokens, width), BF))
        for index in range(count - 1):
            put(index * width, dot_nt(x_ref[...], chunks[index]).astype(BF))

    by_section(first, second)
    finish()


def chosen(first_ref, second_ref):
    return jnp.where(lax.axis_index("section") == 0, first_ref[...], second_ref[...])


def summed(pair_ref, across_ref, beside_ref):
    even = lax.axis_index("mp") % 2 == 0
    lower = jnp.where(even, across_ref[...], beside_ref[...])
    upper = jnp.where(even, beside_ref[...], across_ref[...])
    return pair_ref[...].astype(F32) + jnp.concatenate([lower, upper], axis=0).astype(F32)


def project_kernel(
    r0_ref, r1_ref, pair_ref, across_ref, beside_ref, g0_ref, g1_ref, chunks, out_ref,
    staged, out_sems,
):
    added = summed(pair_ref, across_ref, beside_ref)
    rows = (chosen(r0_ref, r1_ref).astype(F32) + added).astype(BF)
    put, finish = sender(staged, out_ref, out_sems)
    project_rows(rows, chosen(g0_ref, g1_ref), chunks, lambda at: chunks.at[at], put)
    finish()


def head_grad_kernel(
    r0_ref, r1_ref, pair_ref, across_ref, beside_ref, g0_ref, g1_ref, chunks, out_ref, rows_ref,
    staged, out_sems,
):
    added = summed(pair_ref, across_ref, beside_ref)
    rows = chosen(r0_ref, r1_ref).astype(F32) + chosen(g0_ref, g1_ref) * added
    rows_ref[...] = rows.astype(BF)
    count, width, _ = chunks.shape
    put, finish = sender(staged, out_ref, out_sems)
    for index in range(count):
        put(index * width, dot_nt(rows_ref[...], chunks[index]).astype(BF))
    finish()


def add_parts(load, count):
    total = load(0).astype(F32)
    for index in range(1, count):
        total = total + load(index).astype(F32)
    return total


def part_sums(parts, sems):
    def total(index):
        wait_span(parts, sems, index)
        span = spans(parts.shape[2])[index]
        return add_parts(lambda source: parts[source, :, span], parts.shape[0])

    return total


def scaled_sum(total, tile):
    ranges = spans(tile.shape[1])
    squares = jnp.sum(total(len(ranges) - 1), axis=1, keepdims=True)
    scale = lax.rsqrt(squares / MODEL_WIDTH + EPSILON)
    for index, span in enumerate(ranges[:-1]):
        tile[:, span] = (total(index) * scale).astype(BF)
    tile[:, ranges[-1]] = two_lanes(scale)


def plain_sum(total, tile):
    for index, span in enumerate(spans(tile.shape[1])):
        tile[:, span] = total(index).astype(BF)


def first_sum_kernel(parts_ref, out_ref, parts, sems):
    start_spans(parts_ref, parts, sems)
    total = part_sums(parts, sems)
    by_section(lambda: scaled_sum(total, out_ref), lambda: plain_sum(total, out_ref))


def sum_kernel(adder, parts_ref, out_ref, parts, tile, sems, out_sems):
    start_spans(parts_ref, parts, sems)
    adder(part_sums(parts, sems), tile)
    repeat_out(tile, out_ref, out_sems)
    repeat_wait(tile, out_ref, out_sems)


def choose_kernel(first_ref, second_ref, out_ref, sems):
    first = first_ref.at[:, : out_ref.shape[2]]
    second = second_ref.at[:, : out_ref.shape[2]]
    by_section(
        lambda: repeat_out(first, out_ref, sems), lambda: repeat_out(second, out_ref, sems)
    )
    repeat_wait(first, out_ref, sems)


def fill_bias(seq_ref, bias):
    section = lax.axis_index("section")
    tokens = bias.shape[0]
    keys = lax.broadcasted_iota(jnp.int32, (tokens, tokens), 0)
    queries = lax.broadcasted_iota(jnp.int32, (tokens, tokens), 1)
    key_segment = jnp.zeros((tokens, tokens), jnp.int32)
    query_segment = jnp.zeros((tokens, tokens), jnp.int32)
    bound = 0
    for index in range(NSEQ):
        bound = bound + seq_ref[section, index]
        key_segment = key_segment + (keys >= bound).astype(jnp.int32)
        query_segment = query_segment + (queries >= bound).astype(jnp.int32)
    allowed = (keys <= queries) & (key_segment == query_segment)
    bias[...] = jnp.where(allowed, 0.0, MASKED)


def head_columns(head):
    return slice(head * HEAD_SIZE, (head + 1) * HEAD_SIZE)


def softmax_blocks(tokens, body):
    def one_head(head, carry):
        for at in range(0, tokens, QB):
            lanes = pl.ds(pl.multiple_of(head * tokens + at, QB), QB)
            body(slice(at, at + QB), lanes, at + QB)
        return carry

    lax.fori_loop(0, GROUP_HEADS, one_head, 0, unroll=4)


def clear_unreached(target, tokens):
    for head in range(GROUP_HEADS):
        for at in range(0, tokens - QB, QB):
            lanes = slice(head * tokens + at, head * tokens + at + QB)
            target[at + QB :, lanes] = jnp.zeros((tokens - at - QB, QB), target.dtype)


def weights_of(scores, bias):
    scores = scores * (SOFT * LOG2E) + bias
    raised = jnp.exp2(scores - jnp.max(scores, axis=0, keepdims=True))
    return raised * (1.0 / jnp.sum(raised, axis=0, keepdims=True))


def start_qkv(qkv_ref, qkv, q_cols, sems):
    pltpu.make_async_copy(qkv_ref.at[:, q_cols:], qkv.at[:, q_cols:], sems.at[0]).start()
    for group in range(q_cols // (GROUP_HEADS * HEAD_SIZE)):
        start_group(qkv_ref, qkv, sems, 1, group)


def start_group(source, target, sems, first, group):
    width = GROUP_HEADS * HEAD_SIZE
    at = (slice(None), slice(group * width, (group + 1) * width))
    pltpu.make_async_copy(source.at[at], target.at[at], sems.at[first + group]).start()


def wait_group(target, sems, first, group):
    width = GROUP_HEADS * HEAD_SIZE
    at = (slice(None), slice(group * width, (group + 1) * width))
    pltpu.make_async_copy(target.at[at], target.at[at], sems.at[first + group]).wait()


def forward_kernel(seq_ref, qkv_ref, wout0_ref, *refs):
    *wout1_refs, out_ref, qkv, chunks, bias, scores, weights, attended, sems, in_sems = refs
    tokens, q_cols = attended.shape
    start_qkv(qkv_ref, qkv, q_cols, in_sems)
    by_section(
        lambda: start_rows([wout0_ref], chunks, sems),
        lambda: start_rows(wout1_refs, chunks, sems),
    )
    fill_bias(seq_ref, bias)
    clear_unreached(weights, tokens)
    groups = q_cols // (GROUP_HEADS * HEAD_SIZE)
    pltpu.make_async_copy(qkv.at[:, q_cols:], qkv.at[:, q_cols:], in_sems.at[0]).wait()
    for group in range(groups):
        at = q_cols + group * HEAD_SIZE
        keys = qkv[:, at : at + HEAD_SIZE]
        at = at + groups * HEAD_SIZE
        values_t = qkv[:, at : at + HEAD_SIZE].astype(F32).T.astype(BF)
        wait_group(qkv, in_sems, 1, group)
        for index in range(GROUP_HEADS):
            columns = head_columns(group * GROUP_HEADS + index)
            scores[:, index * tokens : (index + 1) * tokens] = dot_nt(keys, qkv[:, columns])

        def block(queries, lanes, reach):
            weights[:reach, lanes] = weights_of(
                scores[:reach, lanes], bias[:reach, queries]
            ).astype(BF)

        softmax_blocks(tokens, block)
        for index in range(GROUP_HEADS):
            columns = head_columns(group * GROUP_HEADS + index)
            mixed = dot_nn(values_t, weights[:, index * tokens : (index + 1) * tokens])
            attended[:, columns] = mixed.T.astype(BF)
    count, width, _ = chunks.shape
    out = dot_nn(attended[:, :width], landed(chunks, sems, 0)[...])
    for index in range(1, count):
        columns = slice(index * width, (index + 1) * width)
        out = out + dot_nn(attended[:, columns], landed(chunks, sems, index)[...])
    out_ref[...] = out.astype(BF)


def backward_kernel(pieces, seq_ref, qkv_ref, grads_ref, *refs):
    wq0_refs, (wq1_ref, wkv0_ref, wkv1_ref, out_ref, *refs) = refs[:pieces], refs[pieces:]
    (
        qkv, grads, chunks, bias, scores, weight_grads, weights, score_grads, scaled_q, scaled_kv,
        sems, in_sems,
    ) = refs
    tokens, q_cols = grads.shape
    groups = q_cols // (GROUP_HEADS * HEAD_SIZE)
    pltpu.make_async_copy(qkv_ref.at[:, q_cols:], qkv.at[:, q_cols:], in_sems.at[0]).start()
    start_group(qkv_ref, qkv, in_sems, 1, 0)
    start_group(grads_ref, grads, in_sems, 1 + groups, 0)
    fill_bias(seq_ref, bias)
    clear_unreached(weights, tokens)
    clear_unreached(score_grads, tokens)
    kv_cols = groups * HEAD_SIZE
    pltpu.make_async_copy(qkv.at[:, q_cols:], qkv.at[:, q_cols:], in_sems.at[0]).wait()
    wait_group(qkv, in_sems, 1, 0)
    wait_group(grads, in_sems, 1 + groups, 0)
    for group in range(1, groups):
        start_group(qkv_ref, qkv, in_sems, 1, group)
        start_group(grads_ref, grads, in_sems, 1 + groups, group)
    by_section(
        lambda: start_joined(wq0_refs, wkv0_ref, chunks, sems),
        lambda: start_joined([wq1_ref], wkv1_ref, chunks, sems),
    )
    scale_lanes = qkv[:, q_cols + 2 * kv_cols :].astype(F32)
    scale_column = jnp.sum(scale_lanes, axis=1, keepdims=True)
    scale_row = jnp.sum(scale_lanes.T, axis=0, keepdims=True) * SOFT
    for group in range(groups):
        at = q_cols + group * HEAD_SIZE
        keys = qkv[:, at : at + HEAD_SIZE]
        keys_t = keys.astype(F32).T.astype(BF)
        at = at + kv_cols
        values = qkv[:, at : at + HEAD_SIZE]
        if group > 0:
            wait_group(qkv, in_sems, 1, group)
            wait_group(grads, in_sems, 1 + groups, group)
        for index in range(GROUP_HEADS):
            columns = head_columns(group * GROUP_HEADS + index)
            lanes = slice(index * tokens, (index + 1) * tokens)
            scores[:, lanes] = dot_nt(keys, qkv[:, columns])
            weight_grads[:, lanes] = dot_nt(values, grads[:, columns])
        def block(queries, lanes, reach):
            weight = weights_of(scores[:reach, lanes], bias[:reach, queries])
            weights[:reach, lanes] = weight.astype(BF)
            weight_grad = weight_grads[:reach, lanes]
            mean = jnp.sum(weight_grad * weight, axis=0, keepdims=True)
            score_grads[:reach, lanes] = (weight * (weight_grad - mean)).astype(BF)

        softmax_blocks(tokens, block)
        key_grad = jnp.zeros((tokens, HEAD_SIZE), F32)
        value_grad = jnp.zeros((tokens, HEAD_SIZE), F32)
        for index in range(GROUP_HEADS):
            columns = head_columns(group * GROUP_HEADS + index)
            lanes = slice(index * tokens, (index + 1) * tokens)
            score_grad = score_grads[:, lanes]
            scaled_q[columns, :] = (dot_nn(keys_t, score_grad) * scale_row).astype(BF)
            key_grad = key_grad + dot_nn(score_grad, qkv[:, columns])
            value_grad = value_grad + dot_nn(weights[:, lanes], grads[:, columns])
        at = group * HEAD_SIZE
        scaled_kv[:, at : at + HEAD_SIZE] = (key_grad * (scale_column * SOFT)).astype(BF)
        at = at + kv_cols
        scaled_kv[:, at : at + HEAD_SIZE] = (value_grad * scale_column).astype(BF)
    count, width, _ = chunks.shape
    through = dot_nt(landed(chunks, sems, count - 1)[...], scaled_kv[...])
    for index in range(count - 1):
        rows = slice(index * width, (index + 1) * width)
        through = through + dot_nn(landed(chunks, sems, index)[...], scaled_q[rows, :])
    out_ref[...] = through.T.astype(BF)


def merger_kernel(
    marks_ref, owners_ref, last_ref, pair_ref, across_ref, beside_ref, g0_ref, g1_ref, weight_ref,
    out_ref, grad_ref, rows, hidden, counts, places,
):
    added = summed(pair_ref, across_ref, beside_ref)
    rows[...] = last_ref[...].astype(F32) + chosen(g0_ref, g1_ref) * added
    share = grad_ref.shape[0]
    at = pl.multiple_of(lax.axis_index("mp") * share, share)
    grad_ref[...] = rows[pl.ds(at, share), :].astype(BF)
    x = rows[...].astype(BF)
    cols = weight_ref.shape[0]
    for start in range(0, cols, 256):
        hidden[:, start : start + 256] = dot_nt(x, weight_ref[start : start + 256, :])
    dp_count, sections = out_ref.shape[:2]
    owner_count = dp_count * sections

    def clear(owner, carry):
        counts[owner] = 0
        for slot in range(CAP):
            places[owner * CAP + slot] = -1
        return carry

    lax.fori_loop(0, owner_count, clear, 0)

    def place(block, carry):
        owner = owners_ref[0, block]

        @pl.when(marks_ref[0, block] == 1)
        def _():
            slot = counts[owner]
            places[owner * CAP + slot] = block
            counts[owner] = slot + 1

        return carry

    lax.fori_loop(0, marks_ref.shape[1], place, 0)

    def send(owner, carry):
        pieces = []
        for slot in range(CAP):
            block = places[owner * CAP + slot]
            at = pl.multiple_of(jnp.maximum(block, 0) * VB, VB)
            pieces.append(jnp.where(block >= 0, hidden[pl.ds(at, VB), :], 0.0))
        out_ref[lax.rem(owner, dp_count), lax.div(owner, dp_count)] = jnp.concatenate(
            pieces, axis=0
        ).astype(BF)
        return carry

    lax.fori_loop(0, owner_count, send, 0)


def merger_sum_kernel(parts_ref, own_ref, other_ref):
    section = lax.axis_index("section")
    sources = parts_ref.shape[0]

    def total(index):
        return add_parts(lambda source: parts_ref[source, index], sources)

    first, second = total(0), total(1)
    own_ref[...] = jnp.where(section == 0, first, second)
    other_ref[...] = jnp.where(section == 0, second, first).astype(BF)


def gelu_slope(values):
    cumulative = 0.5 * (1.0 + lax.erf(values * (1.0 / math.sqrt(2.0))))
    return cumulative + values * jnp.exp(-0.5 * values * values) * (1.0 / math.sqrt(2.0 * math.pi))


def local(
    embeds,
    cotangent,
    norm_gain,
    w_query,
    w_keyval,
    w_out,
    seq_lengths,
    image_mask,
    block_owner,
    merger_weight,
    merger_pre,
):
    section = lax.axis_index("section")
    mp_count = lax.axis_size("mp")
    dp_count = lax.axis_size("dp")
    rows, width = embeds.shape[1:]
    tokens = rows * mp_count
    share = tokens // dp_count
    q_cols = w_query.shape[3]
    kv_cols = w_keyval.shape[4]
    joined = q_cols + 2 * kv_cols + 128
    emb, cot = embeds[0], cotangent[0]
    wq, wout = w_query[0, 0], w_out[0, 0]
    wkv = w_keyval[0, 0].reshape(width, 2 * kv_cols)
    gain = norm_gain[0]

    def partner(index):
        other, rank = 1 - index // mp_count, (index % mp_count + mp_count // 2) % mp_count
        return other * mp_count + rank

    everyone = range(2 * mp_count)
    from_first = [(i, partner(i)) for i in everyone if i < mp_count]
    from_second = [(i, partner(i)) for i in everyone if i >= mp_count]

    def swap(array, pairs):
        return lax.ppermute(array, ("section", "mp"), pairs)

    def scatter(array, axis):
        return lax.all_to_all(array, axis, split_axis=0, concat_axis=0, tiled=True)

    def spread(copies):
        return scatter(copies, "dp").reshape(tokens, copies.shape[2])

    def gather(array, axis):
        return lax.all_gather(array, axis, axis=0, tiled=True)

    def chunks_of(count):
        return pltpu.VMEM((count, width, width), BF)

    own_x, other_x = jnp.where(section == 0, emb, cot), jnp.where(section == 0, cot, emb)
    received_x = swap(other_x, from_first + from_second)
    gain_x = swap(gain, from_first + from_second)
    def vmem(*shape):
        return pltpu.VMEM(shape, BF)

    def dma(count):
        return pltpu.SemaphoreType.DMA((count,))

    def other_rows_parts(x):
        return pl.pallas_call(
            first_kernel,
            out_shape=pltpu.HBM((dp_count, share, joined), BF),
            in_specs=[VMEM] * 2 + [HBM] * 3,
            out_specs=HBM,
            scratch_shapes=[chunks_of(5), vmem(dp_count, share, joined), dma(5), dma(6)],
            compiler_params=params(24),
            cost_estimate=cost(2 * tokens * width * joined, 6 << 20),
        )(x, gain, *in_hbm(wq, wkv, wout))

    def first_sum(parts):
        return pl.pallas_call(
            first_sum_kernel,
            out_shape=shape_of((share, joined), BF),
            in_specs=[ANY],
            out_specs=VMEM,
            scratch_shapes=[vmem(dp_count, share, joined), dma(6)],
            compiler_params=params(24),
            cost_estimate=cost(parts.size, 2 << 20),
        )(parts)

    def summed_copies(adder, parts):
        cols = parts.shape[2]
        return pl.pallas_call(
            functools.partial(sum_kernel, adder),
            out_shape=pltpu.HBM((dp_count, share, cols), BF),
            in_specs=[ANY],
            out_specs=HBM,
            scratch_shapes=[vmem(dp_count, share, cols), vmem(share, cols), dma(6), dma(dp_count)],
            compiler_params=params(24),
            cost_estimate=cost(parts.size, 4 << 20),
        )(parts)

    def chosen_copies(first, second, cols):
        return pl.pallas_call(
            choose_kernel,
            out_shape=pltpu.HBM((dp_count, share, cols), BF),
            in_specs=[VMEM] * 2,
            out_specs=HBM,
            scratch_shapes=[dma(dp_count)],
            compiler_params=params(24),
            cost_estimate=cost(0, 2 << 20),
        )(first, second)

    def loaded(joins, firsts, seconds):
        count = 5 if joins else 4
        return pl.pallas_call(
            functools.partial(load_kernel, joins, len(firsts)),
            out_shape=pltpu.VMEM((count, width, width), BF),
            in_specs=[HBM] * (len(firsts) + len(seconds)),
            out_specs=VMEM,
            scratch_shapes=[dma(count)],
            compiler_params=params(16),
            cost_estimate=cost(0, 5 << 20),
        )(*in_hbm(*firsts, *seconds))

    def beside(array, distance):
        return lax.ppermute(array, "mp", [(i, i ^ distance) for i in range(mp_count)])

    def sum_over_mp(part, *later):
        mate = beside(part, 1)
        at = lax.axis_index("mp") % 2 * (tokens // 2)

        def half(array):
            return lax.dynamic_slice_in_dim(array, at, tokens // 2).astype(F32)

        pair_half = (half(part) + half(mate)).astype(BF)
        across = beside(pair_half, 2)
        pair_half, part, mate, *later = lax.optimization_barrier((pair_half, part, mate, *later))
        pair = (part.astype(F32) + mate.astype(F32)).astype(BF)
        return (pair, across, beside(across, 1)), later

    others = [beside(own_x, distance) for distance in (1, 2, 3)]
    first_chunks = pl.pallas_call(
        first_load_kernel,
        out_shape=pltpu.VMEM((5, width, width), BF),
        in_specs=[HBM] * 3,
        out_specs=VMEM,
        scratch_shapes=[dma(5)],
        compiler_params=params(16),
        cost_estimate=cost(0, 5 << 20),
    )(*in_hbm(wq, wkv, wout))
    own_parts, own_all = pl.pallas_call(
        first_own_kernel,
        out_shape=[pltpu.HBM((dp_count, share, joined), BF), shape_of((tokens, width), BF)],
        in_specs=[VMEM] * 6,
        out_specs=[HBM, VMEM],
        scratch_shapes=[
            pltpu.VMEM((tokens, width), F32),
            vmem(dp_count, share, joined),
            dma(6),
        ],
        compiler_params=params(24),
        cost_estimate=cost(2 * tokens * width * joined, 6 << 20),
    )(own_x, *others, gain, first_chunks)
    own_parts, received_x, gain_x, wq_s, wout_s = lax.optimization_barrier(
        (own_parts, received_x, gain_x, wq, wout)
    )
    own_parts = scatter(own_parts, "dp")
    quarter, cuts = q_cols // 4, (5 * q_cols // 16, 5 * q_cols // 8)
    wq_b0 = swap(wq_s[:, :quarter], from_second)
    wout_a0 = swap(wout_s[: cuts[0]], from_first)
    other_parts = other_rows_parts(gather(received_x, "mp"))
    own_parts, other_parts, wout_a0, wq_b0, wout_s, wq_s = lax.optimization_barrier(
        (own_parts, other_parts, wout_a0, wq_b0, wout, wq)
    )
    wout_a1 = swap(wout_s[cuts[0] : cuts[1]], from_first)
    wq_b1 = swap(wq_s[:, quarter:], from_second)
    wout_a2 = wout_s[cuts[1] :]
    own = first_sum(own_parts)
    other_parts, own, other_x, wout_a2 = lax.optimization_barrier(
        (scatter(other_parts, "dp"), own, other_x, wout_a2)
    )
    other = first_sum(other_parts)
    received = swap(other, from_first)
    received_grad, wkv_s = lax.optimization_barrier((swap(other, from_second), wkv))
    wkv_b = swap(wkv_s, from_second)
    copies, wout_a1, wout_a2 = lax.optimization_barrier(
        (chosen_copies(own, received, joined), wout_a1, wout_a2)
    )
    wout_a2 = swap(wout_a2, from_first)
    mine_all = gather(other_x, "mp")
    grad_copies = chosen_copies(received_grad, own, q_cols)
    qkv_first, grad_copies, mine_all, wq_b1, wq_s, wkv_s = lax.optimization_barrier(
        (spread(copies), grad_copies, mine_all, wq_b1, wq, wkv)
    )
    wout_a = (wout_a0, wout_a1, wout_a2)
    wq_a, wkv_a = swap(wq_s, from_first), swap(wkv_s, from_first)
    head_grad_last = spread(grad_copies)

    def layer_forward(qkv, wouts):
        out = pl.pallas_call(
            forward_kernel,
            out_shape=shape_of((tokens, width), BF),
            in_specs=[SMEM, ANY] + [HBM] * (1 + len(wouts[1])),
            out_specs=VMEM,
            scratch_shapes=[
                vmem(tokens, joined),
                chunks_of(4),
                pltpu.VMEM((tokens, tokens), F32),
                pltpu.VMEM((tokens, GROUP_HEADS * tokens), F32),
                vmem(tokens, GROUP_HEADS * tokens),
                vmem(tokens, q_cols),
                dma(4),
                dma(3),
            ],
            compiler_params=params(32),
            cost_estimate=cost(6 * tokens * tokens * q_cols, 4 << 20),
        )(seq_lengths, qkv, *in_hbm(wouts[0], *wouts[1]))
        return out

    def rows_after(resident, sums):
        even = lax.axis_index("mp") % 2 == 0
        lower, upper = jnp.where(even, *sums[1:]), jnp.where(even, *sums[:0:-1])
        added = sums[0].astype(F32) + jnp.concatenate([lower, upper], axis=0).astype(F32)
        return (resident.astype(F32) + added).astype(BF)

    out, wkv_b = lax.optimization_barrier((layer_forward(qkv_first, (wout, wout_a)), wkv_b))
    sums, pieces = sum_over_mp(out, wq_b0, wq_b1, wkv_b, wq, wkv)
    joined_last = loaded(True, pieces[:3], pieces[3:])
    parts = pl.pallas_call(
        project_kernel,
        out_shape=pltpu.HBM((dp_count, share, joined), BF),
        in_specs=[VMEM] * 8,
        out_specs=HBM,
        scratch_shapes=[vmem(dp_count, share, joined), dma(6)],
        compiler_params=params(24),
        cost_estimate=cost(2 * tokens * width * joined, 6 << 20),
    )(own_all, mine_all, *sums, gain_x, gain, joined_last)
    parts, head_grad_last = lax.optimization_barrier((parts, head_grad_last))
    qkv_last = spread(summed_copies(scaled_sum, scatter(parts, "dp")))
    wout_b = swap(wout, from_second)
    wout_last = jnp.where(section == 0, wout_b, wout)
    h_one = rows_after(jnp.where(section == 0, own_all, mine_all), sums)
    rows_after(h_one, sum_over_mp(layer_forward(qkv_last, (wout_last, (wout_last,))))[0])

    def layer_backward(qkv, head_grads, wqs, wkvs, later=()):
        through = pl.pallas_call(
            functools.partial(backward_kernel, len(wqs[0])),
            out_shape=shape_of((tokens, width), BF),
            in_specs=[SMEM, ANY, ANY] + [HBM] * (3 + len(wqs[0])),
            out_specs=VMEM,
            scratch_shapes=[
                vmem(tokens, joined),
                vmem(tokens, q_cols),
                chunks_of(5),
                pltpu.VMEM((tokens, tokens), F32),
                pltpu.VMEM((tokens, GROUP_HEADS * tokens), F32),
                pltpu.VMEM((tokens, GROUP_HEADS * tokens), F32),
                vmem(tokens, GROUP_HEADS * tokens),
                vmem(tokens, GROUP_HEADS * tokens),
                vmem(q_cols, tokens),
                vmem(tokens, 2 * kv_cols),
                dma(5),
                dma(5),
            ],
            compiler_params=params(32),
            cost_estimate=cost(12 * tokens * tokens * q_cols, 6 << 20),
        )(seq_lengths, qkv, head_grads, *in_hbm(*wqs[0], *wqs[1], *wkvs))
        return sum_over_mp(through, *later)

    sums, pieces = layer_backward(
        qkv_last,
        *in_hbm(head_grad_last),
        ((wq_b0, wq_b1), (wq,)),
        (wkv_b, wkv),
        later=(wout, *wout_a),
    )
    parts, grad_one = pl.pallas_call(
        head_grad_kernel,
        out_shape=[pltpu.HBM((dp_count, share, q_cols), BF), shape_of((tokens, width), BF)],
        in_specs=[VMEM] * 8,
        out_specs=[HBM, VMEM],
        scratch_shapes=[vmem(dp_count, share, q_cols), dma(4)],
        compiler_params=params(24),
        cost_estimate=cost(2 * tokens * width * q_cols, 4 << 20),
    )(mine_all, own_all, *sums, gain_x, gain, loaded(False, pieces[:1], pieces[1:]))
    parts, wq_a, wkv_a = lax.optimization_barrier((scatter(parts, "dp"), wq_a, wkv_a))
    head_grad_first = spread(summed_copies(plain_sum, parts))
    sums, _ = layer_backward(qkv_first, head_grad_first, ((wq,), (wq_a,)), (wkv, wkv_a))

    hidden_cols = merger_weight.shape[0]
    outgoing, input_grad = pl.pallas_call(
        merger_kernel,
        out_shape=[
            shape_of((dp_count, 2, CAP * VB, hidden_cols), BF),
            shape_of((rows, width), BF),
        ],
        in_specs=[SMEM, SMEM] + [VMEM] * 7,
        out_specs=[VMEM] * 2,
        scratch_shapes=[
            pltpu.VMEM((tokens, width), F32),
            pltpu.VMEM((tokens, hidden_cols), F32),
            pltpu.SMEM((2 * dp_count,), jnp.int32),
            pltpu.SMEM((2 * dp_count * CAP,), jnp.int32),
        ],
        compiler_params=params(24),
    )(image_mask, block_owner, grad_one, *sums, gain, gain_x, merger_weight)
    kept, passed = pl.pallas_call(
        merger_sum_kernel,
        out_shape=[
            shape_of((CAP * VB, hidden_cols), F32),
            shape_of((CAP * VB, hidden_cols), BF),
        ],
        in_specs=[VMEM],
        out_specs=[VMEM] * 2,
        compiler_params=params(24),
    )(scatter(outgoing, "dp"))
    crossed = lax.ppermute(passed, "section", [(0, 1), (1, 0)]).astype(F32)
    first = jnp.where(section == 0, kept, crossed)
    second = jnp.where(section == 0, crossed, kept)
    hidden_grad = jnp.stack([first, second]).reshape(2, CAP, VB, hidden_cols)
    merger_grad = gelu_slope(merger_pre[0].astype(F32)) * hidden_grad
    return (input_grad[None], merger_grad[None])


def solution(mesh):
    placed = (
        P("section", "mp", "dp"),
        P("section", "mp", "dp"),
        P(None, "section", "dp"),
        P(None, "section", "dp", "mp"),
        P(None, "section", "dp", None, "mp"),
        P(None, "section", "mp", "dp"),
        P(),
        P("section", None),
        P("section", None),
        P("mp", "dp"),
        P(("section", "dp"), None, None, None, "mp"),
    )
    return jax.shard_map(
        local,
        mesh=mesh,
        in_specs=placed,
        out_specs=(P("section", "mp", "dp"), P(("section", "dp"), None, None, None, "mp")),
        check_vma=False,
    )
```

```python
import functools
import math

import jax
import jax.numpy as jnp
from jax import lax
from jax.experimental import pallas as pl
from jax.experimental.pallas import tpu as pltpu
from jax.sharding import PartitionSpec as P

MODEL_WIDTH = 8192
HEAD_SIZE = 128
GROUP_HEADS = 8
CAP = 2
VB = 8
NSEQ = 3

EPSILON = 1e-06
MASKED = -1e30
SOFT = 1.0 / math.sqrt(HEAD_SIZE)
LOG2E = math.log2(math.e)
QB = 128

BF = jnp.bfloat16
F32 = jnp.float32

VMEM = pl.BlockSpec(memory_space=pltpu.VMEM)
SMEM = pl.BlockSpec(memory_space=pltpu.SMEM)
ANY = pl.BlockSpec(memory_space=pl.ANY)
HBM = pl.BlockSpec(memory_space=pltpu.HBM)


def shape_of(shape, dtype):
    return jax.ShapeDtypeStruct(shape, dtype)


def in_hbm(*arrays):
    return [pltpu.with_memory_space_constraint(array, pltpu.HBM) for array in arrays]


def params(mebibytes):
    return pltpu.CompilerParams(vmem_limit_bytes=mebibytes << 20)


def cost(flops, bytes_accessed):
    return pl.CostEstimate(flops=flops, bytes_accessed=bytes_accessed, transcendentals=0)


def dot_nn(left, right):
    return jnp.dot(left, right, preferred_element_type=F32)


def dot_nt(left, right):
    return lax.dot_general(left, right, (((1,), (1,)), ((), ())), preferred_element_type=F32)


def two_lanes(column):
    high = column.astype(BF).astype(F32)
    lane = lax.broadcasted_iota(jnp.int32, (column.shape[0], 128), 1)
    return jnp.where(lane == 0, high, jnp.where(lane == 1, column - high, 0.0)).astype(BF)


def start_columns(sources, chunks, sems):
    width, index = chunks.shape[2], 0
    for source in sources:
        for start in range(0, source.shape[1], width):
            block = source.at[:, start : start + width]
            pltpu.make_async_copy(block, chunks.at[index], sems.at[index]).start()
            index += 1


def start_rows(sources, chunks, sems):
    rows, at = chunks.shape[1], 0
    for source in sources:
        start = 0
        while start < source.shape[0]:
            index, within = at // rows, at % rows
            count = min(rows - within, source.shape[0] - start)
            block = source.at[start : start + count, :]
            place = chunks.at[index, within : within + count, :]
            pltpu.make_async_copy(block, place, sems.at[index]).start()
            start, at = start + count, at + count


def start_joined(wqs, wkv_ref, chunks, sems):
    start_columns(wqs, chunks, sems)
    last = chunks.shape[0] - 1
    pltpu.make_async_copy(wkv_ref, chunks.at[last], sems.at[last]).start()


def landed(chunks, sems, index):
    pltpu.make_async_copy(chunks.at[index], chunks.at[index], sems.at[index]).wait()
    return chunks.at[index]


def by_section(first, second):
    section = lax.axis_index("section")
    pl.when(section == 0)(first)
    pl.when(section != 0)(second)


def spans(cols):
    return [slice(start, min(start + 512, cols)) for start in range(0, cols, 512)]


def start_spans(source, target, sems):
    for index, span in enumerate(spans(target.shape[-1])):
        at = (slice(None),) * (len(target.shape) - 1) + (span,)
        pltpu.make_async_copy(source.at[at], target.at[at], sems.at[index]).start()


def wait_span(target, sems, index):
    at = (slice(None),) * (len(target.shape) - 1) + (spans(target.shape[-1])[index],)
    pltpu.make_async_copy(target.at[at], target.at[at], sems.at[index]).wait()


def sender(staged, out_ref, sems):
    owners, share, cols = staged.shape

    def put(start, tile):
        span = slice(start, start + tile.shape[1])
        staged[:, :, span] = tile.reshape(owners, share, tile.shape[1])
        index = spans(cols).index(span)
        at = (slice(None), slice(None), span)
        pltpu.make_async_copy(staged.at[at], out_ref.at[at], sems.at[index]).start()

    def finish():
        for index in range(len(spans(cols))):
            wait_span(staged, sems, index)

    return put, finish


def repeat_out(tile, out_ref, sems):
    for place in range(out_ref.shape[0]):
        pltpu.make_async_copy(tile, out_ref.at[place], sems.at[place]).start()


def repeat_wait(tile, out_ref, sems):
    for place in range(out_ref.shape[0]):
        pltpu.make_async_copy(tile, out_ref.at[place], sems.at[place]).wait()


def project_rows(rows, gain, chunks, chunk_at, put):
    rows_f = rows.astype(F32)
    normed = (rows_f * gain).astype(BF)
    count, _, width = chunks.shape
    put(count * width, two_lanes(jnp.sum(rows_f * rows_f, axis=1, keepdims=True)))
    for index in range(count):
        put(index * width, dot_nn(normed, chunk_at(index)[...]).astype(BF))


def load_kernel(joined, pieces, *refs):
    *sources, out_ref, sems = refs

    def load(refs):
        if joined:
            start_joined(refs[:-1], refs[-1], out_ref, sems)
        else:
            start_rows(refs, out_ref, sems)

    by_section(lambda: load(sources[:pieces]), lambda: load(sources[pieces:]))
    for index in range(out_ref.shape[0]):
        landed(out_ref, sems, index)


def first_kernel(
    x_ref, gain_ref, wq_ref, wkv_ref, wout_ref, out_ref, chunks, staged, sems, out_sems
):
    put, finish = sender(staged, out_ref, out_sems)
    tokens = x_ref.shape[0]

    def rows():
        return jnp.concatenate([x_ref[tokens // 2 :, :], x_ref[: tokens // 2, :]], axis=0)

    def first():
        start_joined([wq_ref], wkv_ref, chunks, sems)
        project_rows(rows(), gain_ref[...], chunks, lambda at: landed(chunks, sems, at), put)

    def second():
        start_rows([wout_ref], chunks, sems)
        count, width, _ = chunks.shape
        put(count * width, jnp.zeros((tokens, 128), BF))
        put((count - 1) * width, jnp.zeros((tokens, width), BF))
        x = rows()
        for index in range(count - 1):
            put(index * width, dot_nt(x, landed(chunks, sems, index)[...]).astype(BF))

    by_section(first, second)
    finish()


def first_load_kernel(wq_ref, wkv_ref, wout_ref, out_ref, sems):
    def wait(count):
        for index in range(count):
            landed(out_ref, sems, index)

    def first():
        start_joined([wq_ref], wkv_ref, out_ref, sems)
        wait(out_ref.shape[0])

    def second():
        start_rows([wout_ref], out_ref, sems)
        wait(out_ref.shape[0] - 1)

    by_section(first, second)


def first_own_kernel(
    mine_ref, near_ref, far_ref, cross_ref, gain_ref, chunks, out_ref, x_ref, x, staged, out_sems
):
    rank = lax.axis_index("mp")
    share = mine_ref.shape[0]
    for distance, ref in enumerate((mine_ref, near_ref, far_ref, cross_ref)):
        at = pl.multiple_of(jnp.bitwise_xor(rank, distance) * share, share)
        x[pl.ds(at, share), :] = ref[...].astype(F32)
    x_ref[...] = x[...].astype(BF)
    put, finish = sender(staged, out_ref, out_sems)
    tokens = x_ref.shape[0]
    count, width, _ = chunks.shape

    def first():
        project_rows(x_ref[...], gain_ref[...], chunks, lambda at: chunks.at[at], put)

    def second():
        put(count * width, jnp.zeros((tokens, 128), BF))
        put((count - 1) * width, jnp.zeros((tokens, width), BF))
        for index in range(count - 1):
            put(index * width, dot_nt(x_ref[...], chunks[index]).astype(BF))

    by_section(first, second)
    finish()


def chosen(first_ref, second_ref):
    return jnp.where(lax.axis_index("section") == 0, first_ref[...], second_ref[...])


def summed(pair_ref, across_ref, beside_ref):
    even = lax.axis_index("mp") % 2 == 0
    lower = jnp.where(even, across_ref[...], beside_ref[...])
    upper = jnp.where(even, beside_ref[...], across_ref[...])
    return pair_ref[...].astype(F32) + jnp.concatenate([lower, upper], axis=0).astype(F32)


def project_kernel(
    r0_ref, r1_ref, pair_ref, across_ref, beside_ref, g0_ref, g1_ref, chunks, out_ref,
    staged, out_sems,
):
    added = summed(pair_ref, across_ref, beside_ref)
    rows = (chosen(r0_ref, r1_ref).astype(F32) + added).astype(BF)
    put, finish = sender(staged, out_ref, out_sems)
    project_rows(rows, chosen(g0_ref, g1_ref), chunks, lambda at: chunks.at[at], put)
    finish()


def head_grad_kernel(
    r0_ref, r1_ref, pair_ref, across_ref, beside_ref, g0_ref, g1_ref, chunks, out_ref, rows_ref,
    staged, out_sems,
):
    added = summed(pair_ref, across_ref, beside_ref)
    rows = chosen(r0_ref, r1_ref).astype(F32) + chosen(g0_ref, g1_ref) * added
    rows_ref[...] = rows.astype(BF)
    count, width, _ = chunks.shape
    put, finish = sender(staged, out_ref, out_sems)
    for index in range(count):
        put(index * width, dot_nt(rows_ref[...], chunks[index]).astype(BF))
    finish()


def add_parts(load, count):
    total = load(0).astype(F32)
    for index in range(1, count):
        total = total + load(index).astype(F32)
    return total


def part_sums(parts, sems):
    def total(index):
        wait_span(parts, sems, index)
        span = spans(parts.shape[2])[index]
        return add_parts(lambda source: parts[source, :, span], parts.shape[0])

    return total


def scaled_sum(total, tile):
    ranges = spans(tile.shape[1])
    squares = jnp.sum(total(len(ranges) - 1), axis=1, keepdims=True)
    scale = lax.rsqrt(squares / MODEL_WIDTH + EPSILON)
    for index, span in enumerate(ranges[:-1]):
        tile[:, span] = (total(index) * scale).astype(BF)
    tile[:, ranges[-1]] = two_lanes(scale)


def plain_sum(total, tile):
    for index, span in enumerate(spans(tile.shape[1])):
        tile[:, span] = total(index).astype(BF)


def first_sum_kernel(parts_ref, out_ref, parts, sems):
    start_spans(parts_ref, parts, sems)
    total = part_sums(parts, sems)
    by_section(lambda: scaled_sum(total, out_ref), lambda: plain_sum(total, out_ref))


def sum_kernel(adder, parts_ref, out_ref, parts, tile, sems, out_sems):
    start_spans(parts_ref, parts, sems)
    adder(part_sums(parts, sems), tile)
    repeat_out(tile, out_ref, out_sems)
    repeat_wait(tile, out_ref, out_sems)


def choose_kernel(first_ref, second_ref, out_ref, sems):
    first = first_ref.at[:, : out_ref.shape[2]]
    second = second_ref.at[:, : out_ref.shape[2]]
    by_section(
        lambda: repeat_out(first, out_ref, sems), lambda: repeat_out(second, out_ref, sems)
    )
    repeat_wait(first, out_ref, sems)


def fill_bias(seq_ref, bias):
    section = lax.axis_index("section")
    tokens = bias.shape[0]
    keys = lax.broadcasted_iota(jnp.int32, (tokens, tokens), 0)
    queries = lax.broadcasted_iota(jnp.int32, (tokens, tokens), 1)
    key_segment = jnp.zeros((tokens, tokens), jnp.int32)
    query_segment = jnp.zeros((tokens, tokens), jnp.int32)
    bound = 0
    for index in range(NSEQ):
        bound = bound + seq_ref[section, index]
        key_segment = key_segment + (keys >= bound).astype(jnp.int32)
        query_segment = query_segment + (queries >= bound).astype(jnp.int32)
    allowed = (keys <= queries) & (key_segment == query_segment)
    bias[...] = jnp.where(allowed, 0.0, MASKED)


def head_columns(head):
    return slice(head * HEAD_SIZE, (head + 1) * HEAD_SIZE)


def softmax_blocks(tokens, body):
    def one_head(head, carry):
        for at in range(0, tokens, QB):
            lanes = pl.ds(pl.multiple_of(head * tokens + at, QB), QB)
            body(slice(at, at + QB), lanes, at + QB)
        return carry

    lax.fori_loop(0, GROUP_HEADS, one_head, 0, unroll=4)


def clear_unreached(target, tokens):
    for head in range(GROUP_HEADS):
        for at in range(0, tokens - QB, QB):
            lanes = slice(head * tokens + at, head * tokens + at + QB)
            target[at + QB :, lanes] = jnp.zeros((tokens - at - QB, QB), target.dtype)


def weights_of(scores, bias):
    scores = scores * (SOFT * LOG2E) + bias
    raised = jnp.exp2(scores - jnp.max(scores, axis=0, keepdims=True))
    return raised * (1.0 / jnp.sum(raised, axis=0, keepdims=True))


def start_qkv(qkv_ref, qkv, q_cols, sems):
    pltpu.make_async_copy(qkv_ref.at[:, q_cols:], qkv.at[:, q_cols:], sems.at[0]).start()
    for group in range(q_cols // (GROUP_HEADS * HEAD_SIZE)):
        start_group(qkv_ref, qkv, sems, 1, group)


def start_group(source, target, sems, first, group):
    width = GROUP_HEADS * HEAD_SIZE
    at = (slice(None), slice(group * width, (group + 1) * width))
    pltpu.make_async_copy(source.at[at], target.at[at], sems.at[first + group]).start()


def wait_group(target, sems, first, group):
    width = GROUP_HEADS * HEAD_SIZE
    at = (slice(None), slice(group * width, (group + 1) * width))
    pltpu.make_async_copy(target.at[at], target.at[at], sems.at[first + group]).wait()


def forward_kernel(seq_ref, qkv_ref, wout0_ref, *refs):
    *wout1_refs, out_ref, qkv, chunks, bias, scores, weights, attended, sems, in_sems = refs
    tokens, q_cols = attended.shape
    start_qkv(qkv_ref, qkv, q_cols, in_sems)
    by_section(
        lambda: start_rows([wout0_ref], chunks, sems),
        lambda: start_rows(wout1_refs, chunks, sems),
    )
    fill_bias(seq_ref, bias)
    clear_unreached(weights, tokens)
    groups = q_cols // (GROUP_HEADS * HEAD_SIZE)
    pltpu.make_async_copy(qkv.at[:, q_cols:], qkv.at[:, q_cols:], in_sems.at[0]).wait()
    for group in range(groups):
        at = q_cols + group * HEAD_SIZE
        keys = qkv[:, at : at + HEAD_SIZE]
        at = at + groups * HEAD_SIZE
        values_t = qkv[:, at : at + HEAD_SIZE].astype(F32).T.astype(BF)
        wait_group(qkv, in_sems, 1, group)
        for index in range(GROUP_HEADS):
            columns = head_columns(group * GROUP_HEADS + index)
            scores[:, index * tokens : (index + 1) * tokens] = dot_nt(keys, qkv[:, columns])

        def block(queries, lanes, reach):
            weights[:reach, lanes] = weights_of(
                scores[:reach, lanes], bias[:reach, queries]
            ).astype(BF)

        softmax_blocks(tokens, block)
        for index in range(GROUP_HEADS):
            columns = head_columns(group * GROUP_HEADS + index)
            mixed = dot_nn(values_t, weights[:, index * tokens : (index + 1) * tokens])
            attended[:, columns] = mixed.T.astype(BF)
    count, width, _ = chunks.shape
    out = dot_nn(attended[:, :width], landed(chunks, sems, 0)[...])
    for index in range(1, count):
        columns = slice(index * width, (index + 1) * width)
        out = out + dot_nn(attended[:, columns], landed(chunks, sems, index)[...])
    out_ref[...] = out.astype(BF)


def backward_kernel(
    seq_ref, qkv_ref, grads_ref, wq0_ref, wq1_ref, wkv0_ref, wkv1_ref, out_ref,
    qkv, grads, chunks, bias, scores, weight_grads, weights, score_grads, scaled_q, scaled_kv,
    sems, in_sems,
):
    tokens, q_cols = grads.shape
    groups = q_cols // (GROUP_HEADS * HEAD_SIZE)
    pltpu.make_async_copy(qkv_ref.at[:, q_cols:], qkv.at[:, q_cols:], in_sems.at[0]).start()
    start_group(qkv_ref, qkv, in_sems, 1, 0)
    start_group(grads_ref, grads, in_sems, 1 + groups, 0)
    fill_bias(seq_ref, bias)
    clear_unreached(weights, tokens)
    clear_unreached(score_grads, tokens)
    kv_cols = groups * HEAD_SIZE
    pltpu.make_async_copy(qkv.at[:, q_cols:], qkv.at[:, q_cols:], in_sems.at[0]).wait()
    wait_group(qkv, in_sems, 1, 0)
    wait_group(grads, in_sems, 1 + groups, 0)
    for group in range(1, groups):
        start_group(qkv_ref, qkv, in_sems, 1, group)
        start_group(grads_ref, grads, in_sems, 1 + groups, group)
    by_section(
        lambda: start_joined([wq0_ref], wkv0_ref, chunks, sems),
        lambda: start_joined([wq1_ref], wkv1_ref, chunks, sems),
    )
    scale_lanes = qkv[:, q_cols + 2 * kv_cols :].astype(F32)
    scale_column = jnp.sum(scale_lanes, axis=1, keepdims=True)
    scale_row = jnp.sum(scale_lanes.T, axis=0, keepdims=True) * SOFT
    for group in range(groups):
        at = q_cols + group * HEAD_SIZE
        keys = qkv[:, at : at + HEAD_SIZE]
        keys_t = keys.astype(F32).T.astype(BF)
        at = at + kv_cols
        values = qkv[:, at : at + HEAD_SIZE]
        if group > 0:
            wait_group(qkv, in_sems, 1, group)
            wait_group(grads, in_sems, 1 + groups, group)
        for index in range(GROUP_HEADS):
            columns = head_columns(group * GROUP_HEADS + index)
            lanes = slice(index * tokens, (index + 1) * tokens)
            scores[:, lanes] = dot_nt(keys, qkv[:, columns])
            weight_grads[:, lanes] = dot_nt(values, grads[:, columns])
        def block(queries, lanes, reach):
            weight = weights_of(scores[:reach, lanes], bias[:reach, queries])
            weights[:reach, lanes] = weight.astype(BF)
            weight_grad = weight_grads[:reach, lanes]
            mean = jnp.sum(weight_grad * weight, axis=0, keepdims=True)
            score_grads[:reach, lanes] = (weight * (weight_grad - mean)).astype(BF)

        softmax_blocks(tokens, block)
        key_grad = jnp.zeros((tokens, HEAD_SIZE), F32)
        value_grad = jnp.zeros((tokens, HEAD_SIZE), F32)
        for index in range(GROUP_HEADS):
            columns = head_columns(group * GROUP_HEADS + index)
            lanes = slice(index * tokens, (index + 1) * tokens)
            score_grad = score_grads[:, lanes]
            scaled_q[columns, :] = (dot_nn(keys_t, score_grad) * scale_row).astype(BF)
            key_grad = key_grad + dot_nn(score_grad, qkv[:, columns])
            value_grad = value_grad + dot_nn(weights[:, lanes], grads[:, columns])
        at = group * HEAD_SIZE
        scaled_kv[:, at : at + HEAD_SIZE] = (key_grad * (scale_column * SOFT)).astype(BF)
        at = at + kv_cols
        scaled_kv[:, at : at + HEAD_SIZE] = (value_grad * scale_column).astype(BF)
    count, width, _ = chunks.shape
    through = dot_nt(landed(chunks, sems, count - 1)[...], scaled_kv[...])
    for index in range(count - 1):
        rows = slice(index * width, (index + 1) * width)
        through = through + dot_nn(landed(chunks, sems, index)[...], scaled_q[rows, :])
    out_ref[...] = through.T.astype(BF)


def merger_kernel(
    marks_ref, owners_ref, last_ref, pair_ref, across_ref, beside_ref, g0_ref, g1_ref, weight_ref,
    out_ref, grad_ref, rows, hidden, counts, places,
):
    added = summed(pair_ref, across_ref, beside_ref)
    rows[...] = last_ref[...].astype(F32) + chosen(g0_ref, g1_ref) * added
    share = grad_ref.shape[0]
    at = pl.multiple_of(lax.axis_index("mp") * share, share)
    grad_ref[...] = rows[pl.ds(at, share), :].astype(BF)
    x = rows[...].astype(BF)
    cols = weight_ref.shape[0]
    for start in range(0, cols, 256):
        hidden[:, start : start + 256] = dot_nt(x, weight_ref[start : start + 256, :])
    dp_count, sections = out_ref.shape[:2]
    owner_count = dp_count * sections

    def clear(owner, carry):
        counts[owner] = 0
        for slot in range(CAP):
            places[owner * CAP + slot] = -1
        return carry

    lax.fori_loop(0, owner_count, clear, 0)

    def place(block, carry):
        owner = owners_ref[0, block]

        @pl.when(marks_ref[0, block] == 1)
        def _():
            slot = counts[owner]
            places[owner * CAP + slot] = block
            counts[owner] = slot + 1

        return carry

    lax.fori_loop(0, marks_ref.shape[1], place, 0)

    def send(owner, carry):
        pieces = []
        for slot in range(CAP):
            block = places[owner * CAP + slot]
            at = pl.multiple_of(jnp.maximum(block, 0) * VB, VB)
            pieces.append(jnp.where(block >= 0, hidden[pl.ds(at, VB), :], 0.0))
        out_ref[lax.rem(owner, dp_count), lax.div(owner, dp_count)] = jnp.concatenate(
            pieces, axis=0
        ).astype(BF)
        return carry

    lax.fori_loop(0, owner_count, send, 0)


def merger_sum_kernel(parts_ref, own_ref, other_ref):
    section = lax.axis_index("section")
    sources = parts_ref.shape[0]

    def total(index):
        return add_parts(lambda source: parts_ref[source, index], sources)

    first, second = total(0), total(1)
    own_ref[...] = jnp.where(section == 0, first, second)
    other_ref[...] = jnp.where(section == 0, second, first).astype(BF)


def gelu_slope(values):
    cumulative = 0.5 * (1.0 + lax.erf(values * (1.0 / math.sqrt(2.0))))
    return cumulative + values * jnp.exp(-0.5 * values * values) * (1.0 / math.sqrt(2.0 * math.pi))


def local(
    embeds,
    cotangent,
    norm_gain,
    w_query,
    w_keyval,
    w_out,
    seq_lengths,
    image_mask,
    block_owner,
    merger_weight,
    merger_pre,
):
    section = lax.axis_index("section")
    mp_count = lax.axis_size("mp")
    dp_count = lax.axis_size("dp")
    rows, width = embeds.shape[1:]
    tokens = rows * mp_count
    share = tokens // dp_count
    q_cols = w_query.shape[3]
    kv_cols = w_keyval.shape[4]
    joined = q_cols + 2 * kv_cols + 128
    emb, cot = embeds[0], cotangent[0]
    wq, wout = w_query[0, 0], w_out[0, 0]
    wkv = w_keyval[0, 0].reshape(width, 2 * kv_cols)
    gain = norm_gain[0]

    def partner(index):
        other, rank = 1 - index // mp_count, (index % mp_count + mp_count // 2) % mp_count
        return other * mp_count + rank

    everyone = range(2 * mp_count)
    from_first = [(i, partner(i)) for i in everyone if i < mp_count]
    from_second = [(i, partner(i)) for i in everyone if i >= mp_count]

    def swap(array, pairs):
        return lax.ppermute(array, ("section", "mp"), pairs)

    def scatter(array, axis):
        return lax.all_to_all(array, axis, split_axis=0, concat_axis=0, tiled=True)

    def spread(copies):
        return scatter(copies, "dp").reshape(tokens, copies.shape[2])

    def gather(array, axis):
        return lax.all_gather(array, axis, axis=0, tiled=True)

    def chunks_of(count):
        return pltpu.VMEM((count, width, width), BF)

    own_x, other_x = jnp.where(section == 0, emb, cot), jnp.where(section == 0, cot, emb)
    received_x = swap(other_x, from_first + from_second)
    gain_x = swap(gain, from_first + from_second)
    def vmem(*shape):
        return pltpu.VMEM(shape, BF)

    def dma(count):
        return pltpu.SemaphoreType.DMA((count,))

    def other_rows_parts(x):
        return pl.pallas_call(
            first_kernel,
            out_shape=pltpu.HBM((dp_count, share, joined), BF),
            in_specs=[VMEM] * 2 + [HBM] * 3,
            out_specs=HBM,
            scratch_shapes=[chunks_of(5), vmem(dp_count, share, joined), dma(5), dma(6)],
            compiler_params=params(24),
            cost_estimate=cost(2 * tokens * width * joined, 6 << 20),
        )(x, gain, *in_hbm(wq, wkv, wout))

    def first_sum(parts):
        return pl.pallas_call(
            first_sum_kernel,
            out_shape=shape_of((share, joined), BF),
            in_specs=[ANY],
            out_specs=VMEM,
            scratch_shapes=[vmem(dp_count, share, joined), dma(6)],
            compiler_params=params(24),
            cost_estimate=cost(parts.size, 2 << 20),
        )(parts)

    def summed_copies(adder, parts):
        cols = parts.shape[2]
        return pl.pallas_call(
            functools.partial(sum_kernel, adder),
            out_shape=pltpu.HBM((dp_count, share, cols), BF),
            in_specs=[ANY],
            out_specs=HBM,
            scratch_shapes=[vmem(dp_count, share, cols), vmem(share, cols), dma(6), dma(dp_count)],
            compiler_params=params(24),
            cost_estimate=cost(parts.size, 4 << 20),
        )(parts)

    def chosen_copies(first, second, cols):
        return pl.pallas_call(
            choose_kernel,
            out_shape=pltpu.HBM((dp_count, share, cols), BF),
            in_specs=[VMEM] * 2,
            out_specs=HBM,
            scratch_shapes=[dma(dp_count)],
            compiler_params=params(24),
            cost_estimate=cost(0, 2 << 20),
        )(first, second)

    def loaded(joins, firsts, seconds):
        count = 5 if joins else 4
        return pl.pallas_call(
            functools.partial(load_kernel, joins, len(firsts)),
            out_shape=pltpu.VMEM((count, width, width), BF),
            in_specs=[HBM] * (len(firsts) + len(seconds)),
            out_specs=VMEM,
            scratch_shapes=[dma(count)],
            compiler_params=params(16),
            cost_estimate=cost(0, 5 << 20),
        )(*in_hbm(*firsts, *seconds))

    def beside(array, distance):
        return lax.ppermute(array, "mp", [(i, i ^ distance) for i in range(mp_count)])

    def sum_over_mp(part, *later):
        mate = beside(part, 1)
        at = lax.axis_index("mp") % 2 * (tokens // 2)

        def half(array):
            return lax.dynamic_slice_in_dim(array, at, tokens // 2).astype(F32)

        pair_half = (half(part) + half(mate)).astype(BF)
        across = beside(pair_half, 2)
        pair_half, part, mate, *later = lax.optimization_barrier((pair_half, part, mate, *later))
        pair = (part.astype(F32) + mate.astype(F32)).astype(BF)
        return (pair, across, beside(across, 1)), later

    others = [beside(own_x, distance) for distance in (1, 2, 3)]
    first_chunks = pl.pallas_call(
        first_load_kernel,
        out_shape=pltpu.VMEM((5, width, width), BF),
        in_specs=[HBM] * 3,
        out_specs=VMEM,
        scratch_shapes=[dma(5)],
        compiler_params=params(16),
        cost_estimate=cost(0, 5 << 20),
    )(*in_hbm(wq, wkv, wout))
    own_parts, own_all = pl.pallas_call(
        first_own_kernel,
        out_shape=[pltpu.HBM((dp_count, share, joined), BF), shape_of((tokens, width), BF)],
        in_specs=[VMEM] * 6,
        out_specs=[HBM, VMEM],
        scratch_shapes=[
            pltpu.VMEM((tokens, width), F32),
            vmem(dp_count, share, joined),
            dma(6),
        ],
        compiler_params=params(24),
        cost_estimate=cost(2 * tokens * width * joined, 6 << 20),
    )(own_x, *others, gain, first_chunks)
    own_parts, received_x, gain_x, wq_s, wout_s = lax.optimization_barrier(
        (own_parts, received_x, gain_x, wq, wout)
    )
    own_parts = scatter(own_parts, "dp")
    wq_b = swap(wq_s, from_second)
    cuts = (5 * q_cols // 16, 5 * q_cols // 8)
    wout_a0 = swap(wout_s[: cuts[0]], from_first)
    wout_a1, wout_a2 = wout_s[cuts[0] : cuts[1]], wout_s[cuts[1] :]
    other_parts = other_rows_parts(gather(received_x, "mp"))
    own_parts, other_parts, wout_a0, wout_a1, wout_a2 = lax.optimization_barrier(
        (own_parts, other_parts, wout_a0, wout_a1, wout_a2)
    )
    wout_a1 = swap(wout_a1, from_first)
    own = first_sum(own_parts)
    mine_all = gather(other_x, "mp")
    other_parts, own, mine_all = lax.optimization_barrier(
        (scatter(other_parts, "dp"), own, mine_all)
    )
    other = first_sum(other_parts)
    received = swap(other, from_first)
    received_grad, wkv_s = lax.optimization_barrier((swap(other, from_second), wkv))
    wkv_b = swap(wkv_s, from_second)
    copies, wout_a1, wout_a2 = lax.optimization_barrier(
        (chosen_copies(own, received, joined), wout_a1, wout_a2)
    )
    wout_a2 = swap(wout_a2, from_first)
    grad_copies = chosen_copies(received_grad, own, q_cols)
    qkv_first, grad_copies, wq_b, wq_s, wkv_s = lax.optimization_barrier(
        (spread(copies), grad_copies, wq_b, wq, wkv)
    )
    wout_a = (wout_a0, wout_a1, wout_a2)
    wq_a, wkv_a = swap(wq_s, from_first), swap(wkv_s, from_first)
    head_grad_last = spread(grad_copies)

    def layer_forward(qkv, wouts):
        out = pl.pallas_call(
            forward_kernel,
            out_shape=shape_of((tokens, width), BF),
            in_specs=[SMEM, ANY] + [HBM] * (1 + len(wouts[1])),
            out_specs=VMEM,
            scratch_shapes=[
                vmem(tokens, joined),
                chunks_of(4),
                pltpu.VMEM((tokens, tokens), F32),
                pltpu.VMEM((tokens, GROUP_HEADS * tokens), F32),
                vmem(tokens, GROUP_HEADS * tokens),
                vmem(tokens, q_cols),
                dma(4),
                dma(3),
            ],
            compiler_params=params(32),
            cost_estimate=cost(6 * tokens * tokens * q_cols, 4 << 20),
        )(seq_lengths, qkv, *in_hbm(wouts[0], *wouts[1]))
        return out

    def rows_after(resident, sums):
        even = lax.axis_index("mp") % 2 == 0
        lower, upper = jnp.where(even, *sums[1:]), jnp.where(even, *sums[:0:-1])
        added = sums[0].astype(F32) + jnp.concatenate([lower, upper], axis=0).astype(F32)
        return (resident.astype(F32) + added).astype(BF)

    out, wkv_b = lax.optimization_barrier((layer_forward(qkv_first, (wout, wout_a)), wkv_b))
    sums, pieces = sum_over_mp(out, wq_b, wkv_b, wq, wkv)
    joined_last = loaded(True, pieces[:2], pieces[2:])
    parts = pl.pallas_call(
        project_kernel,
        out_shape=pltpu.HBM((dp_count, share, joined), BF),
        in_specs=[VMEM] * 8,
        out_specs=HBM,
        scratch_shapes=[vmem(dp_count, share, joined), dma(6)],
        compiler_params=params(24),
        cost_estimate=cost(2 * tokens * width * joined, 6 << 20),
    )(own_all, mine_all, *sums, gain_x, gain, joined_last)
    parts, head_grad_last = lax.optimization_barrier((parts, head_grad_last))
    qkv_last = spread(summed_copies(scaled_sum, scatter(parts, "dp")))
    wout_b = swap(wout, from_second)
    wout_last = jnp.where(section == 0, wout_b, wout)
    h_one = rows_after(jnp.where(section == 0, own_all, mine_all), sums)
    rows_after(h_one, sum_over_mp(layer_forward(qkv_last, (wout_last, (wout_last,))))[0])

    def layer_backward(qkv, head_grads, wqs, wkvs, later=()):
        through = pl.pallas_call(
            backward_kernel,
            out_shape=shape_of((tokens, width), BF),
            in_specs=[SMEM, ANY, ANY] + [HBM] * 4,
            out_specs=VMEM,
            scratch_shapes=[
                vmem(tokens, joined),
                vmem(tokens, q_cols),
                chunks_of(5),
                pltpu.VMEM((tokens, tokens), F32),
                pltpu.VMEM((tokens, GROUP_HEADS * tokens), F32),
                pltpu.VMEM((tokens, GROUP_HEADS * tokens), F32),
                vmem(tokens, GROUP_HEADS * tokens),
                vmem(tokens, GROUP_HEADS * tokens),
                vmem(q_cols, tokens),
                vmem(tokens, 2 * kv_cols),
                dma(5),
                dma(5),
            ],
            compiler_params=params(32),
            cost_estimate=cost(12 * tokens * tokens * q_cols, 6 << 20),
        )(seq_lengths, qkv, head_grads, *in_hbm(*wqs, *wkvs))
        return sum_over_mp(through, *later)

    sums, pieces = layer_backward(
        qkv_last,
        *in_hbm(head_grad_last),
        (wq_b, wq),
        (wkv_b, wkv),
        later=(wout, *wout_a),
    )
    parts, grad_one = pl.pallas_call(
        head_grad_kernel,
        out_shape=[pltpu.HBM((dp_count, share, q_cols), BF), shape_of((tokens, width), BF)],
        in_specs=[VMEM] * 8,
        out_specs=[HBM, VMEM],
        scratch_shapes=[vmem(dp_count, share, q_cols), dma(4)],
        compiler_params=params(24),
        cost_estimate=cost(2 * tokens * width * q_cols, 4 << 20),
    )(mine_all, own_all, *sums, gain_x, gain, loaded(False, pieces[:1], pieces[1:]))
    parts, wq_a, wkv_a = lax.optimization_barrier((scatter(parts, "dp"), wq_a, wkv_a))
    head_grad_first = spread(summed_copies(plain_sum, parts))
    sums, _ = layer_backward(qkv_first, head_grad_first, (wq, wq_a), (wkv, wkv_a))

    hidden_cols = merger_weight.shape[0]
    outgoing, input_grad = pl.pallas_call(
        merger_kernel,
        out_shape=[
            shape_of((dp_count, 2, CAP * VB, hidden_cols), BF),
            shape_of((rows, width), BF),
        ],
        in_specs=[SMEM, SMEM] + [VMEM] * 7,
        out_specs=[VMEM] * 2,
        scratch_shapes=[
            pltpu.VMEM((tokens, width), F32),
            pltpu.VMEM((tokens, hidden_cols), F32),
            pltpu.SMEM((2 * dp_count,), jnp.int32),
            pltpu.SMEM((2 * dp_count * CAP,), jnp.int32),
        ],
        compiler_params=params(24),
    )(image_mask, block_owner, grad_one, *sums, gain, gain_x, merger_weight)
    kept, passed = pl.pallas_call(
        merger_sum_kernel,
        out_shape=[
            shape_of((CAP * VB, hidden_cols), F32),
            shape_of((CAP * VB, hidden_cols), BF),
        ],
        in_specs=[VMEM],
        out_specs=[VMEM] * 2,
        compiler_params=params(24),
    )(scatter(outgoing, "dp"))
    crossed = lax.ppermute(passed, "section", [(0, 1), (1, 0)]).astype(F32)
    first = jnp.where(section == 0, kept, crossed)
    second = jnp.where(section == 0, crossed, kept)
    hidden_grad = jnp.stack([first, second]).reshape(2, CAP, VB, hidden_cols)
    merger_grad = gelu_slope(merger_pre[0].astype(F32)) * hidden_grad
    return (input_grad[None], merger_grad[None])


def solution(mesh):
    placed = (
        P("section", "mp", "dp"),
        P("section", "mp", "dp"),
        P(None, "section", "dp"),
        P(None, "section", "dp", "mp"),
        P(None, "section", "dp", None, "mp"),
        P(None, "section", "mp", "dp"),
        P(),
        P("section", None),
        P("section", None),
        P("mp", "dp"),
        P(("section", "dp"), None, None, None, "mp"),
    )
    return jax.shard_map(
        local,
        mesh=mesh,
        in_specs=placed,
        out_specs=(P("section", "mp", "dp"), P(("section", "dp"), None, None, None, "mp")),
        check_vma=False,
    )
```

```python
import functools
import math

import jax
import jax.numpy as jnp
from jax import lax
from jax.experimental import pallas as pl
from jax.experimental.pallas import tpu as pltpu
from jax.sharding import PartitionSpec as P

MODEL_WIDTH = 8192
HEAD_SIZE = 128
GROUP_HEADS = 8
CAP = 2
VB = 8
NSEQ = 3

EPSILON = 1e-06
MASKED = -1e30
SOFT = 1.0 / math.sqrt(HEAD_SIZE)
LOG2E = math.log2(math.e)
QB = 128

BF = jnp.bfloat16
F32 = jnp.float32

VMEM = pl.BlockSpec(memory_space=pltpu.VMEM)
SMEM = pl.BlockSpec(memory_space=pltpu.SMEM)
ANY = pl.BlockSpec(memory_space=pl.ANY)
HBM = pl.BlockSpec(memory_space=pltpu.HBM)


def shape_of(shape, dtype):
    return jax.ShapeDtypeStruct(shape, dtype)


def in_hbm(*arrays):
    return [pltpu.with_memory_space_constraint(array, pltpu.HBM) for array in arrays]


def params(mebibytes):
    return pltpu.CompilerParams(vmem_limit_bytes=mebibytes << 20)


def cost(flops, bytes_accessed):
    return pl.CostEstimate(flops=flops, bytes_accessed=bytes_accessed, transcendentals=0)


def dot_nn(left, right):
    return jnp.dot(left, right, preferred_element_type=F32)


def dot_nt(left, right):
    return lax.dot_general(left, right, (((1,), (1,)), ((), ())), preferred_element_type=F32)


def two_lanes(column):
    high = column.astype(BF).astype(F32)
    lane = lax.broadcasted_iota(jnp.int32, (column.shape[0], 128), 1)
    return jnp.where(lane == 0, high, jnp.where(lane == 1, column - high, 0.0)).astype(BF)


def start_columns(sources, chunks, sems):
    width, index = chunks.shape[2], 0
    for source in sources:
        for start in range(0, source.shape[1], width):
            block = source.at[:, start : start + width]
            pltpu.make_async_copy(block, chunks.at[index], sems.at[index]).start()
            index += 1


def start_rows(sources, chunks, sems):
    rows, at = chunks.shape[1], 0
    for source in sources:
        start = 0
        while start < source.shape[0]:
            index, within = at // rows, at % rows
            count = min(rows - within, source.shape[0] - start)
            block = source.at[start : start + count, :]
            place = chunks.at[index, within : within + count, :]
            pltpu.make_async_copy(block, place, sems.at[index]).start()
            start, at = start + count, at + count


def start_joined(wqs, wkv_ref, chunks, sems):
    start_columns(wqs, chunks, sems)
    last = chunks.shape[0] - 1
    pltpu.make_async_copy(wkv_ref, chunks.at[last], sems.at[last]).start()


def landed(chunks, sems, index):
    pltpu.make_async_copy(chunks.at[index], chunks.at[index], sems.at[index]).wait()
    return chunks.at[index]


def by_section(first, second):
    section = lax.axis_index("section")
    pl.when(section == 0)(first)
    pl.when(section != 0)(second)


def spans(cols):
    return [slice(start, min(start + 512, cols)) for start in range(0, cols, 512)]


def start_spans(source, target, sems):
    for index, span in enumerate(spans(target.shape[-1])):
        at = (slice(None),) * (len(target.shape) - 1) + (span,)
        pltpu.make_async_copy(source.at[at], target.at[at], sems.at[index]).start()


def wait_span(target, sems, index):
    at = (slice(None),) * (len(target.shape) - 1) + (spans(target.shape[-1])[index],)
    pltpu.make_async_copy(target.at[at], target.at[at], sems.at[index]).wait()


def sender(staged, out_ref, sems):
    owners, share, cols = staged.shape

    def put(start, tile):
        span = slice(start, start + tile.shape[1])
        staged[:, :, span] = tile.reshape(owners, share, tile.shape[1])
        index = spans(cols).index(span)
        at = (slice(None), slice(None), span)
        pltpu.make_async_copy(staged.at[at], out_ref.at[at], sems.at[index]).start()

    def finish():
        for index in range(len(spans(cols))):
            wait_span(staged, sems, index)

    return put, finish


def repeat_out(tile, out_ref, sems):
    for place in range(out_ref.shape[0]):
        pltpu.make_async_copy(tile, out_ref.at[place], sems.at[place]).start()


def repeat_wait(tile, out_ref, sems):
    for place in range(out_ref.shape[0]):
        pltpu.make_async_copy(tile, out_ref.at[place], sems.at[place]).wait()


def project_rows(rows, gain, chunks, chunk_at, put):
    rows_f = rows.astype(F32)
    normed = (rows_f * gain).astype(BF)
    count, _, width = chunks.shape
    put(count * width, two_lanes(jnp.sum(rows_f * rows_f, axis=1, keepdims=True)))
    for index in range(count):
        put(index * width, dot_nn(normed, chunk_at(index)[...]).astype(BF))


def load_kernel(joined, pieces, *refs):
    *sources, out_ref, sems = refs

    def load(refs):
        if joined:
            start_joined(refs[:-1], refs[-1], out_ref, sems)
        else:
            start_rows(refs, out_ref, sems)

    by_section(lambda: load(sources[:pieces]), lambda: load(sources[pieces:]))
    for index in range(out_ref.shape[0]):
        landed(out_ref, sems, index)


def first_kernel(
    x_ref, gain_ref, wq_ref, wkv_ref, wout_ref, out_ref, chunks, staged, sems, out_sems
):
    put, finish = sender(staged, out_ref, out_sems)
    tokens = x_ref.shape[0]

    def rows():
        return jnp.concatenate([x_ref[tokens // 2 :, :], x_ref[: tokens // 2, :]], axis=0)

    def first():
        start_joined([wq_ref], wkv_ref, chunks, sems)
        project_rows(rows(), gain_ref[...], chunks, lambda at: landed(chunks, sems, at), put)

    def second():
        start_rows([wout_ref], chunks, sems)
        count, width, _ = chunks.shape
        put(count * width, jnp.zeros((tokens, 128), BF))
        put((count - 1) * width, jnp.zeros((tokens, width), BF))
        x = rows()
        for index in range(count - 1):
            put(index * width, dot_nt(x, landed(chunks, sems, index)[...]).astype(BF))

    by_section(first, second)
    finish()


def first_load_kernel(wq_ref, wkv_ref, wout_ref, out_ref, sems):
    def wait(count):
        for index in range(count):
            landed(out_ref, sems, index)

    def first():
        start_joined([wq_ref], wkv_ref, out_ref, sems)
        wait(out_ref.shape[0])

    def second():
        start_rows([wout_ref], out_ref, sems)
        wait(out_ref.shape[0] - 1)

    by_section(first, second)


def first_own_kernel(
    mine_ref, near_ref, far_ref, cross_ref, gain_ref, chunks, out_ref, x_ref, x, staged, out_sems
):
    rank = lax.axis_index("mp")
    share = mine_ref.shape[0]
    for distance, ref in enumerate((mine_ref, near_ref, far_ref, cross_ref)):
        at = pl.multiple_of(jnp.bitwise_xor(rank, distance) * share, share)
        x[pl.ds(at, share), :] = ref[...].astype(F32)
    x_ref[...] = x[...].astype(BF)
    put, finish = sender(staged, out_ref, out_sems)
    tokens = x_ref.shape[0]
    count, width, _ = chunks.shape

    def first():
        project_rows(x_ref[...], gain_ref[...], chunks, lambda at: chunks.at[at], put)

    def second():
        put(count * width, jnp.zeros((tokens, 128), BF))
        put((count - 1) * width, jnp.zeros((tokens, width), BF))
        for index in range(count - 1):
            put(index * width, dot_nt(x_ref[...], chunks[index]).astype(BF))

    by_section(first, second)
    finish()


def chosen(first_ref, second_ref):
    return jnp.where(lax.axis_index("section") == 0, first_ref[...], second_ref[...])


def summed(pair_ref, across_ref, beside_ref):
    even = lax.axis_index("mp") % 2 == 0
    lower = jnp.where(even, across_ref[...], beside_ref[...])
    upper = jnp.where(even, beside_ref[...], across_ref[...])
    return pair_ref[...].astype(F32) + jnp.concatenate([lower, upper], axis=0).astype(F32)


def project_kernel(
    r0_ref, r1_ref, pair_ref, across_ref, beside_ref, g0_ref, g1_ref, chunks, out_ref,
    staged, out_sems,
):
    added = summed(pair_ref, across_ref, beside_ref)
    rows = (chosen(r0_ref, r1_ref).astype(F32) + added).astype(BF)
    put, finish = sender(staged, out_ref, out_sems)
    project_rows(rows, chosen(g0_ref, g1_ref), chunks, lambda at: chunks.at[at], put)
    finish()


def head_grad_kernel(
    r0_ref, r1_ref, pair_ref, across_ref, beside_ref, g0_ref, g1_ref, chunks, out_ref, rows_ref,
    staged, out_sems,
):
    added = summed(pair_ref, across_ref, beside_ref)
    rows = chosen(r0_ref, r1_ref).astype(F32) + chosen(g0_ref, g1_ref) * added
    rows_ref[...] = rows.astype(BF)
    count, width, _ = chunks.shape
    put, finish = sender(staged, out_ref, out_sems)
    for index in range(count):
        put(index * width, dot_nt(rows_ref[...], chunks[index]).astype(BF))
    finish()


def add_parts(load, count):
    total = load(0).astype(F32)
    for index in range(1, count):
        total = total + load(index).astype(F32)
    return total


def part_sums(parts, sems):
    def total(index):
        wait_span(parts, sems, index)
        span = spans(parts.shape[2])[index]
        return add_parts(lambda source: parts[source, :, span], parts.shape[0])

    return total


def scaled_sum(total, tile):
    ranges = spans(tile.shape[1])
    squares = jnp.sum(total(len(ranges) - 1), axis=1, keepdims=True)
    scale = lax.rsqrt(squares / MODEL_WIDTH + EPSILON)
    for index, span in enumerate(ranges[:-1]):
        tile[:, span] = (total(index) * scale).astype(BF)
    tile[:, ranges[-1]] = two_lanes(scale)


def plain_sum(total, tile):
    for index, span in enumerate(spans(tile.shape[1])):
        tile[:, span] = total(index).astype(BF)


def first_sum_kernel(parts_ref, out_ref, parts, sems):
    start_spans(parts_ref, parts, sems)
    total = part_sums(parts, sems)
    by_section(lambda: scaled_sum(total, out_ref), lambda: plain_sum(total, out_ref))


def sum_kernel(adder, parts_ref, out_ref, parts, tile, sems, out_sems):
    start_spans(parts_ref, parts, sems)
    adder(part_sums(parts, sems), tile)
    repeat_out(tile, out_ref, out_sems)
    repeat_wait(tile, out_ref, out_sems)


def choose_kernel(first_ref, second_ref, out_ref, sems):
    first = first_ref.at[:, : out_ref.shape[2]]
    second = second_ref.at[:, : out_ref.shape[2]]
    by_section(
        lambda: repeat_out(first, out_ref, sems), lambda: repeat_out(second, out_ref, sems)
    )
    repeat_wait(first, out_ref, sems)


def fill_bias(seq_ref, bias):
    section = lax.axis_index("section")
    tokens = bias.shape[0]
    keys = lax.broadcasted_iota(jnp.int32, (tokens, tokens), 0)
    queries = lax.broadcasted_iota(jnp.int32, (tokens, tokens), 1)
    key_segment = jnp.zeros((tokens, tokens), jnp.int32)
    query_segment = jnp.zeros((tokens, tokens), jnp.int32)
    bound = 0
    for index in range(NSEQ):
        bound = bound + seq_ref[section, index]
        key_segment = key_segment + (keys >= bound).astype(jnp.int32)
        query_segment = query_segment + (queries >= bound).astype(jnp.int32)
    allowed = (keys <= queries) & (key_segment == query_segment)
    bias[...] = jnp.where(allowed, 0.0, MASKED)


def head_columns(head):
    return slice(head * HEAD_SIZE, (head + 1) * HEAD_SIZE)


def softmax_blocks(tokens, body):
    def one_head(head, carry):
        for at in range(0, tokens, QB):
            lanes = pl.ds(pl.multiple_of(head * tokens + at, QB), QB)
            body(slice(at, at + QB), lanes, at + QB)
        return carry

    lax.fori_loop(0, GROUP_HEADS, one_head, 0, unroll=4)


def clear_unreached(target, tokens):
    for head in range(GROUP_HEADS):
        for at in range(0, tokens - QB, QB):
            lanes = slice(head * tokens + at, head * tokens + at + QB)
            target[at + QB :, lanes] = jnp.zeros((tokens - at - QB, QB), target.dtype)


def weights_of(scores, bias):
    scores = scores * (SOFT * LOG2E) + bias
    raised = jnp.exp2(scores - jnp.max(scores, axis=0, keepdims=True))
    return raised * (1.0 / jnp.sum(raised, axis=0, keepdims=True))


def start_qkv(qkv_ref, qkv, q_cols, sems):
    pltpu.make_async_copy(qkv_ref.at[:, q_cols:], qkv.at[:, q_cols:], sems.at[0]).start()
    for group in range(q_cols // (GROUP_HEADS * HEAD_SIZE)):
        start_group(qkv_ref, qkv, sems, 1, group)


def start_group(source, target, sems, first, group):
    width = GROUP_HEADS * HEAD_SIZE
    at = (slice(None), slice(group * width, (group + 1) * width))
    pltpu.make_async_copy(source.at[at], target.at[at], sems.at[first + group]).start()


def wait_group(target, sems, first, group):
    width = GROUP_HEADS * HEAD_SIZE
    at = (slice(None), slice(group * width, (group + 1) * width))
    pltpu.make_async_copy(target.at[at], target.at[at], sems.at[first + group]).wait()


def forward_kernel(seq_ref, qkv_ref, wout0_ref, *refs):
    *wout1_refs, out_ref, qkv, chunks, bias, scores, weights, attended, sems, in_sems = refs
    tokens, q_cols = attended.shape
    start_qkv(qkv_ref, qkv, q_cols, in_sems)
    by_section(
        lambda: start_rows([wout0_ref], chunks, sems),
        lambda: start_rows(wout1_refs, chunks, sems),
    )
    fill_bias(seq_ref, bias)
    clear_unreached(weights, tokens)
    groups = q_cols // (GROUP_HEADS * HEAD_SIZE)
    pltpu.make_async_copy(qkv.at[:, q_cols:], qkv.at[:, q_cols:], in_sems.at[0]).wait()
    for group in range(groups):
        at = q_cols + group * HEAD_SIZE
        keys = qkv[:, at : at + HEAD_SIZE]
        at = at + groups * HEAD_SIZE
        values_t = qkv[:, at : at + HEAD_SIZE].astype(F32).T.astype(BF)
        wait_group(qkv, in_sems, 1, group)
        for index in range(GROUP_HEADS):
            columns = head_columns(group * GROUP_HEADS + index)
            scores[:, index * tokens : (index + 1) * tokens] = dot_nt(keys, qkv[:, columns])

        def block(queries, lanes, reach):
            weights[:reach, lanes] = weights_of(
                scores[:reach, lanes], bias[:reach, queries]
            ).astype(BF)

        softmax_blocks(tokens, block)
        for index in range(GROUP_HEADS):
            columns = head_columns(group * GROUP_HEADS + index)
            mixed = dot_nn(values_t, weights[:, index * tokens : (index + 1) * tokens])
            attended[:, columns] = mixed.T.astype(BF)
    count, width, _ = chunks.shape
    out = dot_nn(attended[:, :width], landed(chunks, sems, 0)[...])
    for index in range(1, count):
        columns = slice(index * width, (index + 1) * width)
        out = out + dot_nn(attended[:, columns], landed(chunks, sems, index)[...])
    out_ref[...] = out.astype(BF)


def backward_kernel(
    seq_ref, qkv_ref, grads_ref, wq0_ref, wq1_ref, wkv0_ref, wkv1_ref, out_ref,
    qkv, grads, chunks, bias, scores, weight_grads, weights, score_grads, scaled_q, scaled_kv,
    sems, in_sems,
):
    tokens, q_cols = grads.shape
    groups = q_cols // (GROUP_HEADS * HEAD_SIZE)
    pltpu.make_async_copy(qkv_ref.at[:, q_cols:], qkv.at[:, q_cols:], in_sems.at[0]).start()
    start_group(qkv_ref, qkv, in_sems, 1, 0)
    start_group(grads_ref, grads, in_sems, 1 + groups, 0)
    fill_bias(seq_ref, bias)
    clear_unreached(weights, tokens)
    clear_unreached(score_grads, tokens)
    kv_cols = groups * HEAD_SIZE
    pltpu.make_async_copy(qkv.at[:, q_cols:], qkv.at[:, q_cols:], in_sems.at[0]).wait()
    wait_group(qkv, in_sems, 1, 0)
    wait_group(grads, in_sems, 1 + groups, 0)
    for group in range(1, groups):
        start_group(qkv_ref, qkv, in_sems, 1, group)
        start_group(grads_ref, grads, in_sems, 1 + groups, group)
    by_section(
        lambda: start_joined([wq0_ref], wkv0_ref, chunks, sems),
        lambda: start_joined([wq1_ref], wkv1_ref, chunks, sems),
    )
    scale_lanes = qkv[:, q_cols + 2 * kv_cols :].astype(F32)
    scale_column = jnp.sum(scale_lanes, axis=1, keepdims=True)
    scale_row = jnp.sum(scale_lanes.T, axis=0, keepdims=True) * SOFT
    for group in range(groups):
        at = q_cols + group * HEAD_SIZE
        keys = qkv[:, at : at + HEAD_SIZE]
        keys_t = keys.astype(F32).T.astype(BF)
        at = at + kv_cols
        values = qkv[:, at : at + HEAD_SIZE]
        if group > 0:
            wait_group(qkv, in_sems, 1, group)
            wait_group(grads, in_sems, 1 + groups, group)
        for index in range(GROUP_HEADS):
            columns = head_columns(group * GROUP_HEADS + index)
            lanes = slice(index * tokens, (index + 1) * tokens)
            scores[:, lanes] = dot_nt(keys, qkv[:, columns])
            weight_grads[:, lanes] = dot_nt(values, grads[:, columns])
        def block(queries, lanes, reach):
            weight = weights_of(scores[:reach, lanes], bias[:reach, queries])
            weights[:reach, lanes] = weight.astype(BF)
            weight_grad = weight_grads[:reach, lanes]
            mean = jnp.sum(weight_grad * weight, axis=0, keepdims=True)
            score_grads[:reach, lanes] = (weight * (weight_grad - mean)).astype(BF)

        softmax_blocks(tokens, block)
        key_grad = jnp.zeros((tokens, HEAD_SIZE), F32)
        value_grad = jnp.zeros((tokens, HEAD_SIZE), F32)
        for index in range(GROUP_HEADS):
            columns = head_columns(group * GROUP_HEADS + index)
            lanes = slice(index * tokens, (index + 1) * tokens)
            score_grad = score_grads[:, lanes]
            scaled_q[columns, :] = (dot_nn(keys_t, score_grad) * scale_row).astype(BF)
            key_grad = key_grad + dot_nn(score_grad, qkv[:, columns])
            value_grad = value_grad + dot_nn(weights[:, lanes], grads[:, columns])
        at = group * HEAD_SIZE
        scaled_kv[:, at : at + HEAD_SIZE] = (key_grad * (scale_column * SOFT)).astype(BF)
        at = at + kv_cols
        scaled_kv[:, at : at + HEAD_SIZE] = (value_grad * scale_column).astype(BF)
    count, width, _ = chunks.shape
    through = dot_nt(landed(chunks, sems, count - 1)[...], scaled_kv[...])
    for index in range(count - 1):
        rows = slice(index * width, (index + 1) * width)
        through = through + dot_nn(landed(chunks, sems, index)[...], scaled_q[rows, :])
    out_ref[...] = through.T.astype(BF)


def merger_kernel(
    marks_ref, owners_ref, last_ref, pair_ref, across_ref, beside_ref, g0_ref, g1_ref, weight_ref,
    out_ref, grad_ref, rows, hidden, counts, places,
):
    added = summed(pair_ref, across_ref, beside_ref)
    rows[...] = last_ref[...].astype(F32) + chosen(g0_ref, g1_ref) * added
    share = grad_ref.shape[0]
    at = pl.multiple_of(lax.axis_index("mp") * share, share)
    grad_ref[...] = rows[pl.ds(at, share), :].astype(BF)
    x = rows[...].astype(BF)
    cols = weight_ref.shape[0]
    for start in range(0, cols, 256):
        hidden[:, start : start + 256] = dot_nt(x, weight_ref[start : start + 256, :])
    dp_count, sections = out_ref.shape[:2]
    owner_count = dp_count * sections

    def clear(owner, carry):
        counts[owner] = 0
        for slot in range(CAP):
            places[owner * CAP + slot] = -1
        return carry

    lax.fori_loop(0, owner_count, clear, 0, unroll=8)

    def place(block, carry):
        owner = owners_ref[0, block]

        @pl.when(marks_ref[0, block] == 1)
        def _():
            slot = counts[owner]
            places[owner * CAP + slot] = block
            counts[owner] = slot + 1

        return carry

    lax.fori_loop(0, marks_ref.shape[1], place, 0, unroll=4)

    def send(owner, carry):
        pieces = []
        for slot in range(CAP):
            block = places[owner * CAP + slot]
            at = pl.multiple_of(jnp.maximum(block, 0) * VB, VB)
            pieces.append(jnp.where(block >= 0, hidden[pl.ds(at, VB), :], 0.0))
        out_ref[lax.rem(owner, dp_count), lax.div(owner, dp_count)] = jnp.concatenate(
            pieces, axis=0
        ).astype(BF)
        return carry

    lax.fori_loop(0, owner_count, send, 0, unroll=4)


def merger_sum_kernel(parts_ref, own_ref, other_ref):
    section = lax.axis_index("section")
    sources = parts_ref.shape[0]

    def total(index):
        return add_parts(lambda source: parts_ref[source, index], sources)

    first, second = total(0), total(1)
    own_ref[...] = jnp.where(section == 0, first, second)
    other_ref[...] = jnp.where(section == 0, second, first).astype(BF)


def gelu_slope(values):
    cumulative = 0.5 * (1.0 + lax.erf(values * (1.0 / math.sqrt(2.0))))
    return cumulative + values * jnp.exp(-0.5 * values * values) * (1.0 / math.sqrt(2.0 * math.pi))


def local(
    embeds,
    cotangent,
    norm_gain,
    w_query,
    w_keyval,
    w_out,
    seq_lengths,
    image_mask,
    block_owner,
    merger_weight,
    merger_pre,
):
    section = lax.axis_index("section")
    mp_count = lax.axis_size("mp")
    dp_count = lax.axis_size("dp")
    rows, width = embeds.shape[1:]
    tokens = rows * mp_count
    share = tokens // dp_count
    q_cols = w_query.shape[3]
    kv_cols = w_keyval.shape[4]
    joined = q_cols + 2 * kv_cols + 128
    emb, cot = embeds[0], cotangent[0]
    wq, wout = w_query[0, 0], w_out[0, 0]
    wkv = w_keyval[0, 0].reshape(width, 2 * kv_cols)
    gain = norm_gain[0]

    def partner(index):
        other, rank = 1 - index // mp_count, (index % mp_count + mp_count // 2) % mp_count
        return other * mp_count + rank

    everyone = range(2 * mp_count)
    from_first = [(i, partner(i)) for i in everyone if i < mp_count]
    from_second = [(i, partner(i)) for i in everyone if i >= mp_count]

    def swap(array, pairs):
        return lax.ppermute(array, ("section", "mp"), pairs)

    def scatter(array, axis):
        return lax.all_to_all(array, axis, split_axis=0, concat_axis=0, tiled=True)

    def spread(copies):
        return scatter(copies, "dp").reshape(tokens, copies.shape[2])

    def gather(array, axis):
        return lax.all_gather(array, axis, axis=0, tiled=True)

    def chunks_of(count):
        return pltpu.VMEM((count, width, width), BF)

    own_x, other_x = jnp.where(section == 0, emb, cot), jnp.where(section == 0, cot, emb)
    received_x = swap(other_x, from_first + from_second)
    gain_x = swap(gain, from_first + from_second)
    def vmem(*shape):
        return pltpu.VMEM(shape, BF)

    def dma(count):
        return pltpu.SemaphoreType.DMA((count,))

    def other_rows_parts(x):
        return pl.pallas_call(
            first_kernel,
            out_shape=pltpu.HBM((dp_count, share, joined), BF),
            in_specs=[VMEM] * 2 + [HBM] * 3,
            out_specs=HBM,
            scratch_shapes=[chunks_of(5), vmem(dp_count, share, joined), dma(5), dma(6)],
            compiler_params=params(24),
            cost_estimate=cost(2 * tokens * width * joined, 6 << 20),
        )(x, gain, *in_hbm(wq, wkv, wout))

    def first_sum(parts):
        return pl.pallas_call(
            first_sum_kernel,
            out_shape=shape_of((share, joined), BF),
            in_specs=[ANY],
            out_specs=VMEM,
            scratch_shapes=[vmem(dp_count, share, joined), dma(6)],
            compiler_params=params(24),
            cost_estimate=cost(parts.size, 2 << 20),
        )(parts)

    def summed_copies(adder, parts):
        cols = parts.shape[2]
        return pl.pallas_call(
            functools.partial(sum_kernel, adder),
            out_shape=pltpu.HBM((dp_count, share, cols), BF),
            in_specs=[ANY],
            out_specs=HBM,
            scratch_shapes=[vmem(dp_count, share, cols), vmem(share, cols), dma(6), dma(dp_count)],
            compiler_params=params(24),
            cost_estimate=cost(parts.size, 4 << 20),
        )(parts)

    def chosen_copies(first, second, cols):
        return pl.pallas_call(
            choose_kernel,
            out_shape=pltpu.HBM((dp_count, share, cols), BF),
            in_specs=[VMEM] * 2,
            out_specs=HBM,
            scratch_shapes=[dma(dp_count)],
            compiler_params=params(24),
            cost_estimate=cost(0, 2 << 20),
        )(first, second)

    def loaded(joins, firsts, seconds):
        count = 5 if joins else 4
        return pl.pallas_call(
            functools.partial(load_kernel, joins, len(firsts)),
            out_shape=pltpu.VMEM((count, width, width), BF),
            in_specs=[HBM] * (len(firsts) + len(seconds)),
            out_specs=VMEM,
            scratch_shapes=[dma(count)],
            compiler_params=params(16),
            cost_estimate=cost(0, 5 << 20),
        )(*in_hbm(*firsts, *seconds))

    def beside(array, distance):
        return lax.ppermute(array, "mp", [(i, i ^ distance) for i in range(mp_count)])

    def sum_over_mp(part, *later):
        mate = beside(part, 1)
        at = lax.axis_index("mp") % 2 * (tokens // 2)

        def half(array):
            return lax.dynamic_slice_in_dim(array, at, tokens // 2).astype(F32)

        pair_half = (half(part) + half(mate)).astype(BF)
        across = beside(pair_half, 2)
        pair_half, part, mate, *later = lax.optimization_barrier((pair_half, part, mate, *later))
        pair = (part.astype(F32) + mate.astype(F32)).astype(BF)
        return (pair, across, beside(across, 1)), later

    others = [beside(own_x, distance) for distance in (1, 2, 3)]
    first_chunks = pl.pallas_call(
        first_load_kernel,
        out_shape=pltpu.VMEM((5, width, width), BF),
        in_specs=[HBM] * 3,
        out_specs=VMEM,
        scratch_shapes=[dma(5)],
        compiler_params=params(16),
        cost_estimate=cost(0, 5 << 20),
    )(*in_hbm(wq, wkv, wout))
    own_parts, own_all = pl.pallas_call(
        first_own_kernel,
        out_shape=[pltpu.HBM((dp_count, share, joined), BF), shape_of((tokens, width), BF)],
        in_specs=[VMEM] * 6,
        out_specs=[HBM, VMEM],
        scratch_shapes=[
            pltpu.VMEM((tokens, width), F32),
            vmem(dp_count, share, joined),
            dma(6),
        ],
        compiler_params=params(24),
        cost_estimate=cost(2 * tokens * width * joined, 6 << 20),
    )(own_x, *others, gain, first_chunks)
    own_parts, received_x, gain_x, wq_s, wout_s = lax.optimization_barrier(
        (own_parts, received_x, gain_x, wq, wout)
    )
    own_parts = scatter(own_parts, "dp")
    wq_b = swap(wq_s, from_second)
    cuts = (5 * q_cols // 16, 5 * q_cols // 8)
    wout_a0 = swap(wout_s[: cuts[0]], from_first)
    wout_a1, wout_a2 = wout_s[cuts[0] : cuts[1]], wout_s[cuts[1] :]
    other_parts = other_rows_parts(gather(received_x, "mp"))
    own_parts, other_parts, wout_a0, wout_a1, wout_a2 = lax.optimization_barrier(
        (own_parts, other_parts, wout_a0, wout_a1, wout_a2)
    )
    wout_a1 = swap(wout_a1, from_first)
    own = first_sum(own_parts)
    mine_all = gather(other_x, "mp")
    other_parts, own, mine_all = lax.optimization_barrier(
        (scatter(other_parts, "dp"), own, mine_all)
    )
    other = first_sum(other_parts)
    received = swap(other, from_first)
    received_grad, wkv_s = lax.optimization_barrier((swap(other, from_second), wkv))
    wkv_b = swap(wkv_s, from_second)
    copies, wout_a1, wout_a2 = lax.optimization_barrier(
        (chosen_copies(own, received, joined), wout_a1, wout_a2)
    )
    wout_a2 = swap(wout_a2, from_first)
    grad_copies = chosen_copies(received_grad, own, q_cols)
    qkv_first, grad_copies, wq_b, wq_s, wkv_s = lax.optimization_barrier(
        (spread(copies), grad_copies, wq_b, wq, wkv)
    )
    wout_a = (wout_a0, wout_a1, wout_a2)
    wq_a, wkv_a = swap(wq_s, from_first), swap(wkv_s, from_first)
    head_grad_last = spread(grad_copies)

    def layer_forward(qkv, wouts):
        out = pl.pallas_call(
            forward_kernel,
            out_shape=shape_of((tokens, width), BF),
            in_specs=[SMEM, ANY] + [HBM] * (1 + len(wouts[1])),
            out_specs=VMEM,
            scratch_shapes=[
                vmem(tokens, joined),
                chunks_of(4),
                pltpu.VMEM((tokens, tokens), F32),
                pltpu.VMEM((tokens, GROUP_HEADS * tokens), F32),
                vmem(tokens, GROUP_HEADS * tokens),
                vmem(tokens, q_cols),
                dma(4),
                dma(3),
            ],
            compiler_params=params(32),
            cost_estimate=cost(6 * tokens * tokens * q_cols, 4 << 20),
        )(seq_lengths, qkv, *in_hbm(wouts[0], *wouts[1]))
        return out

    def rows_after(resident, sums):
        even = lax.axis_index("mp") % 2 == 0
        lower, upper = jnp.where(even, *sums[1:]), jnp.where(even, *sums[:0:-1])
        added = sums[0].astype(F32) + jnp.concatenate([lower, upper], axis=0).astype(F32)
        return (resident.astype(F32) + added).astype(BF)

    out, wkv_b = lax.optimization_barrier((layer_forward(qkv_first, (wout, wout_a)), wkv_b))
    sums, pieces = sum_over_mp(out, wq_b, wkv_b, wq, wkv)
    joined_last = loaded(True, pieces[:2], pieces[2:])
    parts = pl.pallas_call(
        project_kernel,
        out_shape=pltpu.HBM((dp_count, share, joined), BF),
        in_specs=[VMEM] * 8,
        out_specs=HBM,
        scratch_shapes=[vmem(dp_count, share, joined), dma(6)],
        compiler_params=params(24),
        cost_estimate=cost(2 * tokens * width * joined, 6 << 20),
    )(own_all, mine_all, *sums, gain_x, gain, joined_last)
    parts, head_grad_last = lax.optimization_barrier((parts, head_grad_last))
    qkv_last = spread(summed_copies(scaled_sum, scatter(parts, "dp")))
    wout_b = swap(wout, from_second)
    wout_last = jnp.where(section == 0, wout_b, wout)
    h_one = rows_after(jnp.where(section == 0, own_all, mine_all), sums)
    rows_after(h_one, sum_over_mp(layer_forward(qkv_last, (wout_last, (wout_last,))))[0])

    def layer_backward(qkv, head_grads, wqs, wkvs, later=()):
        through = pl.pallas_call(
            backward_kernel,
            out_shape=shape_of((tokens, width), BF),
            in_specs=[SMEM, ANY, ANY] + [HBM] * 4,
            out_specs=VMEM,
            scratch_shapes=[
                vmem(tokens, joined),
                vmem(tokens, q_cols),
                chunks_of(5),
                pltpu.VMEM((tokens, tokens), F32),
                pltpu.VMEM((tokens, GROUP_HEADS * tokens), F32),
                pltpu.VMEM((tokens, GROUP_HEADS * tokens), F32),
                vmem(tokens, GROUP_HEADS * tokens),
                vmem(tokens, GROUP_HEADS * tokens),
                vmem(q_cols, tokens),
                vmem(tokens, 2 * kv_cols),
                dma(5),
                dma(5),
            ],
            compiler_params=params(32),
            cost_estimate=cost(12 * tokens * tokens * q_cols, 6 << 20),
        )(seq_lengths, qkv, head_grads, *in_hbm(*wqs, *wkvs))
        return sum_over_mp(through, *later)

    sums, pieces = layer_backward(
        qkv_last,
        *in_hbm(head_grad_last),
        (wq_b, wq),
        (wkv_b, wkv),
        later=(wout, *wout_a),
    )
    parts, grad_one = pl.pallas_call(
        head_grad_kernel,
        out_shape=[pltpu.HBM((dp_count, share, q_cols), BF), shape_of((tokens, width), BF)],
        in_specs=[VMEM] * 8,
        out_specs=[HBM, VMEM],
        scratch_shapes=[vmem(dp_count, share, q_cols), dma(4)],
        compiler_params=params(24),
        cost_estimate=cost(2 * tokens * width * q_cols, 4 << 20),
    )(mine_all, own_all, *sums, gain_x, gain, loaded(False, pieces[:1], pieces[1:]))
    parts, wq_a, wkv_a = lax.optimization_barrier((scatter(parts, "dp"), wq_a, wkv_a))
    head_grad_first = spread(summed_copies(plain_sum, parts))
    sums, _ = layer_backward(qkv_first, head_grad_first, (wq, wq_a), (wkv, wkv_a))

    hidden_cols = merger_weight.shape[0]
    outgoing, input_grad = pl.pallas_call(
        merger_kernel,
        out_shape=[
            shape_of((dp_count, 2, CAP * VB, hidden_cols), BF),
            shape_of((rows, width), BF),
        ],
        in_specs=[SMEM, SMEM] + [VMEM] * 7,
        out_specs=[VMEM] * 2,
        scratch_shapes=[
            pltpu.VMEM((tokens, width), F32),
            pltpu.VMEM((tokens, hidden_cols), F32),
            pltpu.SMEM((2 * dp_count,), jnp.int32),
            pltpu.SMEM((2 * dp_count * CAP,), jnp.int32),
        ],
        compiler_params=params(24),
    )(image_mask, block_owner, grad_one, *sums, gain, gain_x, merger_weight)
    kept, passed = pl.pallas_call(
        merger_sum_kernel,
        out_shape=[
            shape_of((CAP * VB, hidden_cols), F32),
            shape_of((CAP * VB, hidden_cols), BF),
        ],
        in_specs=[VMEM],
        out_specs=[VMEM] * 2,
        compiler_params=params(24),
    )(scatter(outgoing, "dp"))
    crossed = lax.ppermute(passed, "section", [(0, 1), (1, 0)]).astype(F32)
    first = jnp.where(section == 0, kept, crossed)
    second = jnp.where(section == 0, crossed, kept)
    hidden_grad = jnp.stack([first, second]).reshape(2, CAP, VB, hidden_cols)
    merger_grad = gelu_slope(merger_pre[0].astype(F32)) * hidden_grad
    return (input_grad[None], merger_grad[None])


def solution(mesh):
    placed = (
        P("section", "mp", "dp"),
        P("section", "mp", "dp"),
        P(None, "section", "dp"),
        P(None, "section", "dp", "mp"),
        P(None, "section", "dp", None, "mp"),
        P(None, "section", "mp", "dp"),
        P(),
        P("section", None),
        P("section", None),
        P("mp", "dp"),
        P(("section", "dp"), None, None, None, "mp"),
    )
    return jax.shard_map(
        local,
        mesh=mesh,
        in_specs=placed,
        out_specs=(P("section", "mp", "dp"), P(("section", "dp"), None, None, None, "mp")),
        check_vma=False,
    )
```

```python
import functools
import math

import jax
import jax.numpy as jnp
from jax import lax
from jax.experimental import pallas as pl
from jax.experimental.pallas import tpu as pltpu
from jax.sharding import PartitionSpec as P

MODEL_WIDTH = 8192
HEAD_SIZE = 128
GROUP_HEADS = 8
CAP = 2
VB = 8
NSEQ = 3

EPSILON = 1e-06
MASKED = -1e30
SOFT = 1.0 / math.sqrt(HEAD_SIZE)
LOG2E = math.log2(math.e)
QB = 128

BF = jnp.bfloat16
F32 = jnp.float32

VMEM = pl.BlockSpec(memory_space=pltpu.VMEM)
SMEM = pl.BlockSpec(memory_space=pltpu.SMEM)
ANY = pl.BlockSpec(memory_space=pl.ANY)
HBM = pl.BlockSpec(memory_space=pltpu.HBM)


def shape_of(shape, dtype):
    return jax.ShapeDtypeStruct(shape, dtype)


def in_hbm(*arrays):
    return [pltpu.with_memory_space_constraint(array, pltpu.HBM) for array in arrays]


def params(mebibytes):
    return pltpu.CompilerParams(vmem_limit_bytes=mebibytes << 20)


def cost(flops, bytes_accessed):
    return pl.CostEstimate(flops=flops, bytes_accessed=bytes_accessed, transcendentals=0)


def dot_nn(left, right):
    return jnp.dot(left, right, preferred_element_type=F32)


def dot_nt(left, right):
    return lax.dot_general(left, right, (((1,), (1,)), ((), ())), preferred_element_type=F32)


def two_lanes(column):
    high = column.astype(BF).astype(F32)
    lane = lax.broadcasted_iota(jnp.int32, (column.shape[0], 128), 1)
    return jnp.where(lane == 0, high, jnp.where(lane == 1, column - high, 0.0)).astype(BF)


def start_columns(sources, chunks, sems):
    width, index = chunks.shape[2], 0
    for source in sources:
        for start in range(0, source.shape[1], width):
            block = source.at[:, start : start + width]
            pltpu.make_async_copy(block, chunks.at[index], sems.at[index]).start()
            index += 1


def start_rows(sources, chunks, sems):
    rows, at = chunks.shape[1], 0
    for source in sources:
        start = 0
        while start < source.shape[0]:
            index, within = at // rows, at % rows
            count = min(rows - within, source.shape[0] - start)
            block = source.at[start : start + count, :]
            place = chunks.at[index, within : within + count, :]
            pltpu.make_async_copy(block, place, sems.at[index]).start()
            start, at = start + count, at + count


def start_joined(wqs, wkv_ref, chunks, sems):
    start_columns(wqs, chunks, sems)
    last = chunks.shape[0] - 1
    pltpu.make_async_copy(wkv_ref, chunks.at[last], sems.at[last]).start()


def landed(chunks, sems, index):
    pltpu.make_async_copy(chunks.at[index], chunks.at[index], sems.at[index]).wait()
    return chunks.at[index]


def by_section(first, second):
    section = lax.axis_index("section")
    pl.when(section == 0)(first)
    pl.when(section != 0)(second)


def spans(cols):
    return [slice(start, min(start + 512, cols)) for start in range(0, cols, 512)]


def start_spans(source, target, sems):
    for index, span in enumerate(spans(target.shape[-1])):
        at = (slice(None),) * (len(target.shape) - 1) + (span,)
        pltpu.make_async_copy(source.at[at], target.at[at], sems.at[index]).start()


def wait_span(target, sems, index):
    at = (slice(None),) * (len(target.shape) - 1) + (spans(target.shape[-1])[index],)
    pltpu.make_async_copy(target.at[at], target.at[at], sems.at[index]).wait()


def sender(staged, out_ref, sems):
    owners, share, cols = staged.shape

    def put(start, tile):
        span = slice(start, start + tile.shape[1])
        staged[:, :, span] = tile.reshape(owners, share, tile.shape[1])
        index = spans(cols).index(span)
        at = (slice(None), slice(None), span)
        pltpu.make_async_copy(staged.at[at], out_ref.at[at], sems.at[index]).start()

    def finish():
        for index in range(len(spans(cols))):
            wait_span(staged, sems, index)

    return put, finish


def repeat_out(tile, out_ref, sems):
    for place in range(out_ref.shape[0]):
        pltpu.make_async_copy(tile, out_ref.at[place], sems.at[place]).start()


def repeat_wait(tile, out_ref, sems):
    for place in range(out_ref.shape[0]):
        pltpu.make_async_copy(tile, out_ref.at[place], sems.at[place]).wait()


def project_rows(rows, gain, chunks, chunk_at, put):
    rows_f = rows.astype(F32)
    normed = (rows_f * gain).astype(BF)
    count, _, width = chunks.shape
    put(count * width, two_lanes(jnp.sum(rows_f * rows_f, axis=1, keepdims=True)))
    for index in range(count):
        put(index * width, dot_nn(normed, chunk_at(index)[...]).astype(BF))


def load_kernel(joined, pieces, *refs):
    *sources, out_ref, sems = refs

    def load(refs):
        if joined:
            start_joined(refs[:-1], refs[-1], out_ref, sems)
        else:
            start_rows(refs, out_ref, sems)

    by_section(lambda: load(sources[:pieces]), lambda: load(sources[pieces:]))
    for index in range(out_ref.shape[0]):
        landed(out_ref, sems, index)


def first_kernel(
    x_ref, gain_ref, wq_ref, wkv_ref, wout_ref, out_ref, chunks, staged, sems, out_sems
):
    put, finish = sender(staged, out_ref, out_sems)
    tokens = x_ref.shape[0]

    def rows():
        return jnp.concatenate([x_ref[tokens // 2 :, :], x_ref[: tokens // 2, :]], axis=0)

    def first():
        start_joined([wq_ref], wkv_ref, chunks, sems)
        project_rows(rows(), gain_ref[...], chunks, lambda at: landed(chunks, sems, at), put)

    def second():
        start_rows([wout_ref], chunks, sems)
        count, width, _ = chunks.shape
        put(count * width, jnp.zeros((tokens, 128), BF))
        put((count - 1) * width, jnp.zeros((tokens, width), BF))
        x = rows()
        for index in range(count - 1):
            put(index * width, dot_nt(x, landed(chunks, sems, index)[...]).astype(BF))

    by_section(first, second)
    finish()


def first_load_kernel(wq_ref, wkv_ref, wout_ref, out_ref, sems):
    def wait(count):
        for index in range(count):
            landed(out_ref, sems, index)

    def first():
        start_joined([wq_ref], wkv_ref, out_ref, sems)
        wait(out_ref.shape[0])

    def second():
        start_rows([wout_ref], out_ref, sems)
        wait(out_ref.shape[0] - 1)

    by_section(first, second)


def first_own_kernel(
    mine_ref, near_ref, far_ref, cross_ref, gain_ref, chunks, out_ref, x_ref, x, staged, out_sems
):
    rank = lax.axis_index("mp")
    share = mine_ref.shape[0]
    for distance, ref in enumerate((mine_ref, near_ref, far_ref, cross_ref)):
        at = pl.multiple_of(jnp.bitwise_xor(rank, distance) * share, share)
        x[pl.ds(at, share), :] = ref[...].astype(F32)
    x_ref[...] = x[...].astype(BF)
    put, finish = sender(staged, out_ref, out_sems)
    tokens = x_ref.shape[0]
    count, width, _ = chunks.shape

    def first():
        project_rows(x_ref[...], gain_ref[...], chunks, lambda at: chunks.at[at], put)

    def second():
        put(count * width, jnp.zeros((tokens, 128), BF))
        put((count - 1) * width, jnp.zeros((tokens, width), BF))
        for index in range(count - 1):
            put(index * width, dot_nt(x_ref[...], chunks[index]).astype(BF))

    by_section(first, second)
    finish()


def chosen(first_ref, second_ref):
    return jnp.where(lax.axis_index("section") == 0, first_ref[...], second_ref[...])


def summed(pair_ref, across_ref, beside_ref):
    even = lax.axis_index("mp") % 2 == 0
    lower = jnp.where(even, across_ref[...], beside_ref[...])
    upper = jnp.where(even, beside_ref[...], across_ref[...])
    return pair_ref[...].astype(F32) + jnp.concatenate([lower, upper], axis=0).astype(F32)


def project_kernel(
    r0_ref, r1_ref, pair_ref, across_ref, beside_ref, g0_ref, g1_ref, chunks, out_ref,
    staged, out_sems,
):
    added = summed(pair_ref, across_ref, beside_ref)
    rows = (chosen(r0_ref, r1_ref).astype(F32) + added).astype(BF)
    put, finish = sender(staged, out_ref, out_sems)
    project_rows(rows, chosen(g0_ref, g1_ref), chunks, lambda at: chunks.at[at], put)
    finish()


def head_grad_kernel(
    r0_ref, r1_ref, pair_ref, across_ref, beside_ref, g0_ref, g1_ref, chunks, out_ref, rows_ref,
    staged, out_sems,
):
    added = summed(pair_ref, across_ref, beside_ref)
    rows = chosen(r0_ref, r1_ref).astype(F32) + chosen(g0_ref, g1_ref) * added
    rows_ref[...] = rows.astype(BF)
    count, width, _ = chunks.shape
    put, finish = sender(staged, out_ref, out_sems)
    for index in range(count):
        put(index * width, dot_nt(rows_ref[...], chunks[index]).astype(BF))
    finish()


def add_parts(load, count):
    total = load(0).astype(F32)
    for index in range(1, count):
        total = total + load(index).astype(F32)
    return total


def part_sums(parts, sems):
    def total(index):
        wait_span(parts, sems, index)
        span = spans(parts.shape[2])[index]
        return add_parts(lambda source: parts[source, :, span], parts.shape[0])

    return total


def scaled_sum(total, tile):
    ranges = spans(tile.shape[1])
    squares = jnp.sum(total(len(ranges) - 1), axis=1, keepdims=True)
    scale = lax.rsqrt(squares / MODEL_WIDTH + EPSILON)
    for index, span in enumerate(ranges[:-1]):
        tile[:, span] = (total(index) * scale).astype(BF)
    tile[:, ranges[-1]] = two_lanes(scale)


def plain_sum(total, tile):
    for index, span in enumerate(spans(tile.shape[1])):
        tile[:, span] = total(index).astype(BF)


def first_sum_kernel(parts_ref, out_ref, parts, sems):
    start_spans(parts_ref, parts, sems)
    total = part_sums(parts, sems)
    by_section(lambda: scaled_sum(total, out_ref), lambda: plain_sum(total, out_ref))


def sum_kernel(adder, parts_ref, out_ref, parts, tile, sems, out_sems):
    start_spans(parts_ref, parts, sems)
    adder(part_sums(parts, sems), tile)
    repeat_out(tile, out_ref, out_sems)
    repeat_wait(tile, out_ref, out_sems)


def choose_kernel(first_ref, second_ref, out_ref, sems):
    first = first_ref.at[:, : out_ref.shape[2]]
    second = second_ref.at[:, : out_ref.shape[2]]
    by_section(
        lambda: repeat_out(first, out_ref, sems), lambda: repeat_out(second, out_ref, sems)
    )
    repeat_wait(first, out_ref, sems)


def fill_bias(seq_ref, bias):
    section = lax.axis_index("section")
    tokens = bias.shape[0]
    keys = lax.broadcasted_iota(jnp.int32, (tokens, tokens), 0)
    queries = lax.broadcasted_iota(jnp.int32, (tokens, tokens), 1)
    key_segment = jnp.zeros((tokens, tokens), jnp.int32)
    query_segment = jnp.zeros((tokens, tokens), jnp.int32)
    bound = 0
    for index in range(NSEQ):
        bound = bound + seq_ref[section, index]
        key_segment = key_segment + (keys >= bound).astype(jnp.int32)
        query_segment = query_segment + (queries >= bound).astype(jnp.int32)
    allowed = (keys <= queries) & (key_segment == query_segment)
    bias[...] = jnp.where(allowed, 0.0, MASKED)


def head_columns(head):
    return slice(head * HEAD_SIZE, (head + 1) * HEAD_SIZE)


def softmax_blocks(tokens, body):
    def one_head(head, carry):
        for at in range(0, tokens, QB):
            lanes = pl.ds(pl.multiple_of(head * tokens + at, QB), QB)
            body(slice(at, at + QB), lanes, at + QB)
        return carry

    lax.fori_loop(0, GROUP_HEADS, one_head, 0, unroll=4)


def clear_unreached(target, tokens):
    for head in range(GROUP_HEADS):
        for at in range(0, tokens - QB, QB):
            lanes = slice(head * tokens + at, head * tokens + at + QB)
            target[at + QB :, lanes] = jnp.zeros((tokens - at - QB, QB), target.dtype)


def weights_of(scores, bias):
    scores = scores * (SOFT * LOG2E) + bias
    raised = jnp.exp2(scores - jnp.max(scores, axis=0, keepdims=True))
    return raised * (1.0 / jnp.sum(raised, axis=0, keepdims=True))


def start_qkv(qkv_ref, qkv, q_cols, sems):
    pltpu.make_async_copy(qkv_ref.at[:, q_cols:], qkv.at[:, q_cols:], sems.at[0]).start()
    for group in range(q_cols // (GROUP_HEADS * HEAD_SIZE)):
        start_group(qkv_ref, qkv, sems, 1, group)


def start_group(source, target, sems, first, group):
    width = GROUP_HEADS * HEAD_SIZE
    at = (slice(None), slice(group * width, (group + 1) * width))
    pltpu.make_async_copy(source.at[at], target.at[at], sems.at[first + group]).start()


def wait_group(target, sems, first, group):
    width = GROUP_HEADS * HEAD_SIZE
    at = (slice(None), slice(group * width, (group + 1) * width))
    pltpu.make_async_copy(target.at[at], target.at[at], sems.at[first + group]).wait()


def forward_kernel(seq_ref, qkv_ref, wout0_ref, *refs):
    *wout1_refs, out_ref, qkv, chunks, bias, scores, weights, attended, sems, in_sems = refs
    tokens, q_cols = attended.shape
    start_qkv(qkv_ref, qkv, q_cols, in_sems)
    by_section(
        lambda: start_rows([wout0_ref], chunks, sems),
        lambda: start_rows(wout1_refs, chunks, sems),
    )
    fill_bias(seq_ref, bias)
    clear_unreached(weights, tokens)
    groups = q_cols // (GROUP_HEADS * HEAD_SIZE)
    pltpu.make_async_copy(qkv.at[:, q_cols:], qkv.at[:, q_cols:], in_sems.at[0]).wait()
    for group in range(groups):
        at = q_cols + group * HEAD_SIZE
        keys = qkv[:, at : at + HEAD_SIZE]
        at = at + groups * HEAD_SIZE
        values_t = qkv[:, at : at + HEAD_SIZE].astype(F32).T.astype(BF)
        wait_group(qkv, in_sems, 1, group)
        for index in range(GROUP_HEADS):
            columns = head_columns(group * GROUP_HEADS + index)
            scores[:, index * tokens : (index + 1) * tokens] = dot_nt(keys, qkv[:, columns])

        def block(queries, lanes, reach):
            weights[:reach, lanes] = weights_of(
                scores[:reach, lanes], bias[:reach, queries]
            ).astype(BF)

        softmax_blocks(tokens, block)
        for index in range(GROUP_HEADS):
            columns = head_columns(group * GROUP_HEADS + index)
            mixed = dot_nn(values_t, weights[:, index * tokens : (index + 1) * tokens])
            attended[:, columns] = mixed.T.astype(BF)
    count, width, _ = chunks.shape
    out = dot_nn(attended[:, :width], landed(chunks, sems, 0)[...])
    for index in range(1, count):
        columns = slice(index * width, (index + 1) * width)
        out = out + dot_nn(attended[:, columns], landed(chunks, sems, index)[...])
    out_ref[...] = out.astype(BF)


def backward_kernel(
    seq_ref, qkv_ref, grads_ref, wq0_ref, wq1_ref, wkv0_ref, wkv1_ref, out_ref,
    qkv, grads, chunks, bias, scores, weight_grads, weights, score_grads, scaled_q, scaled_kv,
    sems, in_sems,
):
    tokens, q_cols = grads.shape
    groups = q_cols // (GROUP_HEADS * HEAD_SIZE)
    pltpu.make_async_copy(qkv_ref.at[:, q_cols:], qkv.at[:, q_cols:], in_sems.at[0]).start()
    start_group(qkv_ref, qkv, in_sems, 1, 0)
    start_group(grads_ref, grads, in_sems, 1 + groups, 0)
    fill_bias(seq_ref, bias)
    clear_unreached(weights, tokens)
    clear_unreached(score_grads, tokens)
    kv_cols = groups * HEAD_SIZE
    pltpu.make_async_copy(qkv.at[:, q_cols:], qkv.at[:, q_cols:], in_sems.at[0]).wait()
    wait_group(qkv, in_sems, 1, 0)
    wait_group(grads, in_sems, 1 + groups, 0)
    for group in range(1, groups):
        start_group(qkv_ref, qkv, in_sems, 1, group)
        start_group(grads_ref, grads, in_sems, 1 + groups, group)
    by_section(
        lambda: start_joined([wq0_ref], wkv0_ref, chunks, sems),
        lambda: start_joined([wq1_ref], wkv1_ref, chunks, sems),
    )
    scale_lanes = qkv[:, q_cols + 2 * kv_cols :].astype(F32)
    scale_column = jnp.sum(scale_lanes, axis=1, keepdims=True)
    scale_row = jnp.sum(scale_lanes.T, axis=0, keepdims=True) * SOFT
    for group in range(groups):
        at = q_cols + group * HEAD_SIZE
        keys = qkv[:, at : at + HEAD_SIZE]
        keys_t = keys.astype(F32).T.astype(BF)
        at = at + kv_cols
        values = qkv[:, at : at + HEAD_SIZE]
        if group > 0:
            wait_group(qkv, in_sems, 1, group)
            wait_group(grads, in_sems, 1 + groups, group)
        for index in range(GROUP_HEADS):
            columns = head_columns(group * GROUP_HEADS + index)
            lanes = slice(index * tokens, (index + 1) * tokens)
            scores[:, lanes] = dot_nt(keys, qkv[:, columns])
            weight_grads[:, lanes] = dot_nt(values, grads[:, columns])
        def block(queries, lanes, reach):
            weight = weights_of(scores[:reach, lanes], bias[:reach, queries])
            weights[:reach, lanes] = weight.astype(BF)
            weight_grad = weight_grads[:reach, lanes]
            mean = jnp.sum(weight_grad * weight, axis=0, keepdims=True)
            score_grads[:reach, lanes] = (weight * (weight_grad - mean)).astype(BF)

        softmax_blocks(tokens, block)
        key_grad = jnp.zeros((tokens, HEAD_SIZE), F32)
        value_grad = jnp.zeros((tokens, HEAD_SIZE), F32)
        for index in range(GROUP_HEADS):
            columns = head_columns(group * GROUP_HEADS + index)
            lanes = slice(index * tokens, (index + 1) * tokens)
            score_grad = score_grads[:, lanes]
            scaled_q[columns, :] = (dot_nn(keys_t, score_grad) * scale_row).astype(BF)
            key_grad = key_grad + dot_nn(score_grad, qkv[:, columns])
            value_grad = value_grad + dot_nn(weights[:, lanes], grads[:, columns])
        at = group * HEAD_SIZE
        scaled_kv[:, at : at + HEAD_SIZE] = (key_grad * (scale_column * SOFT)).astype(BF)
        at = at + kv_cols
        scaled_kv[:, at : at + HEAD_SIZE] = (value_grad * scale_column).astype(BF)
    count, width, _ = chunks.shape
    through = dot_nt(landed(chunks, sems, count - 1)[...], scaled_kv[...])
    for index in range(count - 1):
        rows = slice(index * width, (index + 1) * width)
        through = through + dot_nn(landed(chunks, sems, index)[...], scaled_q[rows, :])
    out_ref[...] = through.T.astype(BF)


def merger_kernel(
    marks_ref, owners_ref, last_ref, pair_ref, across_ref, beside_ref, g0_ref, g1_ref, weight_ref,
    out_ref, grad_ref, rows, hidden, counts, places,
):
    added = summed(pair_ref, across_ref, beside_ref)
    rows[...] = last_ref[...].astype(F32) + chosen(g0_ref, g1_ref) * added
    share = grad_ref.shape[0]
    at = pl.multiple_of(lax.axis_index("mp") * share, share)
    grad_ref[...] = rows[pl.ds(at, share), :].astype(BF)
    x = rows[...].astype(BF)
    cols = weight_ref.shape[0]
    for start in range(0, cols, 256):
        hidden[:, start : start + 256] = dot_nt(x, weight_ref[start : start + 256, :])
    dp_count, sections = out_ref.shape[:2]
    owner_count = dp_count * sections

    def clear(owner, carry):
        counts[owner] = 0
        for slot in range(CAP):
            places[owner * CAP + slot] = -1
        return carry

    lax.fori_loop(0, owner_count, clear, 0, unroll=8)

    def place(block, carry):
        owner = owners_ref[0, block]

        @pl.when(marks_ref[0, block] == 1)
        def _():
            slot = counts[owner]
            places[owner * CAP + slot] = block
            counts[owner] = slot + 1

        return carry

    lax.fori_loop(0, marks_ref.shape[1], place, 0, unroll=4)

    def send(owner, carry):
        pieces = []
        for slot in range(CAP):
            block = places[owner * CAP + slot]
            at = pl.multiple_of(jnp.maximum(block, 0) * VB, VB)
            pieces.append(jnp.where(block >= 0, hidden[pl.ds(at, VB), :], 0.0))
        out_ref[lax.rem(owner, dp_count), lax.div(owner, dp_count)] = jnp.concatenate(
            pieces, axis=0
        ).astype(BF)
        return carry

    lax.fori_loop(0, owner_count, send, 0, unroll=4)


def merger_sum_kernel(parts_ref, own_ref, other_ref):
    section = lax.axis_index("section")
    sources = parts_ref.shape[0]

    def total(index):
        return add_parts(lambda source: parts_ref[source, index], sources)

    first, second = total(0), total(1)
    own_ref[...] = jnp.where(section == 0, first, second)
    other_ref[...] = jnp.where(section == 0, second, first).astype(BF)


def gelu_slope(values):
    cumulative = 0.5 * (1.0 + lax.erf(values * (1.0 / math.sqrt(2.0))))
    return cumulative + values * jnp.exp(-0.5 * values * values) * (1.0 / math.sqrt(2.0 * math.pi))


def local(
    embeds,
    cotangent,
    norm_gain,
    w_query,
    w_keyval,
    w_out,
    seq_lengths,
    image_mask,
    block_owner,
    merger_weight,
    merger_pre,
):
    section = lax.axis_index("section")
    mp_count = lax.axis_size("mp")
    dp_count = lax.axis_size("dp")
    rows, width = embeds.shape[1:]
    tokens = rows * mp_count
    share = tokens // dp_count
    q_cols = w_query.shape[3]
    kv_cols = w_keyval.shape[4]
    joined = q_cols + 2 * kv_cols + 128
    emb, cot = embeds[0], cotangent[0]
    wq, wout = w_query[0, 0], w_out[0, 0]
    wkv = w_keyval[0, 0].reshape(width, 2 * kv_cols)
    gain = norm_gain[0]

    def partner(index):
        other, rank = 1 - index // mp_count, (index % mp_count + mp_count // 2) % mp_count
        return other * mp_count + rank

    everyone = range(2 * mp_count)
    from_first = [(i, partner(i)) for i in everyone if i < mp_count]
    from_second = [(i, partner(i)) for i in everyone if i >= mp_count]

    def swap(array, pairs):
        return lax.ppermute(array, ("section", "mp"), pairs)

    def scatter(array, axis):
        return lax.all_to_all(array, axis, split_axis=0, concat_axis=0, tiled=True)

    def spread(copies):
        return scatter(copies, "dp").reshape(tokens, copies.shape[2])

    def gather(array, axis):
        return lax.all_gather(array, axis, axis=0, tiled=True)

    def chunks_of(count):
        return pltpu.VMEM((count, width, width), BF)

    own_x, other_x = jnp.where(section == 0, emb, cot), jnp.where(section == 0, cot, emb)
    received_x = swap(other_x, from_first + from_second)
    gain_x = swap(gain, from_first + from_second)
    def vmem(*shape):
        return pltpu.VMEM(shape, BF)

    def dma(count):
        return pltpu.SemaphoreType.DMA((count,))

    def other_rows_parts(x):
        return pl.pallas_call(
            first_kernel,
            out_shape=pltpu.HBM((dp_count, share, joined), BF),
            in_specs=[VMEM] * 2 + [HBM] * 3,
            out_specs=HBM,
            scratch_shapes=[chunks_of(5), vmem(dp_count, share, joined), dma(5), dma(6)],
            compiler_params=params(24),
            cost_estimate=cost(2 * tokens * width * joined, 6 << 20),
        )(x, gain, *in_hbm(wq, wkv, wout))

    def first_sum(parts):
        return pl.pallas_call(
            first_sum_kernel,
            out_shape=shape_of((share, joined), BF),
            in_specs=[ANY],
            out_specs=VMEM,
            scratch_shapes=[vmem(dp_count, share, joined), dma(6)],
            compiler_params=params(24),
            cost_estimate=cost(parts.size, 2 << 20),
        )(parts)

    def summed_copies(adder, parts):
        cols = parts.shape[2]
        return pl.pallas_call(
            functools.partial(sum_kernel, adder),
            out_shape=pltpu.HBM((dp_count, share, cols), BF),
            in_specs=[ANY],
            out_specs=HBM,
            scratch_shapes=[vmem(dp_count, share, cols), vmem(share, cols), dma(6), dma(dp_count)],
            compiler_params=params(24),
            cost_estimate=cost(parts.size, 4 << 20),
        )(parts)

    def chosen_copies(first, second, cols):
        return pl.pallas_call(
            choose_kernel,
            out_shape=pltpu.HBM((dp_count, share, cols), BF),
            in_specs=[VMEM] * 2,
            out_specs=HBM,
            scratch_shapes=[dma(dp_count)],
            compiler_params=params(24),
            cost_estimate=cost(0, 2 << 20),
        )(first, second)

    def loaded(joins, firsts, seconds):
        count = 5 if joins else 4
        return pl.pallas_call(
            functools.partial(load_kernel, joins, len(firsts)),
            out_shape=pltpu.VMEM((count, width, width), BF),
            in_specs=[HBM] * (len(firsts) + len(seconds)),
            out_specs=VMEM,
            scratch_shapes=[dma(count)],
            compiler_params=params(16),
            cost_estimate=cost(0, 5 << 20),
        )(*in_hbm(*firsts, *seconds))

    def beside(array, distance):
        return lax.ppermute(array, "mp", [(i, i ^ distance) for i in range(mp_count)])

    def sum_over_mp(part, *later):
        mate = beside(part, 1)
        at = lax.axis_index("mp") % 2 * (tokens // 2)

        def half(array):
            return lax.dynamic_slice_in_dim(array, at, tokens // 2).astype(F32)

        pair_half = (half(part) + half(mate)).astype(BF)
        across = beside(pair_half, 2)
        pair_half, part, mate, *later = lax.optimization_barrier((pair_half, part, mate, *later))
        pair = (part.astype(F32) + mate.astype(F32)).astype(BF)
        return (pair, across, beside(across, 1)), later

    others = [beside(own_x, distance) for distance in (1, 2, 3)]
    first_chunks = pl.pallas_call(
        first_load_kernel,
        out_shape=pltpu.VMEM((5, width, width), BF),
        in_specs=[HBM] * 3,
        out_specs=VMEM,
        scratch_shapes=[dma(5)],
        compiler_params=params(16),
        cost_estimate=cost(0, 5 << 20),
    )(*in_hbm(wq, wkv, wout))
    own_parts, own_all = pl.pallas_call(
        first_own_kernel,
        out_shape=[pltpu.HBM((dp_count, share, joined), BF), shape_of((tokens, width), BF)],
        in_specs=[VMEM] * 6,
        out_specs=[HBM, VMEM],
        scratch_shapes=[
            pltpu.VMEM((tokens, width), F32),
            vmem(dp_count, share, joined),
            dma(6),
        ],
        compiler_params=params(24),
        cost_estimate=cost(2 * tokens * width * joined, 6 << 20),
    )(own_x, *others, gain, first_chunks)
    own_parts, received_x, gain_x, wq_s, wout_s = lax.optimization_barrier(
        (own_parts, received_x, gain_x, wq, wout)
    )
    own_parts = scatter(own_parts, "dp")
    wq_b = swap(wq_s, from_second)
    cuts = (5 * q_cols // 16, 5 * q_cols // 8)
    wout_a0 = swap(wout_s[: cuts[0]], from_first)
    wout_a1, wout_a2 = wout_s[cuts[0] : cuts[1]], wout_s[cuts[1] :]
    other_parts = other_rows_parts(gather(received_x, "mp"))
    own_parts, other_parts, wout_a0, wout_a1, wout_a2 = lax.optimization_barrier(
        (own_parts, other_parts, wout_a0, wout_a1, wout_a2)
    )
    wout_a1 = swap(wout_a1, from_first)
    own = first_sum(own_parts)
    mine_all = gather(other_x, "mp")
    other_parts, own, mine_all = lax.optimization_barrier(
        (scatter(other_parts, "dp"), own, mine_all)
    )
    other = first_sum(other_parts)
    received = swap(other, from_first)
    received_grad, wkv_s = lax.optimization_barrier((swap(other, from_second), wkv))
    wkv_b = swap(wkv_s, from_second)
    copies, wout_a1, wout_a2 = lax.optimization_barrier(
        (chosen_copies(own, received, joined), wout_a1, wout_a2)
    )
    wout_a2 = swap(wout_a2, from_first)
    grad_copies = chosen_copies(received_grad, own, q_cols)
    qkv_first, grad_copies, wq_b, wq_s, wkv_s = lax.optimization_barrier(
        (spread(copies), grad_copies, wq_b, wq, wkv)
    )
    wout_a = (wout_a0, wout_a1, wout_a2)
    wq_a, wkv_a = swap(wq_s, from_first), swap(wkv_s, from_first)
    head_grad_last = spread(grad_copies)

    def layer_forward(qkv, wouts):
        out = pl.pallas_call(
            forward_kernel,
            out_shape=shape_of((tokens, width), BF),
            in_specs=[SMEM, ANY] + [HBM] * (1 + len(wouts[1])),
            out_specs=VMEM,
            scratch_shapes=[
                vmem(tokens, joined),
                chunks_of(4),
                pltpu.VMEM((tokens, tokens), F32),
                pltpu.VMEM((tokens, GROUP_HEADS * tokens), F32),
                vmem(tokens, GROUP_HEADS * tokens),
                vmem(tokens, q_cols),
                dma(4),
                dma(3),
            ],
            compiler_params=params(32),
            cost_estimate=cost(6 * tokens * tokens * q_cols, 4 << 20),
        )(seq_lengths, qkv, *in_hbm(wouts[0], *wouts[1]))
        return out

    def rows_after(resident, sums):
        even = lax.axis_index("mp") % 2 == 0
        lower, upper = jnp.where(even, *sums[1:]), jnp.where(even, *sums[:0:-1])
        added = sums[0].astype(F32) + jnp.concatenate([lower, upper], axis=0).astype(F32)
        return (resident.astype(F32) + added).astype(BF)

    out, wkv_b = lax.optimization_barrier((layer_forward(qkv_first, (wout, wout_a)), wkv_b))
    sums, pieces = sum_over_mp(out, wq_b, wkv_b, wq, wkv)
    joined_last = loaded(True, pieces[:2], pieces[2:])
    parts = pl.pallas_call(
        project_kernel,
        out_shape=pltpu.HBM((dp_count, share, joined), BF),
        in_specs=[VMEM] * 8,
        out_specs=HBM,
        scratch_shapes=[vmem(dp_count, share, joined), dma(6)],
        compiler_params=params(24),
        cost_estimate=cost(2 * tokens * width * joined, 6 << 20),
    )(own_all, mine_all, *sums, gain_x, gain, joined_last)
    parts, head_grad_last = lax.optimization_barrier((parts, head_grad_last))
    qkv_last = spread(summed_copies(scaled_sum, scatter(parts, "dp")))
    wout_b = swap(wout, from_second)
    wout_last = jnp.where(section == 0, wout_b, wout)
    h_one = rows_after(jnp.where(section == 0, own_all, mine_all), sums)
    rows_after(h_one, sum_over_mp(layer_forward(qkv_last, (wout_last, (wout_last,))))[0])

    def layer_backward(qkv, head_grads, wqs, wkvs, later=()):
        through = pl.pallas_call(
            backward_kernel,
            out_shape=shape_of((tokens, width), BF),
            in_specs=[SMEM, ANY, ANY] + [HBM] * 4,
            out_specs=VMEM,
            scratch_shapes=[
                vmem(tokens, joined),
                vmem(tokens, q_cols),
                chunks_of(5),
                pltpu.VMEM((tokens, tokens), F32),
                pltpu.VMEM((tokens, GROUP_HEADS * tokens), F32),
                pltpu.VMEM((tokens, GROUP_HEADS * tokens), F32),
                vmem(tokens, GROUP_HEADS * tokens),
                vmem(tokens, GROUP_HEADS * tokens),
                vmem(q_cols, tokens),
                vmem(tokens, 2 * kv_cols),
                dma(5),
                dma(5),
            ],
            compiler_params=params(32),
            cost_estimate=cost(12 * tokens * tokens * q_cols, 6 << 20),
        )(seq_lengths, qkv, head_grads, *in_hbm(*wqs, *wkvs))
        return sum_over_mp(through, *later)

    sums, pieces = layer_backward(
        qkv_last,
        *in_hbm(head_grad_last),
        (wq_b, wq),
        (wkv_b, wkv),
        later=(wout, *wout_a),
    )
    parts, grad_one = pl.pallas_call(
        head_grad_kernel,
        out_shape=[pltpu.HBM((dp_count, share, q_cols), BF), shape_of((tokens, width), BF)],
        in_specs=[VMEM] * 8,
        out_specs=[HBM, VMEM],
        scratch_shapes=[vmem(dp_count, share, q_cols), dma(4)],
        compiler_params=params(24),
        cost_estimate=cost(2 * tokens * width * q_cols, 4 << 20),
    )(mine_all, own_all, *sums, gain_x, gain, loaded(False, pieces[:1], pieces[1:]))
    parts, wq_a = lax.optimization_barrier((scatter(parts, "dp"), wq_a))
    head_grad_first, wkv_a = lax.optimization_barrier(
        (spread(summed_copies(plain_sum, parts)), wkv_a)
    )
    sums, _ = layer_backward(qkv_first, head_grad_first, (wq, wq_a), (wkv, wkv_a))

    hidden_cols = merger_weight.shape[0]
    outgoing, input_grad = pl.pallas_call(
        merger_kernel,
        out_shape=[
            shape_of((dp_count, 2, CAP * VB, hidden_cols), BF),
            shape_of((rows, width), BF),
        ],
        in_specs=[SMEM, SMEM] + [VMEM] * 7,
        out_specs=[VMEM] * 2,
        scratch_shapes=[
            pltpu.VMEM((tokens, width), F32),
            pltpu.VMEM((tokens, hidden_cols), F32),
            pltpu.SMEM((2 * dp_count,), jnp.int32),
            pltpu.SMEM((2 * dp_count * CAP,), jnp.int32),
        ],
        compiler_params=params(24),
    )(image_mask, block_owner, grad_one, *sums, gain, gain_x, merger_weight)
    kept, passed = pl.pallas_call(
        merger_sum_kernel,
        out_shape=[
            shape_of((CAP * VB, hidden_cols), F32),
            shape_of((CAP * VB, hidden_cols), BF),
        ],
        in_specs=[VMEM],
        out_specs=[VMEM] * 2,
        compiler_params=params(24),
    )(scatter(outgoing, "dp"))
    crossed = lax.ppermute(passed, "section", [(0, 1), (1, 0)]).astype(F32)
    first = jnp.where(section == 0, kept, crossed)
    second = jnp.where(section == 0, crossed, kept)
    hidden_grad = jnp.stack([first, second]).reshape(2, CAP, VB, hidden_cols)
    merger_grad = gelu_slope(merger_pre[0].astype(F32)) * hidden_grad
    return (input_grad[None], merger_grad[None])


def solution(mesh):
    placed = (
        P("section", "mp", "dp"),
        P("section", "mp", "dp"),
        P(None, "section", "dp"),
        P(None, "section", "dp", "mp"),
        P(None, "section", "dp", None, "mp"),
        P(None, "section", "mp", "dp"),
        P(),
        P("section", None),
        P("section", None),
        P("mp", "dp"),
        P(("section", "dp"), None, None, None, "mp"),
    )
    return jax.shard_map(
        local,
        mesh=mesh,
        in_specs=placed,
        out_specs=(P("section", "mp", "dp"), P(("section", "dp"), None, None, None, "mp")),
        check_vma=False,
    )
```

```python
import functools
import math

import jax
import jax.numpy as jnp
from jax import lax
from jax.experimental import pallas as pl
from jax.experimental.pallas import tpu as pltpu
from jax.sharding import PartitionSpec as P

MODEL_WIDTH = 8192
HEAD_SIZE = 128
GROUP_HEADS = 8
CAP = 2
VB = 8
NSEQ = 3

EPSILON = 1e-06
MASKED = -1e30
SOFT = 1.0 / math.sqrt(HEAD_SIZE)
LOG2E = math.log2(math.e)
QB = 128

BF = jnp.bfloat16
F32 = jnp.float32

VMEM = pl.BlockSpec(memory_space=pltpu.VMEM)
SMEM = pl.BlockSpec(memory_space=pltpu.SMEM)
ANY = pl.BlockSpec(memory_space=pl.ANY)
HBM = pl.BlockSpec(memory_space=pltpu.HBM)


def shape_of(shape, dtype):
    return jax.ShapeDtypeStruct(shape, dtype)


def in_hbm(*arrays):
    return [pltpu.with_memory_space_constraint(array, pltpu.HBM) for array in arrays]


def params(mebibytes):
    return pltpu.CompilerParams(vmem_limit_bytes=mebibytes << 20)


def cost(flops, bytes_accessed):
    return pl.CostEstimate(flops=flops, bytes_accessed=bytes_accessed, transcendentals=0)


def dot_nn(left, right):
    return jnp.dot(left, right, preferred_element_type=F32)


def dot_nt(left, right):
    return lax.dot_general(left, right, (((1,), (1,)), ((), ())), preferred_element_type=F32)


def two_lanes(column):
    high = column.astype(BF).astype(F32)
    lane = lax.broadcasted_iota(jnp.int32, (column.shape[0], 128), 1)
    return jnp.where(lane == 0, high, jnp.where(lane == 1, column - high, 0.0)).astype(BF)


def start_columns(sources, chunks, sems):
    width, index = chunks.shape[2], 0
    for source in sources:
        for start in range(0, source.shape[1], width):
            block = source.at[:, start : start + width]
            pltpu.make_async_copy(block, chunks.at[index], sems.at[index]).start()
            index += 1


def start_rows(sources, chunks, sems):
    rows, at = chunks.shape[1], 0
    for source in sources:
        start = 0
        while start < source.shape[0]:
            index, within = at // rows, at % rows
            count = min(rows - within, source.shape[0] - start)
            block = source.at[start : start + count, :]
            place = chunks.at[index, within : within + count, :]
            pltpu.make_async_copy(block, place, sems.at[index]).start()
            start, at = start + count, at + count


def start_joined(wqs, wkv_ref, chunks, sems):
    start_columns(wqs, chunks, sems)
    last = chunks.shape[0] - 1
    pltpu.make_async_copy(wkv_ref, chunks.at[last], sems.at[last]).start()


def landed(chunks, sems, index):
    pltpu.make_async_copy(chunks.at[index], chunks.at[index], sems.at[index]).wait()
    return chunks.at[index]


def by_section(first, second):
    section = lax.axis_index("section")
    pl.when(section == 0)(first)
    pl.when(section != 0)(second)


def spans(cols):
    return [slice(start, min(start + 512, cols)) for start in range(0, cols, 512)]


def start_spans(source, target, sems):
    for index, span in enumerate(spans(target.shape[-1])):
        at = (slice(None),) * (len(target.shape) - 1) + (span,)
        pltpu.make_async_copy(source.at[at], target.at[at], sems.at[index]).start()


def wait_span(target, sems, index):
    at = (slice(None),) * (len(target.shape) - 1) + (spans(target.shape[-1])[index],)
    pltpu.make_async_copy(target.at[at], target.at[at], sems.at[index]).wait()


def sender(staged, out_ref, sems):
    owners, share, cols = staged.shape

    def put(start, tile):
        span = slice(start, start + tile.shape[1])
        staged[:, :, span] = tile.reshape(owners, share, tile.shape[1])
        index = spans(cols).index(span)
        at = (slice(None), slice(None), span)
        pltpu.make_async_copy(staged.at[at], out_ref.at[at], sems.at[index]).start()

    def finish():
        for index in range(len(spans(cols))):
            wait_span(staged, sems, index)

    return put, finish


def repeat_out(tile, out_ref, sems):
    for place in range(out_ref.shape[0]):
        pltpu.make_async_copy(tile, out_ref.at[place], sems.at[place]).start()


def repeat_wait(tile, out_ref, sems):
    for place in range(out_ref.shape[0]):
        pltpu.make_async_copy(tile, out_ref.at[place], sems.at[place]).wait()


def project_rows(rows, gain, chunks, chunk_at, put):
    rows_f = rows.astype(F32)
    normed = (rows_f * gain).astype(BF)
    count, _, width = chunks.shape
    put(count * width, two_lanes(jnp.sum(rows_f * rows_f, axis=1, keepdims=True)))
    for index in range(count):
        put(index * width, dot_nn(normed, chunk_at(index)[...]).astype(BF))


def load_kernel(joined, pieces, *refs):
    *sources, out_ref, sems = refs

    def load(refs):
        if joined:
            start_joined(refs[:-1], refs[-1], out_ref, sems)
        else:
            start_rows(refs, out_ref, sems)

    by_section(lambda: load(sources[:pieces]), lambda: load(sources[pieces:]))
    for index in range(out_ref.shape[0]):
        landed(out_ref, sems, index)


def first_kernel(
    x_ref, gain_ref, wq_ref, wkv_ref, wout_ref, out_ref, chunks, staged, sems, out_sems
):
    put, finish = sender(staged, out_ref, out_sems)
    tokens = x_ref.shape[0]

    def rows():
        return jnp.concatenate([x_ref[tokens // 2 :, :], x_ref[: tokens // 2, :]], axis=0)

    def first():
        start_joined([wq_ref], wkv_ref, chunks, sems)
        project_rows(rows(), gain_ref[...], chunks, lambda at: landed(chunks, sems, at), put)

    def second():
        start_rows([wout_ref], chunks, sems)
        count, width, _ = chunks.shape
        put(count * width, jnp.zeros((tokens, 128), BF))
        put((count - 1) * width, jnp.zeros((tokens, width), BF))
        x = rows()
        for index in range(count - 1):
            put(index * width, dot_nt(x, landed(chunks, sems, index)[...]).astype(BF))

    by_section(first, second)
    finish()


def first_load_kernel(wq_ref, wkv_ref, wout_ref, out_ref, sems):
    def wait(count):
        for index in range(count):
            landed(out_ref, sems, index)

    def first():
        start_joined([wq_ref], wkv_ref, out_ref, sems)
        wait(out_ref.shape[0])

    def second():
        start_rows([wout_ref], out_ref, sems)
        wait(out_ref.shape[0] - 1)

    by_section(first, second)


def first_own_kernel(
    mine_ref, near_ref, far_ref, cross_ref, gain_ref, chunks, out_ref, x_ref, x, staged, out_sems
):
    rank = lax.axis_index("mp")
    share = mine_ref.shape[0]
    for distance, ref in enumerate((mine_ref, near_ref, far_ref, cross_ref)):
        at = pl.multiple_of(jnp.bitwise_xor(rank, distance) * share, share)
        x[pl.ds(at, share), :] = ref[...].astype(F32)
    x_ref[...] = x[...].astype(BF)
    put, finish = sender(staged, out_ref, out_sems)
    tokens = x_ref.shape[0]
    count, width, _ = chunks.shape

    def first():
        project_rows(x_ref[...], gain_ref[...], chunks, lambda at: chunks.at[at], put)

    def second():
        put(count * width, jnp.zeros((tokens, 128), BF))
        put((count - 1) * width, jnp.zeros((tokens, width), BF))
        for index in range(count - 1):
            put(index * width, dot_nt(x_ref[...], chunks[index]).astype(BF))

    by_section(first, second)
    finish()


def chosen(first_ref, second_ref):
    return jnp.where(lax.axis_index("section") == 0, first_ref[...], second_ref[...])


def summed(pair_ref, across_ref, beside_ref):
    even = lax.axis_index("mp") % 2 == 0
    lower = jnp.where(even, across_ref[...], beside_ref[...])
    upper = jnp.where(even, beside_ref[...], across_ref[...])
    return pair_ref[...].astype(F32) + jnp.concatenate([lower, upper], axis=0).astype(F32)


def project_kernel(
    r0_ref, r1_ref, pair_ref, across_ref, beside_ref, g0_ref, g1_ref, chunks, out_ref,
    staged, out_sems,
):
    added = summed(pair_ref, across_ref, beside_ref)
    rows = (chosen(r0_ref, r1_ref).astype(F32) + added).astype(BF)
    put, finish = sender(staged, out_ref, out_sems)
    project_rows(rows, chosen(g0_ref, g1_ref), chunks, lambda at: chunks.at[at], put)
    finish()


def head_grad_kernel(
    r0_ref, r1_ref, pair_ref, across_ref, beside_ref, g0_ref, g1_ref, chunks, out_ref, rows_ref,
    staged, out_sems,
):
    added = summed(pair_ref, across_ref, beside_ref)
    rows = chosen(r0_ref, r1_ref).astype(F32) + chosen(g0_ref, g1_ref) * added
    rows_ref[...] = rows.astype(BF)
    count, width, _ = chunks.shape
    put, finish = sender(staged, out_ref, out_sems)
    for index in range(count):
        put(index * width, dot_nt(rows_ref[...], chunks[index]).astype(BF))
    finish()


def add_parts(load, count):
    total = load(0).astype(F32)
    for index in range(1, count):
        total = total + load(index).astype(F32)
    return total


def part_sums(parts, sems):
    def total(index):
        wait_span(parts, sems, index)
        span = spans(parts.shape[2])[index]
        return add_parts(lambda source: parts[source, :, span], parts.shape[0])

    return total


def scaled_sum(total, tile):
    ranges = spans(tile.shape[1])
    squares = jnp.sum(total(len(ranges) - 1), axis=1, keepdims=True)
    scale = lax.rsqrt(squares / MODEL_WIDTH + EPSILON)
    for index, span in enumerate(ranges[:-1]):
        tile[:, span] = (total(index) * scale).astype(BF)
    tile[:, ranges[-1]] = two_lanes(scale)


def plain_sum(total, tile):
    for index, span in enumerate(spans(tile.shape[1])):
        tile[:, span] = total(index).astype(BF)


def first_sum_kernel(parts_ref, out_ref, parts, sems):
    start_spans(parts_ref, parts, sems)
    total = part_sums(parts, sems)
    by_section(lambda: scaled_sum(total, out_ref), lambda: plain_sum(total, out_ref))


def sum_kernel(adder, parts_ref, out_ref, parts, tile, sems, out_sems):
    start_spans(parts_ref, parts, sems)
    adder(part_sums(parts, sems), tile)
    repeat_out(tile, out_ref, out_sems)
    repeat_wait(tile, out_ref, out_sems)


def choose_kernel(first_ref, second_ref, out_ref, sems):
    first = first_ref.at[:, : out_ref.shape[2]]
    second = second_ref.at[:, : out_ref.shape[2]]
    by_section(
        lambda: repeat_out(first, out_ref, sems), lambda: repeat_out(second, out_ref, sems)
    )
    repeat_wait(first, out_ref, sems)


def fill_bias(seq_ref, bias):
    section = lax.axis_index("section")
    tokens = bias.shape[0]
    keys = lax.broadcasted_iota(jnp.int32, (tokens, tokens), 0)
    queries = lax.broadcasted_iota(jnp.int32, (tokens, tokens), 1)
    key_segment = jnp.zeros((tokens, tokens), jnp.int32)
    query_segment = jnp.zeros((tokens, tokens), jnp.int32)
    bound = 0
    for index in range(NSEQ):
        bound = bound + seq_ref[section, index]
        key_segment = key_segment + (keys >= bound).astype(jnp.int32)
        query_segment = query_segment + (queries >= bound).astype(jnp.int32)
    allowed = (keys <= queries) & (key_segment == query_segment)
    bias[...] = jnp.where(allowed, 0.0, MASKED)


def head_columns(head):
    return slice(head * HEAD_SIZE, (head + 1) * HEAD_SIZE)


def softmax_blocks(tokens, body):
    def one_head(head, carry):
        for at in range(0, tokens, QB):
            lanes = pl.ds(pl.multiple_of(head * tokens + at, QB), QB)
            body(slice(at, at + QB), lanes, at + QB)
        return carry

    lax.fori_loop(0, GROUP_HEADS, one_head, 0, unroll=8)


def clear_unreached(target, tokens):
    for head in range(GROUP_HEADS):
        for at in range(0, tokens - QB, QB):
            lanes = slice(head * tokens + at, head * tokens + at + QB)
            target[at + QB :, lanes] = jnp.zeros((tokens - at - QB, QB), target.dtype)


def weights_of(scores, bias):
    scores = scores * (SOFT * LOG2E) + bias
    raised = jnp.exp2(scores - jnp.max(scores, axis=0, keepdims=True))
    return raised * (1.0 / jnp.sum(raised, axis=0, keepdims=True))


def start_qkv(qkv_ref, qkv, q_cols, sems):
    pltpu.make_async_copy(qkv_ref.at[:, q_cols:], qkv.at[:, q_cols:], sems.at[0]).start()
    for group in range(q_cols // (GROUP_HEADS * HEAD_SIZE)):
        start_group(qkv_ref, qkv, sems, 1, group)


def start_group(source, target, sems, first, group):
    width = GROUP_HEADS * HEAD_SIZE
    at = (slice(None), slice(group * width, (group + 1) * width))
    pltpu.make_async_copy(source.at[at], target.at[at], sems.at[first + group]).start()


def wait_group(target, sems, first, group):
    width = GROUP_HEADS * HEAD_SIZE
    at = (slice(None), slice(group * width, (group + 1) * width))
    pltpu.make_async_copy(target.at[at], target.at[at], sems.at[first + group]).wait()


def forward_kernel(seq_ref, qkv_ref, wout0_ref, *refs):
    *wout1_refs, out_ref, qkv, chunks, bias, scores, weights, attended, sems, in_sems = refs
    tokens, q_cols = attended.shape
    start_qkv(qkv_ref, qkv, q_cols, in_sems)
    by_section(
        lambda: start_rows([wout0_ref], chunks, sems),
        lambda: start_rows(wout1_refs, chunks, sems),
    )
    fill_bias(seq_ref, bias)
    clear_unreached(weights, tokens)
    groups = q_cols // (GROUP_HEADS * HEAD_SIZE)
    pltpu.make_async_copy(qkv.at[:, q_cols:], qkv.at[:, q_cols:], in_sems.at[0]).wait()
    for group in range(groups):
        at = q_cols + group * HEAD_SIZE
        keys = qkv[:, at : at + HEAD_SIZE]
        at = at + groups * HEAD_SIZE
        values_t = qkv[:, at : at + HEAD_SIZE].astype(F32).T.astype(BF)
        wait_group(qkv, in_sems, 1, group)
        for index in range(GROUP_HEADS):
            columns = head_columns(group * GROUP_HEADS + index)
            scores[:, index * tokens : (index + 1) * tokens] = dot_nt(keys, qkv[:, columns])

        def block(queries, lanes, reach):
            weights[:reach, lanes] = weights_of(
                scores[:reach, lanes], bias[:reach, queries]
            ).astype(BF)

        softmax_blocks(tokens, block)
        for index in range(GROUP_HEADS):
            columns = head_columns(group * GROUP_HEADS + index)
            mixed = dot_nn(values_t, weights[:, index * tokens : (index + 1) * tokens])
            attended[:, columns] = mixed.T.astype(BF)
    count, width, _ = chunks.shape
    out = dot_nn(attended[:, :width], landed(chunks, sems, 0)[...])
    for index in range(1, count):
        columns = slice(index * width, (index + 1) * width)
        out = out + dot_nn(attended[:, columns], landed(chunks, sems, index)[...])
    out_ref[...] = out.astype(BF)


def backward_kernel(
    seq_ref, qkv_ref, grads_ref, wq0_ref, wq1_ref, wkv0_ref, wkv1_ref, out_ref,
    qkv, grads, chunks, bias, scores, weight_grads, weights, score_grads, scaled_q, scaled_kv,
    sems, in_sems,
):
    tokens, q_cols = grads.shape
    groups = q_cols // (GROUP_HEADS * HEAD_SIZE)
    pltpu.make_async_copy(qkv_ref.at[:, q_cols:], qkv.at[:, q_cols:], in_sems.at[0]).start()
    start_group(qkv_ref, qkv, in_sems, 1, 0)
    start_group(grads_ref, grads, in_sems, 1 + groups, 0)
    fill_bias(seq_ref, bias)
    clear_unreached(weights, tokens)
    clear_unreached(score_grads, tokens)
    kv_cols = groups * HEAD_SIZE
    pltpu.make_async_copy(qkv.at[:, q_cols:], qkv.at[:, q_cols:], in_sems.at[0]).wait()
    wait_group(qkv, in_sems, 1, 0)
    wait_group(grads, in_sems, 1 + groups, 0)
    for group in range(1, groups):
        start_group(qkv_ref, qkv, in_sems, 1, group)
        start_group(grads_ref, grads, in_sems, 1 + groups, group)
    by_section(
        lambda: start_joined([wq0_ref], wkv0_ref, chunks, sems),
        lambda: start_joined([wq1_ref], wkv1_ref, chunks, sems),
    )
    scale_lanes = qkv[:, q_cols + 2 * kv_cols :].astype(F32)
    scale_column = jnp.sum(scale_lanes, axis=1, keepdims=True)
    scale_row = jnp.sum(scale_lanes.T, axis=0, keepdims=True) * SOFT
    for group in range(groups):
        at = q_cols + group * HEAD_SIZE
        keys = qkv[:, at : at + HEAD_SIZE]
        keys_t = keys.astype(F32).T.astype(BF)
        at = at + kv_cols
        values = qkv[:, at : at + HEAD_SIZE]
        if group > 0:
            wait_group(qkv, in_sems, 1, group)
            wait_group(grads, in_sems, 1 + groups, group)
        for index in range(GROUP_HEADS):
            columns = head_columns(group * GROUP_HEADS + index)
            lanes = slice(index * tokens, (index + 1) * tokens)
            scores[:, lanes] = dot_nt(keys, qkv[:, columns])
            weight_grads[:, lanes] = dot_nt(values, grads[:, columns])
        def block(queries, lanes, reach):
            weight = weights_of(scores[:reach, lanes], bias[:reach, queries])
            weights[:reach, lanes] = weight.astype(BF)
            weight_grad = weight_grads[:reach, lanes]
            mean = jnp.sum(weight_grad * weight, axis=0, keepdims=True)
            score_grads[:reach, lanes] = (weight * (weight_grad - mean)).astype(BF)

        softmax_blocks(tokens, block)
        key_grad = jnp.zeros((tokens, HEAD_SIZE), F32)
        value_grad = jnp.zeros((tokens, HEAD_SIZE), F32)
        for index in range(GROUP_HEADS):
            columns = head_columns(group * GROUP_HEADS + index)
            lanes = slice(index * tokens, (index + 1) * tokens)
            score_grad = score_grads[:, lanes]
            scaled_q[columns, :] = (dot_nn(keys_t, score_grad) * scale_row).astype(BF)
            key_grad = key_grad + dot_nn(score_grad, qkv[:, columns])
            value_grad = value_grad + dot_nn(weights[:, lanes], grads[:, columns])
        at = group * HEAD_SIZE
        scaled_kv[:, at : at + HEAD_SIZE] = (key_grad * (scale_column * SOFT)).astype(BF)
        at = at + kv_cols
        scaled_kv[:, at : at + HEAD_SIZE] = (value_grad * scale_column).astype(BF)
    count, width, _ = chunks.shape
    through = dot_nt(landed(chunks, sems, count - 1)[...], scaled_kv[...])
    for index in range(count - 1):
        rows = slice(index * width, (index + 1) * width)
        through = through + dot_nn(landed(chunks, sems, index)[...], scaled_q[rows, :])
    out_ref[...] = through.T.astype(BF)


def merger_kernel(
    marks_ref, owners_ref, last_ref, pair_ref, across_ref, beside_ref, g0_ref, g1_ref, weight_ref,
    out_ref, grad_ref, rows, hidden, counts, places,
):
    added = summed(pair_ref, across_ref, beside_ref)
    rows[...] = last_ref[...].astype(F32) + chosen(g0_ref, g1_ref) * added
    share = grad_ref.shape[0]
    at = pl.multiple_of(lax.axis_index("mp") * share, share)
    grad_ref[...] = rows[pl.ds(at, share), :].astype(BF)
    x = rows[...].astype(BF)
    cols = weight_ref.shape[0]
    for start in range(0, cols, 256):
        hidden[:, start : start + 256] = dot_nt(x, weight_ref[start : start + 256, :])
    dp_count, sections = out_ref.shape[:2]
    owner_count = dp_count * sections

    def clear(owner, carry):
        counts[owner] = 0
        for slot in range(CAP):
            places[owner * CAP + slot] = -1
        return carry

    lax.fori_loop(0, owner_count, clear, 0, unroll=8)

    def place(block, carry):
        owner = owners_ref[0, block]

        @pl.when(marks_ref[0, block] == 1)
        def _():
            slot = counts[owner]
            places[owner * CAP + slot] = block
            counts[owner] = slot + 1

        return carry

    lax.fori_loop(0, marks_ref.shape[1], place, 0, unroll=4)

    def send(owner, carry):
        pieces = []
        for slot in range(CAP):
            block = places[owner * CAP + slot]
            at = pl.multiple_of(jnp.maximum(block, 0) * VB, VB)
            pieces.append(jnp.where(block >= 0, hidden[pl.ds(at, VB), :], 0.0))
        out_ref[lax.rem(owner, dp_count), lax.div(owner, dp_count)] = jnp.concatenate(
            pieces, axis=0
        ).astype(BF)
        return carry

    lax.fori_loop(0, owner_count, send, 0, unroll=4)


def merger_sum_kernel(parts_ref, own_ref, other_ref):
    section = lax.axis_index("section")
    sources = parts_ref.shape[0]

    def total(index):
        return add_parts(lambda source: parts_ref[source, index], sources)

    first, second = total(0), total(1)
    own_ref[...] = jnp.where(section == 0, first, second)
    other_ref[...] = jnp.where(section == 0, second, first).astype(BF)


def gelu_slope(values):
    cumulative = 0.5 * (1.0 + lax.erf(values * (1.0 / math.sqrt(2.0))))
    return cumulative + values * jnp.exp(-0.5 * values * values) * (1.0 / math.sqrt(2.0 * math.pi))


def local(
    embeds,
    cotangent,
    norm_gain,
    w_query,
    w_keyval,
    w_out,
    seq_lengths,
    image_mask,
    block_owner,
    merger_weight,
    merger_pre,
):
    section = lax.axis_index("section")
    mp_count = lax.axis_size("mp")
    dp_count = lax.axis_size("dp")
    rows, width = embeds.shape[1:]
    tokens = rows * mp_count
    share = tokens // dp_count
    q_cols = w_query.shape[3]
    kv_cols = w_keyval.shape[4]
    joined = q_cols + 2 * kv_cols + 128
    emb, cot = embeds[0], cotangent[0]
    wq, wout = w_query[0, 0], w_out[0, 0]
    wkv = w_keyval[0, 0].reshape(width, 2 * kv_cols)
    gain = norm_gain[0]

    def partner(index):
        other, rank = 1 - index // mp_count, (index % mp_count + mp_count // 2) % mp_count
        return other * mp_count + rank

    everyone = range(2 * mp_count)
    from_first = [(i, partner(i)) for i in everyone if i < mp_count]
    from_second = [(i, partner(i)) for i in everyone if i >= mp_count]

    def swap(array, pairs):
        return lax.ppermute(array, ("section", "mp"), pairs)

    def scatter(array, axis):
        return lax.all_to_all(array, axis, split_axis=0, concat_axis=0, tiled=True)

    def spread(copies):
        return scatter(copies, "dp").reshape(tokens, copies.shape[2])

    def gather(array, axis):
        return lax.all_gather(array, axis, axis=0, tiled=True)

    def chunks_of(count):
        return pltpu.VMEM((count, width, width), BF)

    own_x, other_x = jnp.where(section == 0, emb, cot), jnp.where(section == 0, cot, emb)
    received_x = swap(other_x, from_first + from_second)
    gain_x = swap(gain, from_first + from_second)
    def vmem(*shape):
        return pltpu.VMEM(shape, BF)

    def dma(count):
        return pltpu.SemaphoreType.DMA((count,))

    def other_rows_parts(x):
        return pl.pallas_call(
            first_kernel,
            out_shape=pltpu.HBM((dp_count, share, joined), BF),
            in_specs=[VMEM] * 2 + [HBM] * 3,
            out_specs=HBM,
            scratch_shapes=[chunks_of(5), vmem(dp_count, share, joined), dma(5), dma(6)],
            compiler_params=params(24),
            cost_estimate=cost(2 * tokens * width * joined, 6 << 20),
        )(x, gain, *in_hbm(wq, wkv, wout))

    def first_sum(parts):
        return pl.pallas_call(
            first_sum_kernel,
            out_shape=shape_of((share, joined), BF),
            in_specs=[ANY],
            out_specs=VMEM,
            scratch_shapes=[vmem(dp_count, share, joined), dma(6)],
            compiler_params=params(24),
            cost_estimate=cost(parts.size, 2 << 20),
        )(parts)

    def summed_copies(adder, parts):
        cols = parts.shape[2]
        return pl.pallas_call(
            functools.partial(sum_kernel, adder),
            out_shape=pltpu.HBM((dp_count, share, cols), BF),
            in_specs=[ANY],
            out_specs=HBM,
            scratch_shapes=[vmem(dp_count, share, cols), vmem(share, cols), dma(6), dma(dp_count)],
            compiler_params=params(24),
            cost_estimate=cost(parts.size, 4 << 20),
        )(parts)

    def chosen_copies(first, second, cols):
        return pl.pallas_call(
            choose_kernel,
            out_shape=pltpu.HBM((dp_count, share, cols), BF),
            in_specs=[VMEM] * 2,
            out_specs=HBM,
            scratch_shapes=[dma(dp_count)],
            compiler_params=params(24),
            cost_estimate=cost(0, 2 << 20),
        )(first, second)

    def loaded(joins, firsts, seconds):
        count = 5 if joins else 4
        return pl.pallas_call(
            functools.partial(load_kernel, joins, len(firsts)),
            out_shape=pltpu.VMEM((count, width, width), BF),
            in_specs=[HBM] * (len(firsts) + len(seconds)),
            out_specs=VMEM,
            scratch_shapes=[dma(count)],
            compiler_params=params(16),
            cost_estimate=cost(0, 5 << 20),
        )(*in_hbm(*firsts, *seconds))

    def beside(array, distance):
        return lax.ppermute(array, "mp", [(i, i ^ distance) for i in range(mp_count)])

    def sum_over_mp(part, *later):
        mate = beside(part, 1)
        at = lax.axis_index("mp") % 2 * (tokens // 2)

        def half(array):
            return lax.dynamic_slice_in_dim(array, at, tokens // 2).astype(F32)

        pair_half = (half(part) + half(mate)).astype(BF)
        across = beside(pair_half, 2)
        pair_half, part, mate, *later = lax.optimization_barrier((pair_half, part, mate, *later))
        pair = (part.astype(F32) + mate.astype(F32)).astype(BF)
        return (pair, across, beside(across, 1)), later

    others = [beside(own_x, distance) for distance in (1, 2, 3)]
    first_chunks = pl.pallas_call(
        first_load_kernel,
        out_shape=pltpu.VMEM((5, width, width), BF),
        in_specs=[HBM] * 3,
        out_specs=VMEM,
        scratch_shapes=[dma(5)],
        compiler_params=params(16),
        cost_estimate=cost(0, 5 << 20),
    )(*in_hbm(wq, wkv, wout))
    own_parts, own_all = pl.pallas_call(
        first_own_kernel,
        out_shape=[pltpu.HBM((dp_count, share, joined), BF), shape_of((tokens, width), BF)],
        in_specs=[VMEM] * 6,
        out_specs=[HBM, VMEM],
        scratch_shapes=[
            pltpu.VMEM((tokens, width), F32),
            vmem(dp_count, share, joined),
            dma(6),
        ],
        compiler_params=params(24),
        cost_estimate=cost(2 * tokens * width * joined, 6 << 20),
    )(own_x, *others, gain, first_chunks)
    own_parts, received_x, gain_x, wq_s, wout_s = lax.optimization_barrier(
        (own_parts, received_x, gain_x, wq, wout)
    )
    own_parts = scatter(own_parts, "dp")
    wq_b = swap(wq_s, from_second)
    cuts = (5 * q_cols // 16, 5 * q_cols // 8)
    wout_a0 = swap(wout_s[: cuts[0]], from_first)
    wout_a1, wout_a2 = wout_s[cuts[0] : cuts[1]], wout_s[cuts[1] :]
    other_parts = other_rows_parts(gather(received_x, "mp"))
    own_parts, other_parts, wout_a0, wout_a1, wout_a2 = lax.optimization_barrier(
        (own_parts, other_parts, wout_a0, wout_a1, wout_a2)
    )
    wout_a1 = swap(wout_a1, from_first)
    own = first_sum(own_parts)
    mine_all = gather(other_x, "mp")
    other_parts, own, mine_all = lax.optimization_barrier(
        (scatter(other_parts, "dp"), own, mine_all)
    )
    other = first_sum(other_parts)
    received = swap(other, from_first)
    received_grad, wkv_s = lax.optimization_barrier((swap(other, from_second), wkv))
    wkv_b = swap(wkv_s, from_second)
    copies, wout_a1, wout_a2 = lax.optimization_barrier(
        (chosen_copies(own, received, joined), wout_a1, wout_a2)
    )
    wout_a2 = swap(wout_a2, from_first)
    grad_copies = chosen_copies(received_grad, own, q_cols)
    qkv_first, grad_copies, wq_b, wq_s, wkv_s = lax.optimization_barrier(
        (spread(copies), grad_copies, wq_b, wq, wkv)
    )
    wout_a = (wout_a0, wout_a1, wout_a2)
    wq_a, wkv_a = swap(wq_s, from_first), swap(wkv_s, from_first)
    head_grad_last = spread(grad_copies)

    def layer_forward(qkv, wouts):
        out = pl.pallas_call(
            forward_kernel,
            out_shape=shape_of((tokens, width), BF),
            in_specs=[SMEM, ANY] + [HBM] * (1 + len(wouts[1])),
            out_specs=VMEM,
            scratch_shapes=[
                vmem(tokens, joined),
                chunks_of(4),
                pltpu.VMEM((tokens, tokens), F32),
                pltpu.VMEM((tokens, GROUP_HEADS * tokens), F32),
                vmem(tokens, GROUP_HEADS * tokens),
                vmem(tokens, q_cols),
                dma(4),
                dma(3),
            ],
            compiler_params=params(32),
            cost_estimate=cost(6 * tokens * tokens * q_cols, 4 << 20),
        )(seq_lengths, qkv, *in_hbm(wouts[0], *wouts[1]))
        return out

    def rows_after(resident, sums):
        even = lax.axis_index("mp") % 2 == 0
        lower, upper = jnp.where(even, *sums[1:]), jnp.where(even, *sums[:0:-1])
        added = sums[0].astype(F32) + jnp.concatenate([lower, upper], axis=0).astype(F32)
        return (resident.astype(F32) + added).astype(BF)

    out, wkv_b = lax.optimization_barrier((layer_forward(qkv_first, (wout, wout_a)), wkv_b))
    sums, pieces = sum_over_mp(out, wq_b, wkv_b, wq, wkv)
    joined_last = loaded(True, pieces[:2], pieces[2:])
    parts = pl.pallas_call(
        project_kernel,
        out_shape=pltpu.HBM((dp_count, share, joined), BF),
        in_specs=[VMEM] * 8,
        out_specs=HBM,
        scratch_shapes=[vmem(dp_count, share, joined), dma(6)],
        compiler_params=params(24),
        cost_estimate=cost(2 * tokens * width * joined, 6 << 20),
    )(own_all, mine_all, *sums, gain_x, gain, joined_last)
    parts, head_grad_last = lax.optimization_barrier((parts, head_grad_last))
    qkv_last = spread(summed_copies(scaled_sum, scatter(parts, "dp")))
    wout_b = swap(wout, from_second)
    wout_last = jnp.where(section == 0, wout_b, wout)
    h_one = rows_after(jnp.where(section == 0, own_all, mine_all), sums)
    rows_after(h_one, sum_over_mp(layer_forward(qkv_last, (wout_last, (wout_last,))))[0])

    def layer_backward(qkv, head_grads, wqs, wkvs, later=()):
        through = pl.pallas_call(
            backward_kernel,
            out_shape=shape_of((tokens, width), BF),
            in_specs=[SMEM, ANY, ANY] + [HBM] * 4,
            out_specs=VMEM,
            scratch_shapes=[
                vmem(tokens, joined),
                vmem(tokens, q_cols),
                chunks_of(5),
                pltpu.VMEM((tokens, tokens), F32),
                pltpu.VMEM((tokens, GROUP_HEADS * tokens), F32),
                pltpu.VMEM((tokens, GROUP_HEADS * tokens), F32),
                vmem(tokens, GROUP_HEADS * tokens),
                vmem(tokens, GROUP_HEADS * tokens),
                vmem(q_cols, tokens),
                vmem(tokens, 2 * kv_cols),
                dma(5),
                dma(5),
            ],
            compiler_params=params(32),
            cost_estimate=cost(12 * tokens * tokens * q_cols, 6 << 20),
        )(seq_lengths, qkv, head_grads, *in_hbm(*wqs, *wkvs))
        return sum_over_mp(through, *later)

    sums, pieces = layer_backward(
        qkv_last,
        *in_hbm(head_grad_last),
        (wq_b, wq),
        (wkv_b, wkv),
        later=(wout, *wout_a),
    )
    parts, grad_one = pl.pallas_call(
        head_grad_kernel,
        out_shape=[pltpu.HBM((dp_count, share, q_cols), BF), shape_of((tokens, width), BF)],
        in_specs=[VMEM] * 8,
        out_specs=[HBM, VMEM],
        scratch_shapes=[vmem(dp_count, share, q_cols), dma(4)],
        compiler_params=params(24),
        cost_estimate=cost(2 * tokens * width * q_cols, 4 << 20),
    )(mine_all, own_all, *sums, gain_x, gain, loaded(False, pieces[:1], pieces[1:]))
    parts, wq_a = lax.optimization_barrier((scatter(parts, "dp"), wq_a))
    head_grad_first, wkv_a = lax.optimization_barrier(
        (spread(summed_copies(plain_sum, parts)), wkv_a)
    )
    sums, _ = layer_backward(qkv_first, head_grad_first, (wq, wq_a), (wkv, wkv_a))

    hidden_cols = merger_weight.shape[0]
    outgoing, input_grad = pl.pallas_call(
        merger_kernel,
        out_shape=[
            shape_of((dp_count, 2, CAP * VB, hidden_cols), BF),
            shape_of((rows, width), BF),
        ],
        in_specs=[SMEM, SMEM] + [VMEM] * 7,
        out_specs=[VMEM] * 2,
        scratch_shapes=[
            pltpu.VMEM((tokens, width), F32),
            pltpu.VMEM((tokens, hidden_cols), F32),
            pltpu.SMEM((2 * dp_count,), jnp.int32),
            pltpu.SMEM((2 * dp_count * CAP,), jnp.int32),
        ],
        compiler_params=params(24),
    )(image_mask, block_owner, grad_one, *sums, gain, gain_x, merger_weight)
    kept, passed = pl.pallas_call(
        merger_sum_kernel,
        out_shape=[
            shape_of((CAP * VB, hidden_cols), F32),
            shape_of((CAP * VB, hidden_cols), BF),
        ],
        in_specs=[VMEM],
        out_specs=[VMEM] * 2,
        compiler_params=params(24),
    )(scatter(outgoing, "dp"))
    crossed = lax.ppermute(passed, "section", [(0, 1), (1, 0)]).astype(F32)
    first = jnp.where(section == 0, kept, crossed)
    second = jnp.where(section == 0, crossed, kept)
    hidden_grad = jnp.stack([first, second]).reshape(2, CAP, VB, hidden_cols)
    merger_grad = gelu_slope(merger_pre[0].astype(F32)) * hidden_grad
    return (input_grad[None], merger_grad[None])


def solution(mesh):
    placed = (
        P("section", "mp", "dp"),
        P("section", "mp", "dp"),
        P(None, "section", "dp"),
        P(None, "section", "dp", "mp"),
        P(None, "section", "dp", None, "mp"),
        P(None, "section", "mp", "dp"),
        P(),
        P("section", None),
        P("section", None),
        P("mp", "dp"),
        P(("section", "dp"), None, None, None, "mp"),
    )
    return jax.shard_map(
        local,
        mesh=mesh,
        in_specs=placed,
        out_specs=(P("section", "mp", "dp"), P(("section", "dp"), None, None, None, "mp")),
        check_vma=False,
    )
```
